128 devices in a mesh: gx: 16 (over x, y), gy: 8 (over z, core).
Axes of the slice: x: 4, y: 4, z: 4, core: 2. Of those that a mesh axis runs over, the one named last changes fastest.
Arguments:
- fields: float32 [6, 256, 256, 128], P(None, 'gx', 'gy'), may hold values from -0.0029296875 to 0.0029296875
- region: int32 [256, 256, 128], P('gx', 'gy'), may hold values from 0 to 15
- eps_table: float32 [16], replicated, may hold values from 1 to 2
Outputs:
- advanced: float32 [6, 256, 256, 128], P(None, 'gx', 'gy')
The draws below stay inside these ranges and needn't reach their ends.
All inputs are finite; a program needn't handle non-finite values.
Results may differ from the reference program's by a relative error of at most 0.0003.
Values sent between devices are 32-bit elements; how exact they have to be, the bound alone decides.
No kernel may reach another device: no remote copies, remote signals or barrier semaphores. Data moves between devices by JAX's collectives and lax.ppermute only.
A program may use at most 128 MiB of HBM per device.

```python
import math
import jax
import jax.numpy as jnp
from jax import lax

NZ = 128
REGIONS = 16
NX = 256
NY = 256


def set_ends(values, key, least, high):
    index_at = [jax.random.randint(jax.random.fold_in(key, axis), (), 0, length) for axis, length in enumerate(values.shape)]
    main_axis = values.shape.index(max(values.shape))
    neighbour = index_at[:main_axis] + [(index_at[main_axis] + 1) % values.shape[main_axis]] + index_at[main_axis + 1:]
    return values.at[tuple(index_at)].set(least).at[tuple(neighbour)].set(high)


def levels(stream_key, extent, pieces, low, top_value):
    def one(dim, blocks):
        steps = jax.random.uniform(jax.random.fold_in(jax.random.fold_in(stream_key, 6), dim), (blocks,), jnp.float32, low / len(pieces), top_value / len(pieces))
        return jnp.repeat(jnp.exp(steps), extent[dim] // blocks).reshape((-1,) + (1,) * (len(extent) - dim - 1))

    loudness = one(*pieces[0])
    for cut in pieces[1:]:
        loudness = loudness * one(*cut)
    return loudness


def scatter_about(key, extent, deviation, bound, cuts=(), dtype=jnp.bfloat16):
    level = levels(key, extent, cuts, -0.22, 0.18) if cuts else 1.0
    values = jax.random.normal(key, extent, jnp.float32) * deviation * level
    return jnp.minimum(jnp.maximum(values, -bound), bound).astype(dtype)


def setup_inputs(seed: int = 0) -> dict:
    keys = jax.random.split(jax.random.key(seed), 4)
    fields = scatter_about(keys[0], (6, NX, NY, NZ), 0.0005, 0.0029296875, ((1, 16), (2, 8)), jnp.float32)
    region = set_ends(jax.random.randint(keys[1], (NX, NY, NZ), 0, REGIONS), jax.random.fold_in(keys[1], 1), 0, REGIONS - 1).astype(jnp.int32)
    eps_table = jnp.clip(jnp.exp(jax.random.uniform(keys[2], (REGIONS,), jnp.float32, math.log(1.0), math.log(2.0))), 1.0, 2.0)
    return {"fields": fields, "region": region, "eps_table": eps_table}


plane_ratio = 32.0
depth_ratio = 0.5


def step_next(values, along_axis):
    tail_zeros = jnp.zeros_like(lax.slice_in_dim(values, 0, 1, axis=along_axis))
    shifted = jnp.concatenate([lax.slice_in_dim(values, 1, values.shape[along_axis], axis=along_axis), tail_zeros], axis=along_axis)
    return shifted - values


def step_prev(values, along_axis):
    head_zeros = jnp.zeros_like(lax.slice_in_dim(values, 0, 1, axis=along_axis))
    shifted = jnp.concatenate([head_zeros, lax.slice_in_dim(values, 0, values.shape[along_axis] - 1, axis=along_axis)], axis=along_axis)
    return values - shifted


def solve_lines(coupling, right_side):
    length = coupling.shape[0]
    position = jnp.arange(length)[:, None, None]
    lower_band = jnp.where(position > 0, -coupling, 0.0 * coupling)
    upper_band = jnp.where(position < length - 1, -coupling, 0.0 * coupling)
    diagonal = 1.0 + coupling * jnp.where(position == 0, 1.0, 2.0)

    def forward_step(carried, entries):
        carried_upper, carried_source = carried
        lower_row, diag_row, upper_row, source = entries
        divisor = diag_row - lower_row * carried_upper
        new_upper = upper_row / divisor
        new_source = (source - lower_row * carried_source) / divisor
        return (new_upper, new_source), (new_upper, new_source)

    start_row = jnp.zeros_like(coupling[0])
    _, (uppers, sources) = lax.scan(forward_step, (start_row, start_row), (lower_band, diagonal, upper_band, right_side))

    def backward_step(behind, entries):
        upper_row, source = entries
        solved = source - upper_row * behind
        return solved, solved

    _, solution = lax.scan(backward_step, start_row, (uppers, sources), reverse=True)
    return solution


def solve_x(coupling, right_side):
    return solve_lines(coupling, right_side)


def solve_y(coupling, right_side):
    solved = solve_lines(jnp.swapaxes(coupling, 0, 1), jnp.swapaxes(right_side, 0, 1))
    return jnp.swapaxes(solved, 0, 1)


def reference(fields, region, eps_table):
    inv_eps = (1.0 / eps_table)[region]
    plane_coef = plane_ratio * inv_eps
    depth_coef = depth_ratio * inv_eps
    coupling = plane_ratio * plane_coef
    ex_now = fields[0]
    ey_now = fields[1]
    ez_now = fields[2]
    hx_now = fields[3]
    hy_now = fields[4]
    hz_now = fields[5]
    partial_hz = hz_now - plane_ratio * step_next(ey_now, 0)
    partial_hy = hy_now - depth_ratio * step_next(ex_now, 2)
    ey_one = ey_now + depth_coef * step_prev(hx_now, 2) - plane_coef * step_prev(hz_now, 0)
    ex_one = solve_y(coupling, ex_now + plane_coef * step_prev(partial_hz, 1) - depth_coef * step_prev(hy_now, 2))
    ez_one = solve_x(coupling, ez_now + plane_coef * step_prev(partial_hy, 0) - plane_coef * step_prev(hx_now, 1))
    hz_one = partial_hz + plane_ratio * step_next(ex_one, 1)
    hy_one = partial_hy + plane_ratio * step_next(ez_one, 0)
    hx_one = hx_now - plane_ratio * step_next(ez_one, 1) + depth_ratio * step_next(ey_one, 2)
    ex_two = ex_one + plane_coef * step_prev(hz_one, 1) - depth_coef * step_prev(hy_one, 2)
    partial_z = hz_one + plane_ratio * step_next(ex_one, 1)
    partial_x = hx_one + depth_ratio * step_next(ey_one, 2)
    ey_two = solve_x(coupling, ey_one + depth_coef * step_prev(hx_one, 2) - plane_coef * step_prev(partial_z, 0))
    ez_two = solve_y(coupling, ez_one + plane_coef * step_prev(hy_one, 0) - plane_coef * step_prev(partial_x, 1))
    hz_two = partial_z - plane_ratio * step_next(ey_two, 0)
    hx_two = partial_x - plane_ratio * step_next(ez_two, 1)
    hy_two = hy_one - depth_ratio * step_next(ex_two, 2) + plane_ratio * step_next(ez_two, 0)
    return jnp.stack([ex_two, ey_two, ez_two, hx_two, hy_two, hz_two])
```

```python
import functools

import jax
import jax.numpy as jnp
from jax import lax
from jax.experimental import pallas as pl
from jax.experimental.pallas import tpu as pltpu
from jax.sharding import PartitionSpec as P

PX, PY, PZ = 16, 32, 128
XR = 40
YR = 24
F32 = jnp.float32
EX, EY, EZ, HX, HY, HZ = range(6)


def lane():
    return lax.broadcasted_iota(jnp.int32, (PY, PZ), 1)


def sub():
    return lax.broadcasted_iota(jnp.int32, (PY, PZ), 0)


def lanes_of(v):
    return lax.broadcasted_iota(jnp.int32, v.shape, 1)


def z_next(v):
    return jnp.where(lanes_of(v) == PZ - 1, 0.0, pltpu.roll(v, PZ - 1, 1))


def z_prev(v):
    return jnp.where(lanes_of(v) == 0, 0.0, pltpu.roll(v, 1, 1))


def fz(v):
    return z_next(v) - v


def bz(v):
    return v - z_prev(v)


def y_prev(v, row):
    return jnp.where(sub() == 0, row, pltpu.roll(v, 1, 0))


def y_next(v, row):
    return jnp.where(sub() == PY - 1, row, pltpu.roll(v, PY - 1, 0))


def plane(ref, k, size=PY):
    return ref[pl.ds(k * size, size), :]


def put(ref, k, v, size=PY):
    ref[pl.ds(k * size, size), :] = v


def fplane(ref, f, x):
    return plane(ref, f * PX + x)


def lookup(region, table):
    level = [table[i] for i in range(16)]
    for bit in range(4):
        on = (region & (1 << bit)) != 0
        level = [jnp.where(on, level[2 * i + 1], level[2 * i]) for i in range(len(level) // 2)]
    return level[0]


def k_edges(f, reg, table, eps, xup, xdn, yup, ydn):
    tab = [table[i] for i in range(16)]
    for x in range(PX):
        put(eps, x, lookup(plane(reg, x), tab))
    for i, c in enumerate((EX, EY, HY, HZ)):
        put(xup, i, fplane(f, c, PX - 1))
    put(xup, 4, plane(eps, PX - 1))
    for i, c in enumerate((EY, EZ, HX, HZ)):
        put(xdn, i, fplane(f, c, 0))
    put(xdn, 4, plane(eps, 0))

    def row(ref, base, y):
        return ref[pl.ds(base * PX * PY + y, PX, stride=PY), :]

    for i, (c, y) in enumerate(((EX, 31), (HY, 31), (EZ, 31), (HX, 31), (HX, 30))):
        put(yup, i, row(f, c, y), PX)
    put(yup, 5, row(eps, 0, PY - 1), PX)
    for i, c in enumerate((EX, HY, EZ, HX)):
        put(ydn, i, row(f, c, 0), PX)
    put(ydn, 4, row(eps, 0, 0), PX)


def factor(m_at, count, first, h, b, rows):
    hv = jnp.ones((rows, PZ), F32)
    hs = jnp.where(first, jnp.zeros_like(hv), jnp.ones_like(hv))
    bv = jnp.ones((rows, PZ), F32)
    bs = jnp.ones((rows, PZ), F32)
    for i in range(count):
        k = count - 1 - i
        put(h, i, hv, rows)
        put(b, k, bv, rows)
        hs = hs + m_at(i) * hv
        bs = bs + m_at(k) * bv
        hlast, blast = hv, bv
        hv = hv + hs
        bv = bv + bs
    hn = 1.0 / hv
    bn = 1.0 / bv
    return hn, bn, blast * bn, hn, hlast * hn


def sweep(m_at, r_at, count, v, rows):
    vv = jnp.zeros((rows, PZ), F32)
    vs = jnp.zeros((rows, PZ), F32)
    for i in range(count):
        put(v, i, vv, rows)
        vs = vs + m_at(i) * (vv - r_at(i))
        last = vv
        vv = vv + vs
    return last, vv


def ends(last, vn, hn, c):
    return -vn * hn, last - c * vn


def spread(msg, count, values):
    block = sum(v.shape[0] for v in values)
    for k in range(count):
        at = k * block
        for v in values:
            msg[pl.ds(at, v.shape[0]), :] = v
            at += v.shape[0]


def k_x1(f, eps, xl, xr, yl, yr, msg, q1, m, h, b, v, hb, r):
    gx = lax.axis_index("gx")
    gy = lax.axis_index("gy")
    n = lax.axis_size("gx")
    xlo = gx > 0
    ylo = gy > 0
    yhi = gy < lax.axis_size("gy") - 1
    yin = jnp.where(ylo, 1.0, 0.0)
    yon = jnp.where(yhi, 1.0, 0.0)
    q1lo = yin * (plane(yl, 1, PX) - 0.5 * fz(plane(yl, 0, PX)))
    q1hi = yon * (plane(yr, 1, PX) - 0.5 * fz(plane(yr, 0, PX)))
    hxlo = yin * plane(yl, 3, PX)
    epslo = plane(yl, 5, PX)
    epshi = plane(yr, 4, PX)
    hx31 = f[pl.ds(HX * PX * PY + PY - 1, PX, stride=PY), :]
    bxlo = jnp.concatenate([q1lo[:1], q1lo[1:] - q1lo[:-1]], 0)
    bxhi = jnp.concatenate([q1hi[:1], q1hi[1:] - q1hi[:-1]], 0)
    rlo = yin * plane(yl, 2, PX) + (32.0 / epslo) * (bxlo - (hxlo - yin * plane(yl, 4, PX)))
    rhi = yon * plane(yr, 2, PX) + (32.0 / epshi) * (bxhi - (yon * plane(yr, 3, PX) - hx31))
    pad = jnp.zeros((XR - PY - 2, PZ), F32)
    one = jnp.ones((XR - PY - 2, PZ), F32)
    before = jnp.where(xlo, plane(xl, 2) - 0.5 * fz(plane(xl, 0)), 0.0)
    for x in range(PX):
        q = fplane(f, HY, x) - 0.5 * fz(fplane(f, EX, x))
        put(q1, x, q)
        e = plane(eps, x)
        hx = fplane(f, HX, x)
        ce = 32.0 / e
        rr = fplane(f, EZ, x) + ce * ((q - before) - (hx - y_prev(hx, hxlo[x : x + 1])))
        before = q
        r[pl.ds(x * XR, PY), :] = rr
        r[pl.ds(x * XR + PY, 8), :] = jnp.concatenate([rlo[x : x + 1], rhi[x : x + 1], pad], 0)
        m[pl.ds(x * XR, PY), :] = e * (1.0 / 1024.0)
        m[pl.ds(x * XR + PY, 8), :] = (
            jnp.concatenate([epslo[x : x + 1], epshi[x : x + 1], one], 0) * (1.0 / 1024.0)
        )
    m_at = lambda i: plane(m, i, XR)
    hn, bn, a, bb, c = factor(m_at, PX, gx == 0, h, b, XR)
    last, vn = sweep(m_at, lambda i: plane(r, i, XR), PX, v, XR)
    pf, plast = ends(last, vn, hn, c)
    put(hb, 0, hn, XR)
    put(hb, 1, bn, XR)
    put(hb, 2, c, XR)
    put(hb, 3, vn, XR)
    zq = jnp.zeros((6, PZ), F32)
    qq = jnp.concatenate([q1lo[PX - 1 :], q1hi[PX - 1 :], zq], 0) * (-1.0 / 32.0)
    spread(msg, n, (pf, plast, a, bb, c, qq))


def k_y1(f, eps, xl, xr, order, msg, p1, ey1, m, h, b, v, hb, r, ep):
    gx = lax.axis_index("gx")
    gy = lax.axis_index("gy")
    n = lax.axis_size("gy")
    xlo = gx > 0
    xin = jnp.where(xlo, 1.0, 0.0)
    xon = jnp.where(gx < lax.axis_size("gx") - 1, 1.0, 0.0)
    zero = jnp.zeros((1, PZ), F32)
    zeros = jnp.zeros((PY, PZ), F32)
    exl, eyl, hyl, hzl = [xin * plane(xl, i) for i in range(4)]
    eyr, ezr, hxr, hzr = [xon * plane(xr, i) for i in range(4)]
    for x in range(PX):
        put(ep, x, plane(eps, x))
    put(ep, PX, plane(xl, 4))
    put(ep, PX + 1, plane(xr, 4))
    for x in range(PX + 2, YR):
        put(ep, x, zeros + 1.0)
        put(r, x, zeros)
    put(r, PX + 1, zeros)

    def rex(ex, hy, pp, e):
        ie = 1.0 / e
        return ex + (32.0 * ie) * (pp - y_prev(pp, zero)) - (0.5 * ie) * bz(hy)

    p = hzl - 32.0 * (fplane(f, EY, 0) - eyl)
    p = jnp.where(xlo, p, 0.0)
    put(p1, PX, p)
    put(r, PX, rex(exl, hyl, p, plane(ep, PX)))
    for x in range(PX):
        ey = fplane(f, EY, x)
        nxt = fplane(f, EY, x + 1) if x < PX - 1 else eyr
        hz = fplane(f, HZ, x)
        hzp = fplane(f, HZ, x - 1) if x > 0 else hzl
        e = plane(ep, x)
        p = hz - 32.0 * (nxt - ey)
        put(p1, x, p)
        put(r, x, rex(fplane(f, EX, x), fplane(f, HY, x), p, e))
        ie = 1.0 / e
        put(ey1, x, ey + (0.5 * ie) * bz(fplane(f, HX, x)) - (32.0 * ie) * (hz - hzp))
    ie = 1.0 / plane(ep, PX + 1)
    put(ey1, PX, eyr + (0.5 * ie) * bz(hxr) - (32.0 * ie) * (hzr - fplane(f, HZ, PX - 1)))

    def rows(ref, j):
        return ref[pl.ds(j, YR, stride=PY), :]

    for j in range(PY):
        put(m, j, rows(ep, j) * (1.0 / 1024.0), YR)
    m_at = lambda j: plane(m, j, YR)
    hn, bn, a, bb, c = factor(m_at, PY, gy == 0, h, b, YR)
    last, vn = sweep(m_at, lambda j: rows(r, j), PY, v, YR)
    pf, plast = ends(last, vn, hn, c)
    put(hb, 0, hn, YR)
    put(hb, 1, bn, YR)
    put(hb, 2, c, YR)
    put(hb, 3, vn, YR)
    lastrow = lambda ref, at, k: ref[pl.ds(at * PY + PY - 1, k, stride=PY), :]
    tail = jnp.zeros((7, PZ), F32)
    qq = jnp.concatenate([lastrow(p1, 0, PX), lastrow(p1, PX, 1), tail], 0) * (-1.0 / 32.0)
    tail = jnp.zeros((6, PZ), F32)
    ee = fz(jnp.concatenate([lastrow(ey1, 0, PX), zero, lastrow(ey1, PX, 1), tail], 0))
    spread(msg, n, (pf, plast, a, bb, c, qq, ee))


def coefficients(part, n, rows, tp, bp, ts, bs, bet, dele):
    zero = jnp.zeros((rows, PZ), F32)
    beta = zero
    put(bet, 0, zero, rows)
    for j in range(n):
        a, b, c = part(j, 2), part(j, 3), part(j, 4)
        bd = b / (1.0 - a * beta)
        t = bd * beta
        put(tp, j, t, rows)
        put(bp, j, bd, rows)
        beta = c + t * b
        put(bet, j + 1, beta, rows)
    delta = zero
    put(dele, n, zero, rows)
    for j in range(n - 1, -1, -1):
        a, b, c = part(j, 2), part(j, 3), part(j, 4)
        bd = b / (1.0 - c * delta)
        t = bd * delta
        put(ts, j, t, rows)
        put(bs, j, bd, rows)
        delta = a + t * b
        put(dele, j, delta, rows)


def interface(part, n, me, rows, tp, bp, ts, bs, bet, dele, al, ga, crows=None):
    crows = crows or rows
    zero = jnp.zeros((rows, PZ), F32)
    take = lambda ref, j: ref[pl.ds(j * crows, rows), :]
    alpha = zero
    put(al, 0, zero, rows)
    gamma = zero
    put(ga, n, zero, rows)
    for j in range(n):
        k = n - 1 - j
        alpha = part(j, 1) + take(tp, j) * part(j, 0) + take(bp, j) * alpha
        gamma = part(k, 0) + take(ts, k) * part(k, 1) + take(bs, k) * gamma
        put(al, j + 1, alpha, rows)
        put(ga, k, gamma, rows)
    at = lambda ref, d, size: ref[pl.ds(pl.multiple_of(d * size, 8), rows), :]
    a0, a1 = at(al, me, rows), at(al, me + 1, rows)
    g0, g1 = at(ga, me, rows), at(ga, me + 1, rows)
    b0, b1 = at(bet, me, crows), at(bet, me + 1, crows)
    d0, d1 = at(dele, me, crows), at(dele, me + 1, crows)
    left = a0 + b0 * ((g0 + d0 * a0) / (1.0 - d0 * b0))
    right = g1 + d1 * ((a1 + b1 * g1) / (1.0 - b1 * d1))
    return left, right


def k_y2(msg, p1, h, b, v, hb, ex1, p2, elo, tp, bp, ts, bs, bet, dele, al, ga, dex):
    n = lax.axis_size("gy")
    me = lax.axis_index("gy")
    block = 7 * YR
    raw = lambda j, k: msg[pl.ds(j * block + k * YR, YR), :]
    coefficients(raw, n, YR, tp, bp, ts, bs, bet, dele)

    def part(j, k):
        own = raw(j, k)
        if j == 0:
            return own
        return own + raw(j, 2 + k) * raw(j - 1, 5)

    left, right = interface(part, n, me, YR, tp, bp, ts, bs, bet, dele, al, ga)
    prev = pl.multiple_of(jnp.maximum(me - 1, 0) * block, 8)
    live = jnp.where(me > 0, 1.0, 0.0)
    q = live * msg[pl.ds(prev + 5 * YR, YR), :]
    elo[...] = live * msg[pl.ds(prev + 6 * YR, YR), :]
    lw = (left + q) * plane(hb, 1, YR)
    rw = (right - plane(hb, 3, YR)) * plane(hb, 0, YR)
    later = right
    for j in range(PY - 1, -1, -1):
        w = plane(v, j, YR) + plane(b, j, YR) * lw + plane(h, j, YR) * rw
        ex1[pl.ds(j, YR, stride=PY), :] = w
        dex[pl.ds(j, YR, stride=PY), :] = later - w
        later = w
    live = jnp.where(lax.axis_index("gx") > 0, 1.0, 0.0)
    for x in range(PX):
        put(p2, x, plane(p1, x) + 64.0 * plane(dex, x))
    put(p2, PX, live * (plane(p1, PX) + 64.0 * plane(dex, PX)))


def k_x2(msg, f, eps, q1, ey1, p2, h, b, v, m, hb, ez1, hx1, msg2, v2, vn2, tp, bp, ts, bs, bet, dele, al, ga, r):
    n = lax.axis_size("gx")
    me = lax.axis_index("gx")
    gy = lax.axis_index("gy")
    yon = jnp.where(gy < lax.axis_size("gy") - 1, 1.0, 0.0)
    block = 5 * XR + 8
    raw = lambda j, k: msg[pl.ds(j * block + k * XR, XR), :]
    coefficients(raw, n, XR, tp, bp, ts, bs, bet, dele)

    def part(j, k):
        if j == 0:
            return raw(j, k)
        own = msg[pl.ds(j * block + k * XR, PY), :]
        more = (
            msg[pl.ds(j * block + k * XR + PY, 8), :]
            + msg[pl.ds(j * block + (2 + k) * XR + PY, 8), :] * msg[pl.ds((j - 1) * block + 5 * XR, 8), :]
        )
        return jnp.concatenate([own, more], 0)

    left, right = interface(part, n, me, XR, tp, bp, ts, bs, bet, dele, al, ga)
    prev = pl.multiple_of(jnp.maximum(me - 1, 0) * block, 8)
    q = jnp.where(me > 0, 1.0, 0.0) * msg[pl.ds(prev + 5 * XR, 8), :]
    left = jnp.concatenate([left[:PY], left[PY:] + q], 0)
    lw = left * plane(hb, 1, XR)
    rw = (right - plane(hb, 3, XR)) * plane(hb, 0, XR)
    for x in range(PX):
        put(ez1, x, plane(v, x, XR) + plane(b, x, XR) * lw + plane(h, x, XR) * rw, XR)
    put(ez1, PX, right, XR)
    before = plane(p2, PX)
    for x in range(PX):
        z = ez1[pl.ds(x * XR, PY), :]
        z32 = yon * ez1[pl.ds(x * XR + PY + 1, 1), :]
        ey = plane(ey1, x)
        t = fplane(f, HX, x) - 32.0 * (y_next(z, z32) - z) + 0.5 * fz(ey)
        put(hx1, x, t)
        p = plane(p2, x)
        ie = 1.0 / plane(eps, x)
        put(r, x, ey + (0.5 * ie) * bz(t) - (32.0 * ie) * (p - before))
        before = p
    last, vn = sweep(lambda i: m[pl.ds(i * XR, PY), :], lambda i: plane(r, i), PX, v2, PY)
    vn2[...] = vn
    pf, plast = ends(last, vn, hb[pl.ds(0, PY), :], hb[pl.ds(2 * XR, PY), :])
    spread(msg2, n, (pf, plast))


def k_y3(f, xr, q1, eps, ey1, ez1, hx1, ex1, elo, m, hb, msg2, v2, vn2, ex2, hy1, q2, r):
    n = lax.axis_size("gy")
    gy = lax.axis_index("gy")
    yon = jnp.where(gy < n - 1, 1.0, 0.0)
    yin = jnp.where(gy > 0, 1.0, 0.0)
    zeros = jnp.zeros((PY, PZ), F32)
    for x in range(PX + 2, YR):
        put(r, x, zeros)
    put(r, PX, zeros)
    for x in range(PX + 1):
        at = x * XR
        z = ez1[pl.ds(at, PY), :]
        zlo = ez1[pl.ds(at + PY, 1), :]
        zhi = yon * ez1[pl.ds(at + PY + 1, 1), :]
        fe = fz(plane(ey1, x))
        d = 32.0 * (y_next(z, zhi) - z) - fe
        k = x if x < PX else PX + 1
        dlo = yin * (32.0 * (z[:1] - zlo) - elo[pl.ds(k, 1), :])
        ez = fplane(f, EZ, x) if x < PX else plane(xr, 1)
        e = plane(eps, x) if x < PX else plane(xr, 4)
        ie = 1.0 / e
        put(r, k, 2.0 * z - ez + (32.0 * ie) * (d - y_prev(d, dlo)))
        if x < PX:
            t = plane(q1, x) + 32.0 * (ez1[pl.ds(at + XR, PY), :] - z)
            put(hy1, x, t)
            put(ex2, x, 2.0 * plane(ex1, x) - fplane(f, EX, x) + (0.5 * ie) * bz(fplane(f, HY, x) - t))
            put(q2, x, plane(hx1, x) + 0.5 * fe)
    m_at = lambda j: plane(m, j, YR)
    last, vn = sweep(m_at, lambda j: r[pl.ds(j, YR, stride=PY), :], PY, v2, YR)
    vn2[...] = vn
    pf, plast = ends(last, vn, plane(hb, 0, YR), plane(hb, 2, YR))
    spread(msg2, n, (pf, plast))


def k_y4(msg, h, b, v2, vn2, hb, tp, bp, ts, bs, bet, dele, ex2, hy1, q2, ez2, hx2, hy2, al, ga, w2, dw):
    n = lax.axis_size("gy")
    me = lax.axis_index("gy")
    part = lambda j, k: msg[pl.ds((2 * j + k) * YR, YR), :]
    left, right = interface(part, n, me, YR, tp, bp, ts, bs, bet, dele, al, ga)
    lw = left * plane(hb, 1, YR)
    rw = (right - vn2[...]) * plane(hb, 0, YR)
    later = right
    for j in range(PY - 1, -1, -1):
        w = plane(v2, j, YR) + plane(b, j, YR) * lw + plane(h, j, YR) * rw
        w2[pl.ds(j, YR, stride=PY), :] = w
        dw[pl.ds(j, YR, stride=PY), :] = later - w
        later = w
    xon = jnp.where(lax.axis_index("gx") < lax.axis_size("gx") - 1, 1.0, 0.0)
    for x in range(PX):
        w = plane(w2, x)
        nxt = plane(w2, x + 1) if x < PX - 1 else xon * plane(w2, PX + 1)
        put(ez2, x, w)
        put(hx2, x, plane(q2, x) - 32.0 * plane(dw, x))
        put(hy2, x, plane(hy1, x) - 0.5 * fz(plane(ex2, x)) + 32.0 * (nxt - w))


def k_x4(msg, h, b, v2, vn2, hb, tp, bp, ts, bs, bet, dele, p2, ex2, ez2, hx2, hy2, out, al, ga):
    n = lax.axis_size("gx")
    me = lax.axis_index("gx")
    part = lambda j, k: msg[pl.ds((2 * j + k) * PY, PY), :]
    left, right = interface(part, n, me, PY, tp, bp, ts, bs, bet, dele, al, ga, XR)
    lw = left * hb[pl.ds(XR, PY), :]
    rw = (right - vn2[...]) * hb[pl.ds(0, PY), :]
    later = right
    for x in range(PX - 1, -1, -1):
        w = plane(v2, x) + b[pl.ds(x * XR, PY), :] * lw + h[pl.ds(x * XR, PY), :] * rw
        put(out, EY * PX + x, w)
        put(out, HZ * PX + x, plane(p2, x) - 32.0 * (later - w))
        later = w
        put(out, EX * PX + x, plane(ex2, x))
        put(out, EZ * PX + x, plane(ez2, x))
        put(out, HX * PX + x, plane(hx2, x))
        put(out, HY * PX + x, plane(hy2, x))


def rows_of(*counts):
    return [jax.ShapeDtypeStruct((c, PZ), F32) for c in counts]


def call(kernel, outs, args, scratch=(), smem=(), name=None):
    vm = pl.BlockSpec(memory_space=pltpu.VMEM)
    sm = pl.BlockSpec(memory_space=pltpu.SMEM)
    return pl.pallas_call(
        kernel,
        out_shape=rows_of(*outs),
        in_specs=[sm if i in smem else vm for i in range(len(args))],
        out_specs=[vm] * len(outs),
        scratch_shapes=[pltpu.VMEM((c, PZ), F32) for c in scratch],
        compiler_params=pltpu.CompilerParams(vmem_limit_bytes=24 * 1024 * 1024),
        cost_estimate=pl.CostEstimate(flops=4_000_000, bytes_accessed=4_000_000, transcendentals=0),
        name=name,
    )(*args)


def ring(block, axis, step):
    n = lax.axis_size(axis)
    return lax.ppermute(block, axis, [(i, (i + step) % n) for i in range(n)])


def swap(msg, axis):
    n = lax.axis_size(axis)
    got = lax.all_to_all(msg.reshape(n, -1, PZ), axis, 0, 0, tiled=True)
    return got.reshape(-1, PZ)


def local(fields, region, eps_table):
    nx = lax.axis_size("gx")
    ny = lax.axis_size("gy")
    cells = PX * PY
    f = fields.reshape(6 * cells, PZ)
    reg = region.reshape(cells, PZ)
    eps, xup, xdn, yup, ydn = call(
        k_edges, (cells, 5 * PY, 5 * PY, 6 * PX, 6 * PX), (f, reg, eps_table), smem=(2,), name="edges"
    )
    xl = ring(xup, "gx", 1)
    xr = ring(xdn, "gx", -1)
    yl = ring(yup, "gy", 1)
    yr = ring(ydn, "gy", -1)
    nxl, nyl = PX * XR, PY * YR
    msgx, q1, mx, hx, bx, vx, hbx = call(
        k_x1,
        (nx * (5 * XR + 8), cells, nxl, nxl, nxl, nxl, 4 * XR),
        (f, eps, xl, xr, yl, yr),
        (nxl,),
        name="x1",
    )
    gotx = swap(msgx, "gx")
    msgy, p1, ey1, my, hy, by, vy, hby = call(
        k_y1,
        (ny * 7 * YR, cells + PY, cells + PY, nyl, nyl, nyl, nyl, 4 * YR),
        (f, eps, xl, xr, hbx),
        (YR * PY, YR * PY),
        name="y1",
    )
    goty = swap(msgy, "gy")
    chain = lambda n, rows: (n * rows,) * 4 + ((n + 1) * rows,) * 2
    ex1, p2, elo, *cy = call(
        k_y2,
        (YR * PY, cells + PY, YR) + chain(ny, YR),
        (goty, p1, hy, by, vy, hby),
        ((ny + 1) * YR, (ny + 1) * YR, YR * PY),
        name="y2",
    )
    ez1, hx1, msgx2, vx2, vnx2, *cx = call(
        k_x2,
        (nxl + XR, cells, nx * 2 * PY, cells, PY) + chain(nx, XR),
        (gotx, f, eps, q1, ey1, p2, hx, bx, vx, mx, hbx),
        ((nx + 1) * XR, (nx + 1) * XR, cells),
        name="x2",
    )
    gotx2 = swap(msgx2, "gx")
    msgy2, vy2, vny2, ex2, hy1, q2 = call(
        k_y3,
        (ny * 2 * YR, nyl, YR, cells, cells, cells),
        (f, xr, q1, eps, ey1, ez1, hx1, ex1, elo, my, hby),
        (YR * PY,),
        name="y3",
    )
    goty2 = swap(msgy2, "gy")
    ez2, hx2, hy2 = call(
        k_y4,
        (cells, cells, cells),
        (goty2, hy, by, vy2, vny2, hby, *cy, ex2, hy1, q2),
        ((ny + 1) * YR, (ny + 1) * YR, YR * PY, YR * PY),
        name="y4",
    )
    (out,) = call(
        k_x4,
        (6 * cells,),
        (gotx2, hx, bx, vx2, vnx2, hbx, *cx, p2, ex2, ez2, hx2, hy2),
        ((nx + 1) * PY, (nx + 1) * PY),
        name="x4",
    )
    return out.reshape(6, PX, PY, PZ)


def solution(mesh):
    return jax.shard_map(
        local,
        mesh=mesh,
        in_specs=(P(None, "gx", "gy", None), P("gx", "gy", None), P()),
        out_specs=P(None, "gx", "gy", None),
        check_vma=False,
    )
```

```python
import functools

import jax
import jax.numpy as jnp
from jax import lax
from jax.experimental import pallas as pl
from jax.experimental.pallas import tpu as pltpu
from jax.sharding import PartitionSpec as P

PX, PY, PZ = 16, 32, 128
XR = 40
YR = 24
F32 = jnp.float32
EX, EY, EZ, HX, HY, HZ = range(6)


def lane():
    return lax.broadcasted_iota(jnp.int32, (PY, PZ), 1)


def sub():
    return lax.broadcasted_iota(jnp.int32, (PY, PZ), 0)


def lanes_of(v):
    return lax.broadcasted_iota(jnp.int32, v.shape, 1)


def z_next(v):
    return jnp.where(lanes_of(v) == PZ - 1, 0.0, pltpu.roll(v, PZ - 1, 1))


def z_prev(v):
    return jnp.where(lanes_of(v) == 0, 0.0, pltpu.roll(v, 1, 1))


def fz(v):
    return z_next(v) - v


def bz(v):
    return v - z_prev(v)


def y_prev(v, row):
    return jnp.where(sub() == 0, row, pltpu.roll(v, 1, 0))


def y_next(v, row):
    return jnp.where(sub() == PY - 1, row, pltpu.roll(v, PY - 1, 0))


def plane(ref, k, size=PY):
    return ref[pl.ds(k * size, size), :]


def put(ref, k, v, size=PY):
    ref[pl.ds(k * size, size), :] = v


def fplane(ref, f, x):
    return plane(ref, f * PX + x)


def lookup(region, table):
    level = [table[i] for i in range(16)]
    for bit in range(4):
        on = (region & (1 << bit)) != 0
        level = [jnp.where(on, level[2 * i + 1], level[2 * i]) for i in range(len(level) // 2)]
    return level[0]


def k_edges(f, reg, table, eps, xup, xdn, yup, ydn):
    tab = [table[i] for i in range(16)]
    for x in range(PX):
        put(eps, x, lookup(plane(reg, x), tab))
    for i, c in enumerate((EX, EY, HY, HZ)):
        put(xup, i, fplane(f, c, PX - 1))
    put(xup, 4, plane(eps, PX - 1))
    for i, c in enumerate((EY, EZ, HX, HZ)):
        put(xdn, i, fplane(f, c, 0))
    put(xdn, 4, plane(eps, 0))

    def row(ref, base, y):
        return ref[pl.ds(base * PX * PY + y, PX, stride=PY), :]

    for i, (c, y) in enumerate(((EX, 31), (HY, 31), (EZ, 31), (HX, 31), (HX, 30))):
        put(yup, i, row(f, c, y), PX)
    put(yup, 5, row(eps, 0, PY - 1), PX)
    for i, c in enumerate((EX, HY, EZ, HX)):
        put(ydn, i, row(f, c, 0), PX)
    put(ydn, 4, row(eps, 0, 0), PX)


def factor(m_at, count, first, h, b, rows):
    hv = jnp.ones((rows, PZ), F32)
    hs = jnp.where(first, jnp.zeros_like(hv), jnp.ones_like(hv))
    bv = jnp.ones((rows, PZ), F32)
    bs = jnp.ones((rows, PZ), F32)
    for i in range(count):
        k = count - 1 - i
        put(h, i, hv, rows)
        put(b, k, bv, rows)
        hs = hs + m_at(i) * hv
        bs = bs + m_at(k) * bv
        hlast, blast = hv, bv
        hv = hv + hs
        bv = bv + bs
    hn = 1.0 / hv
    bn = 1.0 / bv
    return hn, bn, blast * bn, hn, hlast * hn


def sweep(m_at, r_at, count, v, rows):
    vv = jnp.zeros((rows, PZ), F32)
    vs = jnp.zeros((rows, PZ), F32)
    for i in range(count):
        put(v, i, vv, rows)
        vs = vs + m_at(i) * (vv - r_at(i))
        last = vv
        vv = vv + vs
    return last, vv


def ends(last, vn, hn, c):
    return -vn * hn, last - c * vn


def spread(msg, count, values):
    block = sum(v.shape[0] for v in values)
    for k in range(count):
        at = k * block
        for v in values:
            msg[pl.ds(at, v.shape[0]), :] = v
            at += v.shape[0]


def k_x1(f, eps, xl, xr, yl, yr, msg, q1, m, h, b, v, hb, r):
    gx = lax.axis_index("gx")
    gy = lax.axis_index("gy")
    n = lax.axis_size("gx")
    xlo = gx > 0
    ylo = gy > 0
    yhi = gy < lax.axis_size("gy") - 1
    yin = jnp.where(ylo, 1.0, 0.0)
    yon = jnp.where(yhi, 1.0, 0.0)
    q1lo = yin * (plane(yl, 1, PX) - 0.5 * fz(plane(yl, 0, PX)))
    q1hi = yon * (plane(yr, 1, PX) - 0.5 * fz(plane(yr, 0, PX)))
    hxlo = yin * plane(yl, 3, PX)
    epslo = plane(yl, 5, PX)
    epshi = plane(yr, 4, PX)
    hx31 = f[pl.ds(HX * PX * PY + PY - 1, PX, stride=PY), :]
    bxlo = jnp.concatenate([q1lo[:1], q1lo[1:] - q1lo[:-1]], 0)
    bxhi = jnp.concatenate([q1hi[:1], q1hi[1:] - q1hi[:-1]], 0)
    rlo = yin * plane(yl, 2, PX) + (32.0 / epslo) * (bxlo - (hxlo - yin * plane(yl, 4, PX)))
    rhi = yon * plane(yr, 2, PX) + (32.0 / epshi) * (bxhi - (yon * plane(yr, 3, PX) - hx31))
    pad = jnp.zeros((XR - PY - 2, PZ), F32)
    one = jnp.ones((XR - PY - 2, PZ), F32)
    before = jnp.where(xlo, plane(xl, 2) - 0.5 * fz(plane(xl, 0)), 0.0)
    for x in range(PX):
        q = fplane(f, HY, x) - 0.5 * fz(fplane(f, EX, x))
        put(q1, x, q)
        e = plane(eps, x)
        hx = fplane(f, HX, x)
        ce = 32.0 / e
        rr = fplane(f, EZ, x) + ce * ((q - before) - (hx - y_prev(hx, hxlo[x : x + 1])))
        before = q
        r[pl.ds(x * XR, PY), :] = rr
        r[pl.ds(x * XR + PY, 8), :] = jnp.concatenate([rlo[x : x + 1], rhi[x : x + 1], pad], 0)
        m[pl.ds(x * XR, PY), :] = e * (1.0 / 1024.0)
        m[pl.ds(x * XR + PY, 8), :] = (
            jnp.concatenate([epslo[x : x + 1], epshi[x : x + 1], one], 0) * (1.0 / 1024.0)
        )
    m_at = lambda i: plane(m, i, XR)
    hn, bn, a, bb, c = factor(m_at, PX, gx == 0, h, b, XR)
    last, vn = sweep(m_at, lambda i: plane(r, i, XR), PX, v, XR)
    pf, plast = ends(last, vn, hn, c)
    put(hb, 0, hn, XR)
    put(hb, 1, bn, XR)
    put(hb, 2, c, XR)
    put(hb, 3, vn, XR)
    zq = jnp.zeros((6, PZ), F32)
    qq = jnp.concatenate([q1lo[PX - 1 :], q1hi[PX - 1 :], zq], 0) * (-1.0 / 32.0)
    spread(msg, n, (pf, plast, a, bb, c, qq))


def k_y1(f, eps, xl, xr, msg, p1, ey1, m, h, b, v, hb, r, ep):
    gx = lax.axis_index("gx")
    gy = lax.axis_index("gy")
    n = lax.axis_size("gy")
    xlo = gx > 0
    xin = jnp.where(xlo, 1.0, 0.0)
    xon = jnp.where(gx < lax.axis_size("gx") - 1, 1.0, 0.0)
    zero = jnp.zeros((1, PZ), F32)
    zeros = jnp.zeros((PY, PZ), F32)
    exl, eyl, hyl, hzl = [xin * plane(xl, i) for i in range(4)]
    eyr, ezr, hxr, hzr = [xon * plane(xr, i) for i in range(4)]
    for x in range(PX):
        put(ep, x, plane(eps, x))
    put(ep, PX, plane(xl, 4))
    put(ep, PX + 1, plane(xr, 4))
    for x in range(PX + 2, YR):
        put(ep, x, zeros + 1.0)
        put(r, x, zeros)
    put(r, PX + 1, zeros)

    def rex(ex, hy, pp, e):
        ie = 1.0 / e
        return ex + (32.0 * ie) * (pp - y_prev(pp, zero)) - (0.5 * ie) * bz(hy)

    p = hzl - 32.0 * (fplane(f, EY, 0) - eyl)
    p = jnp.where(xlo, p, 0.0)
    put(p1, PX, p)
    put(r, PX, rex(exl, hyl, p, plane(ep, PX)))
    for x in range(PX):
        ey = fplane(f, EY, x)
        nxt = fplane(f, EY, x + 1) if x < PX - 1 else eyr
        hz = fplane(f, HZ, x)
        hzp = fplane(f, HZ, x - 1) if x > 0 else hzl
        e = plane(ep, x)
        p = hz - 32.0 * (nxt - ey)
        put(p1, x, p)
        put(r, x, rex(fplane(f, EX, x), fplane(f, HY, x), p, e))
        ie = 1.0 / e
        put(ey1, x, ey + (0.5 * ie) * bz(fplane(f, HX, x)) - (32.0 * ie) * (hz - hzp))
    ie = 1.0 / plane(ep, PX + 1)
    put(ey1, PX, eyr + (0.5 * ie) * bz(hxr) - (32.0 * ie) * (hzr - fplane(f, HZ, PX - 1)))

    def rows(ref, j):
        return ref[pl.ds(j, YR, stride=PY), :]

    for j in range(PY):
        put(m, j, rows(ep, j) * (1.0 / 1024.0), YR)
    m_at = lambda j: plane(m, j, YR)
    hn, bn, a, bb, c = factor(m_at, PY, gy == 0, h, b, YR)
    last, vn = sweep(m_at, lambda j: rows(r, j), PY, v, YR)
    pf, plast = ends(last, vn, hn, c)
    put(hb, 0, hn, YR)
    put(hb, 1, bn, YR)
    put(hb, 2, c, YR)
    put(hb, 3, vn, YR)
    lastrow = lambda ref, at, k: ref[pl.ds(at * PY + PY - 1, k, stride=PY), :]
    tail = jnp.zeros((7, PZ), F32)
    qq = jnp.concatenate([lastrow(p1, 0, PX), lastrow(p1, PX, 1), tail], 0) * (-1.0 / 32.0)
    tail = jnp.zeros((6, PZ), F32)
    ee = fz(jnp.concatenate([lastrow(ey1, 0, PX), zero, lastrow(ey1, PX, 1), tail], 0))
    spread(msg, 1, (pf, plast, a, bb, c, qq, ee))


def coefficients(part, n, rows, tp, bp, ts, bs, bet, dele):
    zero = jnp.zeros((rows, PZ), F32)
    beta = zero
    put(bet, 0, zero, rows)
    for j in range(n):
        a, b, c = part(j, 2), part(j, 3), part(j, 4)
        bd = b / (1.0 - a * beta)
        t = bd * beta
        put(tp, j, t, rows)
        put(bp, j, bd, rows)
        beta = c + t * b
        put(bet, j + 1, beta, rows)
    delta = zero
    put(dele, n, zero, rows)
    for j in range(n - 1, -1, -1):
        a, b, c = part(j, 2), part(j, 3), part(j, 4)
        bd = b / (1.0 - c * delta)
        t = bd * delta
        put(ts, j, t, rows)
        put(bs, j, bd, rows)
        delta = a + t * b
        put(dele, j, delta, rows)


def interface(part, n, me, rows, tp, bp, ts, bs, bet, dele, al, ga, crows=None):
    crows = crows or rows
    zero = jnp.zeros((rows, PZ), F32)
    take = lambda ref, j: ref[pl.ds(j * crows, rows), :]
    alpha = zero
    put(al, 0, zero, rows)
    gamma = zero
    put(ga, n, zero, rows)
    for j in range(n):
        k = n - 1 - j
        alpha = part(j, 1) + take(tp, j) * part(j, 0) + take(bp, j) * alpha
        gamma = part(k, 0) + take(ts, k) * part(k, 1) + take(bs, k) * gamma
        put(al, j + 1, alpha, rows)
        put(ga, k, gamma, rows)
    at = lambda ref, d, size: ref[pl.ds(pl.multiple_of(d * size, 8), rows), :]
    a0, a1 = at(al, me, rows), at(al, me + 1, rows)
    g0, g1 = at(ga, me, rows), at(ga, me + 1, rows)
    b0, b1 = at(bet, me, crows), at(bet, me + 1, crows)
    d0, d1 = at(dele, me, crows), at(dele, me + 1, crows)
    left = a0 + b0 * ((g0 + d0 * a0) / (1.0 - d0 * b0))
    right = g1 + d1 * ((a1 + b1 * g1) / (1.0 - b1 * d1))
    return left, right


def k_y2(msg, p1, h, b, v, hb, ex1, p2, elo, tp, bp, ts, bs, bet, dele, al, ga, dex):
    n = lax.axis_size("gy")
    me = lax.axis_index("gy")
    block = 7 * YR
    raw = lambda j, k: msg[pl.ds(j * block + k * YR, YR), :]
    coefficients(raw, n, YR, tp, bp, ts, bs, bet, dele)

    def part(j, k):
        own = raw(j, k)
        if j == 0:
            return own
        return own + raw(j, 2 + k) * raw(j - 1, 5)

    left, right = interface(part, n, me, YR, tp, bp, ts, bs, bet, dele, al, ga)
    prev = pl.multiple_of(jnp.maximum(me - 1, 0) * block, 8)
    live = jnp.where(me > 0, 1.0, 0.0)
    q = live * msg[pl.ds(prev + 5 * YR, YR), :]
    elo[...] = live * msg[pl.ds(prev + 6 * YR, YR), :]
    lw = (left + q) * plane(hb, 1, YR)
    rw = (right - plane(hb, 3, YR)) * plane(hb, 0, YR)
    later = right
    for j in range(PY - 1, -1, -1):
        w = plane(v, j, YR) + plane(b, j, YR) * lw + plane(h, j, YR) * rw
        ex1[pl.ds(j, YR, stride=PY), :] = w
        dex[pl.ds(j, YR, stride=PY), :] = later - w
        later = w
    live = jnp.where(lax.axis_index("gx") > 0, 1.0, 0.0)
    for x in range(PX):
        put(p2, x, plane(p1, x) + 64.0 * plane(dex, x))
    put(p2, PX, live * (plane(p1, PX) + 64.0 * plane(dex, PX)))


def k_x2(msg, f, eps, q1, ey1, p2, h, b, v, m, hb, ez1, hx1, msg2, v2, vn2, tp, bp, ts, bs, bet, dele, al, ga, r):
    n = lax.axis_size("gx")
    me = lax.axis_index("gx")
    gy = lax.axis_index("gy")
    yon = jnp.where(gy < lax.axis_size("gy") - 1, 1.0, 0.0)
    block = 5 * XR + 8
    raw = lambda j, k: msg[pl.ds(j * block + k * XR, XR), :]
    coefficients(raw, n, XR, tp, bp, ts, bs, bet, dele)

    def part(j, k):
        if j == 0:
            return raw(j, k)
        own = msg[pl.ds(j * block + k * XR, PY), :]
        more = (
            msg[pl.ds(j * block + k * XR + PY, 8), :]
            + msg[pl.ds(j * block + (2 + k) * XR + PY, 8), :] * msg[pl.ds((j - 1) * block + 5 * XR, 8), :]
        )
        return jnp.concatenate([own, more], 0)

    left, right = interface(part, n, me, XR, tp, bp, ts, bs, bet, dele, al, ga)
    prev = pl.multiple_of(jnp.maximum(me - 1, 0) * block, 8)
    q = jnp.where(me > 0, 1.0, 0.0) * msg[pl.ds(prev + 5 * XR, 8), :]
    left = jnp.concatenate([left[:PY], left[PY:] + q], 0)
    lw = left * plane(hb, 1, XR)
    rw = (right - plane(hb, 3, XR)) * plane(hb, 0, XR)
    for x in range(PX):
        put(ez1, x, plane(v, x, XR) + plane(b, x, XR) * lw + plane(h, x, XR) * rw, XR)
    put(ez1, PX, right, XR)
    before = plane(p2, PX)
    for x in range(PX):
        z = ez1[pl.ds(x * XR, PY), :]
        z32 = yon * ez1[pl.ds(x * XR + PY + 1, 1), :]
        ey = plane(ey1, x)
        t = fplane(f, HX, x) - 32.0 * (y_next(z, z32) - z) + 0.5 * fz(ey)
        put(hx1, x, t)
        p = plane(p2, x)
        ie = 1.0 / plane(eps, x)
        put(r, x, ey + (0.5 * ie) * bz(t) - (32.0 * ie) * (p - before))
        before = p
    last, vn = sweep(lambda i: m[pl.ds(i * XR, PY), :], lambda i: plane(r, i), PX, v2, PY)
    vn2[...] = vn
    pf, plast = ends(last, vn, hb[pl.ds(0, PY), :], hb[pl.ds(2 * XR, PY), :])
    spread(msg2, n, (pf, plast))


def k_y3(f, xr, q1, eps, ey1, ez1, hx1, ex1, elo, m, hb, msg2, v2, vn2, ex2, hy1, q2, r):
    n = lax.axis_size("gy")
    gy = lax.axis_index("gy")
    yon = jnp.where(gy < n - 1, 1.0, 0.0)
    yin = jnp.where(gy > 0, 1.0, 0.0)
    zeros = jnp.zeros((PY, PZ), F32)
    for x in range(PX + 2, YR):
        put(r, x, zeros)
    put(r, PX, zeros)
    for x in range(PX + 1):
        at = x * XR
        z = ez1[pl.ds(at, PY), :]
        zlo = ez1[pl.ds(at + PY, 1), :]
        zhi = yon * ez1[pl.ds(at + PY + 1, 1), :]
        fe = fz(plane(ey1, x))
        d = 32.0 * (y_next(z, zhi) - z) - fe
        k = x if x < PX else PX + 1
        dlo = yin * (32.0 * (z[:1] - zlo) - elo[pl.ds(k, 1), :])
        ez = fplane(f, EZ, x) if x < PX else plane(xr, 1)
        e = plane(eps, x) if x < PX else plane(xr, 4)
        ie = 1.0 / e
        put(r, k, 2.0 * z - ez + (32.0 * ie) * (d - y_prev(d, dlo)))
        if x < PX:
            t = plane(q1, x) + 32.0 * (ez1[pl.ds(at + XR, PY), :] - z)
            put(hy1, x, t)
            put(ex2, x, 2.0 * plane(ex1, x) - fplane(f, EX, x) + (0.5 * ie) * bz(fplane(f, HY, x) - t))
            put(q2, x, plane(hx1, x) + 0.5 * fe)
    m_at = lambda j: plane(m, j, YR)
    last, vn = sweep(m_at, lambda j: r[pl.ds(j, YR, stride=PY), :], PY, v2, YR)
    vn2[...] = vn
    pf, plast = ends(last, vn, plane(hb, 0, YR), plane(hb, 2, YR))
    spread(msg2, 1, (pf, plast))


def k_y4(msg, h, b, v2, vn2, hb, tp, bp, ts, bs, bet, dele, ex2, hy1, q2, out, al, ga, w2, dw):
    n = lax.axis_size("gy")
    me = lax.axis_index("gy")
    part = lambda j, k: msg[pl.ds((2 * j + k) * YR, YR), :]
    left, right = interface(part, n, me, YR, tp, bp, ts, bs, bet, dele, al, ga)
    lw = left * plane(hb, 1, YR)
    rw = (right - vn2[...]) * plane(hb, 0, YR)
    later = right
    for j in range(PY - 1, -1, -1):
        w = plane(v2, j, YR) + plane(b, j, YR) * lw + plane(h, j, YR) * rw
        w2[pl.ds(j, YR, stride=PY), :] = w
        dw[pl.ds(j, YR, stride=PY), :] = later - w
        later = w
    xon = jnp.where(lax.axis_index("gx") < lax.axis_size("gx") - 1, 1.0, 0.0)
    for x in range(PX):
        w = plane(w2, x)
        nxt = plane(w2, x + 1) if x < PX - 1 else xon * plane(w2, PX + 1)
        e2 = plane(ex2, x)
        put(out, EX * PX + x, e2)
        put(out, EZ * PX + x, w)
        put(out, HX * PX + x, plane(q2, x) - 32.0 * plane(dw, x))
        put(out, HY * PX + x, plane(hy1, x) - 0.5 * fz(e2) + 32.0 * (nxt - w))


def k_x4(msg, h, b, v2, vn2, hb, tp, bp, ts, bs, bet, dele, p2, out, al, ga):
    n = lax.axis_size("gx")
    me = lax.axis_index("gx")
    part = lambda j, k: msg[pl.ds((2 * j + k) * PY, PY), :]
    left, right = interface(part, n, me, PY, tp, bp, ts, bs, bet, dele, al, ga, XR)
    lw = left * hb[pl.ds(XR, PY), :]
    rw = (right - vn2[...]) * hb[pl.ds(0, PY), :]
    later = right
    for x in range(PX - 1, -1, -1):
        w = plane(v2, x) + b[pl.ds(x * XR, PY), :] * lw + h[pl.ds(x * XR, PY), :] * rw
        put(out, EY * PX + x, w)
        put(out, HZ * PX + x, plane(p2, x) - 32.0 * (later - w))
        later = w


def call(name, parts, args, outs, scratch=(), smem=(), into=(), flush=()):
    into, flush, scratch = dict(into), dict(flush), dict(scratch)
    moved = [k for k in args if k not in smem]
    pieces = {k for group in flush.values() for k, _, _ in group}
    last = {k: max(i for i, (_, used) in enumerate(parts) if k in used) for k in outs}
    leave = [
        [(k, 0, outs[k]) for k in outs if last[k] == i and k not in pieces] + list(flush.get(i, ()))
        for i in range(len(parts))
    ]
    own = [k for k in moved if k not in into]

    def body(*refs):
        take = iter(refs)
        hbm = {k: next(take) for k in args}
        results = {k: next(take) for k in outs}
        env = {k: next(take) for k in own}
        env.update({k: next(take) for k in outs})
        env.update({k: next(take) for k in scratch})
        env.update({k: hbm[k] for k in smem})
        sem_in, sem_out = next(take), next(take)
        pending = {}
        for i, k in enumerate(moved):
            where = env.get(k)
            if k in into:
                buffer, row = into[k]
                where = env[buffer].at[pl.ds(row(), args[k].shape[0]), :]
            copy = pltpu.make_async_copy(hbm[k], where, sem_in.at[i])
            copy.start()
            pending.setdefault(into[k][0] if k in into else k, []).append(copy)
        sent = []
        for i, (function, used) in enumerate(parts):
            for k in used:
                for copy in pending.pop(k, ()):
                    copy.wait()
            function(*[env[k] for k in used])
            for k, row, rows in leave[i]:
                window = pl.ds(row, rows)
                copy = pltpu.make_async_copy(
                    env[k].at[window, :], results[k].at[window, :], sem_out.at[len(sent)]
                )
                copy.start()
                sent.append(copy)
        for copy in sent:
            copy.wait()

    anywhere = pl.BlockSpec(memory_space=pl.ANY)
    scalars = pl.BlockSpec(memory_space=pltpu.SMEM)
    got = pl.pallas_call(
        body,
        out_shape=[jax.ShapeDtypeStruct((c, PZ), F32) for c in outs.values()],
        in_specs=[scalars if k in smem else anywhere for k in args],
        out_specs=[anywhere] * len(outs),
        scratch_shapes=[pltpu.VMEM(args[k].shape, args[k].dtype) for k in own]
        + [pltpu.VMEM((c, PZ), F32) for c in list(outs.values()) + list(scratch.values())]
        + [
            pltpu.SemaphoreType.DMA((len(moved),)),
            pltpu.SemaphoreType.DMA((sum(len(group) for group in leave),)),
        ],
        compiler_params=pltpu.CompilerParams(vmem_limit_bytes=56 * 1024 * 1024),
        cost_estimate=pl.CostEstimate(flops=1000, bytes_accessed=1000, transcendentals=0),
        name=name,
    )(*args.values())
    return dict(zip(outs, got))


def ring(block, axis, step):
    n = lax.axis_size(axis)
    return lax.ppermute(block, axis, [(i, (i + step) % n) for i in range(n)])


def swap(msg, axis):
    n = lax.axis_size(axis)
    got = lax.all_to_all(msg.reshape(n, -1, PZ), axis, 0, 0, tiled=True)
    return got.reshape(-1, PZ)


def from_all(msg, axis, buffer):
    n = lax.axis_size(axis)
    rows = msg.shape[0]
    args, into = {}, {}
    for step in range(n):
        k = buffer + str(step)
        args[k] = ring(msg, axis, step) if step else msg

        def row(step=step):
            return pl.multiple_of(lax.rem(lax.axis_index(axis) - step + n, n) * rows, 8)

        into[k] = (buffer, row)
    return args, into


def local(fields, region, eps_table):
    nx = lax.axis_size("gx")
    ny = lax.axis_size("gy")
    cells = PX * PY
    nxl, nyl = PX * XR, PY * YR
    f = fields.reshape(6 * cells, PZ)
    reg = region.reshape(cells, PZ)
    halo = ("xup", "xdn", "yup", "ydn")
    got = call(
        "edges",
        [(k_edges, ("f", "reg", "table", "eps") + halo)],
        dict(f=f, reg=reg, table=eps_table),
        dict(eps=cells, xup=5 * PY, xdn=5 * PY, yup=6 * PX, ydn=6 * PX),
        smem=("table",),
    )
    base = dict(f=f, eps=got["eps"])
    xl = ring(got["xup"], "gx", 1)
    xr = ring(got["xdn"], "gx", -1)
    yl = ring(got["yup"], "gy", 1)
    yr = ring(got["ydn"], "gy", -1)
    linex = ("mx", "hx", "bx", "vx", "hbx")
    liney = ("my", "hy", "by", "vy", "hby")
    one = call(
        "one",
        [
            (k_x1, ("f", "eps", "xl", "xr", "yl", "yr", "msgx", "q1") + linex + ("r",)),
            (k_y1, ("f", "eps", "xl", "xr", "msgy", "p1", "ey1") + liney + ("rt", "ep")),
        ],
        dict(base, xl=xl, xr=xr, yl=yl, yr=yr),
        dict(
            zip(
                ("msgx", "q1") + linex + ("msgy", "p1", "ey1") + liney,
                (nx * (5 * XR + 8), cells, nxl, nxl, nxl, nxl, 4 * XR)
                + (7 * YR, cells + PY, cells + PY, nyl, nyl, nyl, nyl, 4 * YR),
            )
        ),
        dict(r=nxl, rt=YR * PY, ep=YR * PY),
    )
    gotx = swap(one["msgx"], "gx")
    argy, into = from_all(one["msgy"], "gy", "gy")
    chains = ("tp", "bp", "ts", "bs", "bet", "del")
    cx, cy = [tuple(k + a for k in chains) for a in "xy"]
    size = lambda n, rows: (n * rows,) * 4 + ((n + 1) * rows,) * 2
    keep = {k: one[k] for k in ("q1", "p1", "ey1") + linex + liney}
    two = call(
        "two",
        [
            (k_y2, ("gy", "p1", "hy", "by", "vy", "hby", "ex1", "p2", "elo") + cy + ("aly", "gay", "dex")),
            (
                k_x2,
                ("gx", "f", "eps", "q1", "ey1", "p2", "hx", "bx", "vx", "mx", "hbx")
                + ("ez1", "hx1", "msgx2", "vx2", "vnx2")
                + cx
                + ("alx", "gax", "r"),
            ),
            (
                k_y3,
                ("f", "xr", "q1", "eps", "ey1", "ez1", "hx1", "ex1", "elo", "my", "hby")
                + ("msgy2", "vy2", "vny2", "ex2", "hy1", "q2", "rt"),
            ),
        ],
        dict(argy, gx=gotx, xr=xr, **base, **keep),
        dict(
            zip(
                ("p2",) + cy + ("msgx2", "vx2", "vnx2") + cx + ("msgy2", "vy2", "vny2", "ex2", "hy1", "q2"),
                (cells + PY,)
                + size(ny, YR)
                + (nx * 2 * PY, cells, PY)
                + size(nx, XR)
                + (2 * YR, nyl, YR, cells, cells, cells),
            )
        ),
        dict(
            gy=ny * 7 * YR, ex1=YR * PY, elo=YR, aly=(ny + 1) * YR, gay=(ny + 1) * YR, dex=YR * PY,
            ez1=nxl + XR, hx1=cells, alx=(nx + 1) * XR, gax=(nx + 1) * XR, r=cells, rt=YR * PY,
        ),
        into=into,
    )
    gotx = swap(two["msgx2"], "gx")
    argy, into = from_all(two["msgy2"], "gy", "gy")
    need = {k: one[k] for k in ("hx", "bx", "hbx", "hy", "by", "hby")}
    need.update({k: two[k] for k in ("p2",) + cy + cx + ("vx2", "vnx2", "vy2", "vny2", "ex2", "hy1", "q2")})
    three = call(
        "three",
        [
            (
                k_y4,
                ("gy", "hy", "by", "vy2", "vny2", "hby") + cy + ("ex2", "hy1", "q2", "out")
                + ("aly", "gay", "w2", "dw"),
            ),
            (k_x4, ("gx", "hx", "bx", "vx2", "vnx2", "hbx") + cx + ("p2", "out", "alx", "gax")),
        ],
        dict(argy, gx=gotx, **need),
        dict(out=6 * cells),
        dict(
            gy=ny * 2 * YR, aly=(ny + 1) * YR, gay=(ny + 1) * YR, w2=YR * PY, dw=YR * PY,
            alx=(nx + 1) * PY, gax=(nx + 1) * PY,
        ),
        into=into,
        flush={
            0: [("out", EX * cells, cells), ("out", EZ * cells, 3 * cells)],
            1: [("out", EY * cells, cells), ("out", HZ * cells, cells)],
        },
    )
    return three["out"].reshape(6, PX, PY, PZ)


def solution(mesh):
    return jax.shard_map(
        local,
        mesh=mesh,
        in_specs=(P(None, "gx", "gy", None), P("gx", "gy", None), P()),
        out_specs=P(None, "gx", "gy", None),
        check_vma=False,
    )
```

```python
import functools

import jax
import jax.numpy as jnp
from jax import lax
from jax.experimental import pallas as pl
from jax.experimental.pallas import tpu as pltpu
from jax.sharding import Mesh
from jax.sharding import PartitionSpec as P

PX, PY, PZ = 16, 32, 128
XR = 40
YR = 24
F32 = jnp.float32
LIMIT = 30
EX, EY, EZ, HX, HY, HZ = range(6)


def x_index():
    return lax.axis_index("ga") * lax.axis_size("gb") + lax.axis_index("gb")


def y_index():
    return lax.axis_index("gz") * lax.axis_size("gc") + lax.axis_index("gc")


def y_size():
    return lax.axis_size("gz") * lax.axis_size("gc")


def x_size():
    return lax.axis_size("ga") * lax.axis_size("gb")


def sub():
    return lax.broadcasted_iota(jnp.int32, (PY, PZ), 0)


def lanes_of(v):
    return lax.broadcasted_iota(jnp.int32, v.shape, 1)


def z_next(v):
    return jnp.where(lanes_of(v) == PZ - 1, 0.0, pltpu.roll(v, PZ - 1, 1))


def z_prev(v):
    return jnp.where(lanes_of(v) == 0, 0.0, pltpu.roll(v, 1, 1))


def fz(v):
    return z_next(v) - v


def bz(v):
    return v - z_prev(v)


def y_prev(v, row):
    return jnp.where(sub() == 0, row, pltpu.roll(v, 1, 0))


def y_next(v, row):
    return jnp.where(sub() == PY - 1, row, pltpu.roll(v, PY - 1, 0))


def plane(ref, k, size=PY):
    return ref[pl.ds(k * size, size), :]


def put(ref, k, v, size=PY):
    ref[pl.ds(k * size, size), :] = v


def fplane(ref, f, x):
    return plane(ref, f * PX + x)


def lookup(region, table):
    level = [table[i] for i in range(16)]
    for bit in range(4):
        on = (region & (1 << bit)) != 0
        level = [jnp.where(on, level[2 * i + 1], level[2 * i]) for i in range(len(level) // 2)]
    return level[0]


def k_eps(reg, table, eps):
    tab = [table[i] for i in range(16)]
    for x in range(PX):
        put(eps, x, lookup(plane(reg, x), tab))


def k_edges(f, reg, table, xup, xdn, yup, ydn, tab, ends, low, high, rlow, rhigh, sems):
    up, down = (EX, EY, HY, HZ), (EY, EZ, HX, HZ)
    rows = (EX, HY, EZ, HX)
    top = pl.ds(PY - 8, 8)
    pairs = [(table, tab), (reg.at[PX - 1], ends.at[0]), (reg.at[0], ends.at[1])]
    pairs += [(reg.at[:, top, :], rhigh), (reg.at[:, pl.ds(0, 8), :], rlow)]
    for i in range(4):
        pairs += [
            (f.at[up[i], PX - 1], xup.at[pl.ds(i * PY, PY), :]),
            (f.at[down[i], 0], xdn.at[pl.ds(i * PY, PY), :]),
            (f.at[rows[i], :, top, :], high.at[i]),
            (f.at[rows[i], :, pl.ds(0, 8), :], low.at[i]),
        ]
    copies = [pltpu.make_async_copy(p, q, sems.at[i]) for i, (p, q) in enumerate(pairs)]
    for copy in copies:
        copy.start()
    for copy in copies:
        copy.wait()
    t = [tab[i] for i in range(16)]
    put(xup, 4, lookup(ends[0], t))
    put(xdn, 4, lookup(ends[1], t))
    for i in range(4):
        put(yup, i, high[i, :, 7, :], PX)
        put(ydn, i, low[i, :, 0, :], PX)
    put(yup, 4, high[3, :, 6, :], PX)
    put(yup, 5, lookup(rhigh[:, 7, :], t), PX)
    put(ydn, 4, lookup(rlow[:, 0, :], t), PX)


def edges(fields, region, eps_table):
    vmem, hbm = [pl.BlockSpec(memory_space=m) for m in (pltpu.VMEM, pltpu.HBM)]
    return pl.pallas_call(
        k_edges,
        out_shape=[pltpu.VMEM((c, PZ), F32) for c in (5 * PY, 5 * PY, 6 * PX, 6 * PX)],
        in_specs=[hbm] * 3,
        out_specs=[vmem] * 4,
        scratch_shapes=[
            pltpu.SMEM((16,), F32),
            pltpu.VMEM((2, PY, PZ), jnp.int32),
            pltpu.VMEM((4, PX, 8, PZ), F32),
            pltpu.VMEM((4, PX, 8, PZ), F32),
            pltpu.VMEM((PX, 8, PZ), jnp.int32),
            pltpu.VMEM((PX, 8, PZ), jnp.int32),
            pltpu.SemaphoreType.DMA((21,)),
        ],
        cost_estimate=pl.CostEstimate(flops=1000, bytes_accessed=1000, transcendentals=0),
        name="edges",
    )(*[pltpu.with_memory_space_constraint(v, pltpu.HBM) for v in (fields, region, eps_table)])


def factor(m_at, count, first, h, b, rows):
    hv = jnp.ones((rows, PZ), F32)
    hs = jnp.where(first, jnp.zeros_like(hv), jnp.ones_like(hv))
    bv = jnp.ones((rows, PZ), F32)
    bs = jnp.ones((rows, PZ), F32)
    for i in range(count):
        k = count - 1 - i
        put(h, i, hv, rows)
        put(b, k, bv, rows)
        hs = hs + m_at(i) * hv
        bs = bs + m_at(k) * bv
        hlast, blast = hv, bv
        hv = hv + hs
        bv = bv + bs
    hn = 1.0 / hv
    bn = 1.0 / bv
    return hn, bn, blast * bn, hn, hlast * hn


def sweep(m_at, r_at, count, v, rows):
    vv = jnp.zeros((rows, PZ), F32)
    vs = jnp.zeros((rows, PZ), F32)
    for i in range(count):
        put(v, i, vv, rows)
        vs = vs + m_at(i) * (vv - r_at(i))
        last = vv
        vv = vv + vs
    return last, vv


def ends(last, vn, hn, c):
    return -vn * hn, last - c * vn


def spread(msg, count, values):
    block = sum(v.shape[0] for v in values)
    for k in range(count):
        at = k * block
        for v in values:
            msg[pl.ds(at, v.shape[0]), :] = v
            at += v.shape[0]


def k_x1(f, eps, xl, xr, yl, yr, msg, q1, m, h, b, v, hb, r):
    gx = x_index()
    gy = y_index()
    xlo = gx > 0
    ylo = gy > 0
    yhi = gy < y_size() - 1
    yin = jnp.where(ylo, 1.0, 0.0)
    yon = jnp.where(yhi, 1.0, 0.0)
    q1lo = yin * (plane(yl, 1, PX) - 0.5 * fz(plane(yl, 0, PX)))
    q1hi = yon * (plane(yr, 1, PX) - 0.5 * fz(plane(yr, 0, PX)))
    hxlo = yin * plane(yl, 3, PX)
    epslo = plane(yl, 5, PX)
    epshi = plane(yr, 4, PX)
    hx31 = f[pl.ds(HX * PX * PY + PY - 1, PX, stride=PY), :]
    bxlo = jnp.concatenate([q1lo[:1], q1lo[1:] - q1lo[:-1]], 0)
    bxhi = jnp.concatenate([q1hi[:1], q1hi[1:] - q1hi[:-1]], 0)
    rlo = yin * plane(yl, 2, PX) + (32.0 / epslo) * (bxlo - (hxlo - yin * plane(yl, 4, PX)))
    rhi = yon * plane(yr, 2, PX) + (32.0 / epshi) * (bxhi - (yon * plane(yr, 3, PX) - hx31))
    pad = jnp.zeros((XR - PY - 2, PZ), F32)
    one = jnp.ones((XR - PY - 2, PZ), F32)
    before = jnp.where(xlo, plane(xl, 2) - 0.5 * fz(plane(xl, 0)), 0.0)
    for x in range(PX):
        q = fplane(f, HY, x) - 0.5 * fz(fplane(f, EX, x))
        put(q1, x, q)
        e = plane(eps, x)
        hx = fplane(f, HX, x)
        ce = 32.0 / e
        rr = fplane(f, EZ, x) + ce * ((q - before) - (hx - y_prev(hx, hxlo[x : x + 1])))
        before = q
        r[pl.ds(x * XR, PY), :] = rr
        r[pl.ds(x * XR + PY, 8), :] = jnp.concatenate([rlo[x : x + 1], rhi[x : x + 1], pad], 0)
        m[pl.ds(x * XR, PY), :] = e * (1.0 / 1024.0)
        m[pl.ds(x * XR + PY, 8), :] = (
            jnp.concatenate([epslo[x : x + 1], epshi[x : x + 1], one], 0) * (1.0 / 1024.0)
        )
    m_at = lambda i: plane(m, i, XR)
    hn, bn, a, bb, c = factor(m_at, PX, gx == 0, h, b, XR)
    last, vn = sweep(m_at, lambda i: plane(r, i, XR), PX, v, XR)
    pf, plast = ends(last, vn, hn, c)
    put(hb, 0, hn, XR)
    put(hb, 1, bn, XR)
    put(hb, 2, c, XR)
    put(hb, 3, vn, XR)
    zq = jnp.zeros((6, PZ), F32)
    qq = jnp.concatenate([q1lo[PX - 1 :], q1hi[PX - 1 :], zq], 0) * (-1.0 / 32.0)
    spread(msg, lax.axis_size("gb"), (pf, plast, a, bb, c, qq))


def k_y1(f, eps, xl, xr, msg, p1, ey1, m, h, b, v, hb, r, ep):
    gx = x_index()
    gy = y_index()
    n = y_size()
    xlo = gx > 0
    xin = jnp.where(xlo, 1.0, 0.0)
    xon = jnp.where(gx < x_size() - 1, 1.0, 0.0)
    zero = jnp.zeros((1, PZ), F32)
    zeros = jnp.zeros((PY, PZ), F32)
    exl, eyl, hyl, hzl = [xin * plane(xl, i) for i in range(4)]
    eyr, ezr, hxr, hzr = [xon * plane(xr, i) for i in range(4)]
    for x in range(PX):
        put(ep, x, plane(eps, x))
    put(ep, PX, plane(xl, 4))
    put(ep, PX + 1, plane(xr, 4))
    for x in range(PX + 2, YR):
        put(ep, x, zeros + 1.0)
        put(r, x, zeros)
    put(r, PX + 1, zeros)

    def rex(ex, hy, pp, e):
        ie = 1.0 / e
        return ex + (32.0 * ie) * (pp - y_prev(pp, zero)) - (0.5 * ie) * bz(hy)

    p = hzl - 32.0 * (fplane(f, EY, 0) - eyl)
    p = jnp.where(xlo, p, 0.0)
    put(p1, PX, p)
    put(r, PX, rex(exl, hyl, p, plane(ep, PX)))
    for x in range(PX):
        ey = fplane(f, EY, x)
        nxt = fplane(f, EY, x + 1) if x < PX - 1 else eyr
        hz = fplane(f, HZ, x)
        hzp = fplane(f, HZ, x - 1) if x > 0 else hzl
        e = plane(ep, x)
        p = hz - 32.0 * (nxt - ey)
        put(p1, x, p)
        put(r, x, rex(fplane(f, EX, x), fplane(f, HY, x), p, e))
        ie = 1.0 / e
        put(ey1, x, ey + (0.5 * ie) * bz(fplane(f, HX, x)) - (32.0 * ie) * (hz - hzp))
    ie = 1.0 / plane(ep, PX + 1)
    put(ey1, PX, eyr + (0.5 * ie) * bz(hxr) - (32.0 * ie) * (hzr - fplane(f, HZ, PX - 1)))

    def rows(ref, j):
        return ref[pl.ds(j, YR, stride=PY), :]

    for j in range(PY):
        put(m, j, rows(ep, j) * (1.0 / 1024.0), YR)
    m_at = lambda j: plane(m, j, YR)
    hn, bn, a, bb, c = factor(m_at, PY, gy == 0, h, b, YR)
    last, vn = sweep(m_at, lambda j: rows(r, j), PY, v, YR)
    pf, plast = ends(last, vn, hn, c)
    put(hb, 0, hn, YR)
    put(hb, 1, bn, YR)
    put(hb, 2, c, YR)
    put(hb, 3, vn, YR)
    lastrow = lambda ref, at, k: ref[pl.ds(at * PY + PY - 1, k, stride=PY), :]
    tail = jnp.zeros((7, PZ), F32)
    qq = jnp.concatenate([lastrow(p1, 0, PX), lastrow(p1, PX, 1), tail], 0) * (-1.0 / 32.0)
    tail = jnp.zeros((6, PZ), F32)
    ee = fz(jnp.concatenate([lastrow(ey1, 0, PX), zero, lastrow(ey1, PX, 1), tail], 0))
    spread(msg, 1, (pf, plast, a, bb, c, qq, ee))


def coefficients(part, n, rows, tp, bp, ts, bs, bet, dele):
    zero = jnp.zeros((rows, PZ), F32)
    beta = zero
    put(bet, 0, zero, rows)
    for j in range(n):
        a, b, c = part(j, 2), part(j, 3), part(j, 4)
        bd = b / (1.0 - a * beta)
        t = bd * beta
        put(tp, j, t, rows)
        put(bp, j, bd, rows)
        beta = c + t * b
        put(bet, j + 1, beta, rows)
    delta = zero
    put(dele, n, zero, rows)
    for j in range(n - 1, -1, -1):
        a, b, c = part(j, 2), part(j, 3), part(j, 4)
        bd = b / (1.0 - c * delta)
        t = bd * delta
        put(ts, j, t, rows)
        put(bs, j, bd, rows)
        delta = a + t * b
        put(dele, j, delta, rows)


def chain(part, n, rows, crows, tp, bp, ts, bs, al, ga, start, stop):
    take = lambda ref, j: ref[pl.ds(j * crows, rows), :]
    alpha, gamma = start, stop
    put(al, 0, alpha, rows)
    put(ga, n, gamma, rows)
    for j in range(n):
        k = n - 1 - j
        alpha = part(j, 1) + take(tp, j) * part(j, 0) + take(bp, j) * alpha
        gamma = part(k, 0) + take(ts, k) * part(k, 1) + take(bs, k) * gamma
        put(al, j + 1, alpha, rows)
        put(ga, k, gamma, rows)
    return gamma, alpha


def interface(part, n, me, rows, coefs, al, ga, start=None, stop=None, crows=None):
    crows = crows or rows
    tp, bp, ts, bs, bet, dele = coefs
    zero = jnp.zeros((rows, PZ), F32)
    start = zero if start is None else start
    stop = zero if stop is None else stop
    chain(part, n, rows, crows, tp, bp, ts, bs, al, ga, start, stop)
    at = lambda ref, d, size: ref[pl.ds(pl.multiple_of(d * size, 8), rows), :]
    a0, a1 = at(al, me, rows), at(al, me + 1, rows)
    g0, g1 = at(ga, me, rows), at(ga, me + 1, rows)
    b0, b1 = at(bet, me, crows), at(bet, me + 1, crows)
    d0, d1 = at(dele, me, crows), at(dele, me + 1, crows)
    left = a0 + b0 * ((g0 + d0 * a0) / (1.0 - d0 * b0))
    right = g1 + d1 * ((a1 + b1 * g1) / (1.0 - b1 * d1))
    return left, right


XB = 5 * XR + 8


def x_raw(msg):
    return lambda j, k: msg[pl.ds(j * XB + k * XR, XR), :]


def x_part(msg):
    def part(j, k):
        if j == 0:
            return x_raw(msg)(j, k)
        own = msg[pl.ds(j * XB + k * XR, PY), :]
        more = (
            msg[pl.ds(j * XB + k * XR + PY, 8), :]
            + msg[pl.ds(j * XB + (2 + k) * XR + PY, 8), :] * msg[pl.ds((j - 1) * XB + 5 * XR, 8), :]
        )
        return jnp.concatenate([own, more], 0)

    return part


def x_passed(msg, me):
    prev = pl.multiple_of(jnp.maximum(me - 1, 0) * XB, 8)
    return jnp.where(me > 0, msg[pl.ds(prev + 5 * XR, 8), :], 0.0)


YB = 7 * YR


def y_raw(msg):
    return lambda j, k: msg[pl.ds(j * YB + k * YR, YR), :]


def y_part(msg):
    raw = y_raw(msg)
    return lambda j, k: raw(j, k) + raw(j, 2 + k) * raw(j - 1, 5) if j else raw(j, k)


def y_passed(msg, me, k):
    prev = pl.multiple_of(jnp.maximum(me - 1, 0) * YB, 8)
    return jnp.where(me > 0, msg[pl.ds(prev + k * YR, YR), :], 0.0)


def k_y2(gi, go, p1, h, b, v, hb, ex1, p2, elo, *more):
    coi, coo, (al, ga, dex) = more[:6], more[6:12], more[12:]
    nz, nc = lax.axis_size("gz"), lax.axis_size("gc")
    iz, ic = lax.axis_index("gz"), lax.axis_index("gc")
    coefficients(y_raw(go), nz, YR, *coo)
    coefficients(y_raw(gi), nc, YR, *coi)
    left, right = interface(y_part(go), nz, iz, YR, coo, al, ga)
    left = left + y_passed(go, iz, 5)
    left, right = interface(y_part(gi), nc, ic, YR, coi, al, ga, left, right)
    left = left + y_passed(gi, ic, 5)
    elo[...] = jnp.where(ic > 0, y_passed(gi, ic, 6), y_passed(go, iz, 6))
    lw = left * plane(hb, 1, YR)
    rw = (right - plane(hb, 3, YR)) * plane(hb, 0, YR)
    later = right
    for j in range(PY - 1, -1, -1):
        w = plane(v, j, YR) + plane(b, j, YR) * lw + plane(h, j, YR) * rw
        ex1[pl.ds(j, YR, stride=PY), :] = w
        dex[pl.ds(j, YR, stride=PY), :] = later - w
        later = w
    live = jnp.where(x_index() > 0, 1.0, 0.0)
    for x in range(PX):
        put(p2, x, plane(p1, x) + 64.0 * plane(dex, x))
    put(p2, PX, live * (plane(p1, PX) + 64.0 * plane(dex, PX)))


def join(part, raw, count):
    pf, ph, a, b, c = part(0, 0), part(0, 1), raw(0, 2), raw(0, 3), raw(0, 4)
    for j in range(1, count):
        qf, qh, a2, b2, c2 = part(j, 0), part(j, 1), raw(j, 2), raw(j, 3), raw(j, 4)
        den = 1.0 / (1.0 - c * a2)
        low, high = b * den, b2 * den
        pf, ph = pf + low * (qf + a2 * ph), qh + high * (ph + c * qf)
        a, b, c = a + low * b * a2, low * b2, c2 + high * b2 * c
    return pf, ph, a, b, c


def k_join_y(gi, msg):
    nc = lax.axis_size("gc")
    raw = y_raw(gi)
    spread(msg, 1, join(y_part(gi), raw, nc) + (raw(nc - 1, 5), raw(nc - 1, 6)))


def k_join_x(gi, msg, inner):
    inner[...] = gi[...]
    nb = lax.axis_size("gb")
    last = gi[pl.ds((nb - 1) * XB + 5 * XR, 8), :]
    spread(msg, lax.axis_size("ga"), join(x_part(gi), x_raw(gi), nb) + (last,))


def shares(pf, ph, coefs, count, me, rows, crows):
    tp, bp, ts, bs = coefs[:4]
    low = high = jnp.ones((rows, PZ), F32)
    for k in range(count):
        low = jnp.where(k < me, low * bs[pl.ds(k * crows, rows), :], low)
        high = jnp.where(k > me, high * bp[pl.ds(k * crows, rows), :], high)
    mine = pl.ds(pl.multiple_of(me * crows, 8), rows)
    return low * (pf + ts[mine, :] * ph), high * (ph + tp[mine, :] * pf)


def gathered(msg, n, m, ia, ib, rows, crows, coi, coo, al, ga):
    zero = jnp.zeros((rows, PZ), F32)

    def inside(j, k):
        at = pl.multiple_of(((ia * m + j) * 2 + k) * rows, 8)
        return msg[pl.ds(at, rows), :]

    whole = chain(inside, m, rows, crows, *coi[:4], al, ga, zero, zero)

    def group(j, k):
        total = sum(msg[pl.ds(((j * m + i) * 2 + k) * rows, rows), :] for i in range(m))
        return jnp.where(ia == j, whole[k], total)

    left, right = interface(group, n, ia, rows, coo, al, ga, crows=crows)
    return interface(inside, m, ib, rows, coi, al, ga, left, right, crows)


def k_x2(gi, go, f, q1, ey1, p2, h, b, v, m, hb, ez1, hx1, msg2, v2, vn2, *more):
    coi, coo, (al, ga, r) = more[:6], more[6:12], more[12:]
    na, nb = lax.axis_size("ga"), lax.axis_size("gb")
    ia, ib = lax.axis_index("ga"), lax.axis_index("gb")
    gy = y_index()
    yon = jnp.where(gy < y_size() - 1, 1.0, 0.0)
    coefficients(x_raw(go), na, XR, *coo)
    coefficients(x_raw(gi), nb, XR, *coi)
    left, right = interface(x_part(go), na, ia, XR, coo, al, ga)
    left = jnp.concatenate([left[:PY], left[PY:] + x_passed(go, ia)], 0)
    left, right = interface(x_part(gi), nb, ib, XR, coi, al, ga, left, right)
    left = jnp.concatenate([left[:PY], left[PY:] + x_passed(gi, ib)], 0)
    lw = left * plane(hb, 1, XR)
    rw = (right - plane(hb, 3, XR)) * plane(hb, 0, XR)
    for x in range(PX):
        put(ez1, x, plane(v, x, XR) + plane(b, x, XR) * lw + plane(h, x, XR) * rw, XR)
    put(ez1, PX, right, XR)
    before = plane(p2, PX)
    for x in range(PX):
        z = ez1[pl.ds(x * XR, PY), :]
        z32 = yon * ez1[pl.ds(x * XR + PY + 1, 1), :]
        ey = plane(ey1, x)
        t = fplane(f, HX, x) - 32.0 * (y_next(z, z32) - z) + 0.5 * fz(ey)
        put(hx1, x, t)
        p = plane(p2, x)
        ie = 1.0 / (m[pl.ds(x * XR, PY), :] * 1024.0)
        put(r, x, ey + (0.5 * ie) * bz(t) - (32.0 * ie) * (p - before))
        before = p
    last, vn = sweep(lambda i: m[pl.ds(i * XR, PY), :], lambda i: plane(r, i), PX, v2, PY)
    vn2[...] = vn
    pf, plast = ends(last, vn, hb[pl.ds(0, PY), :], hb[pl.ds(2 * XR, PY), :])
    share = shares(pf, plast, coi, nb, ib, PY, XR)
    for k in range(na * nb):
        for i, (own, joined) in enumerate(zip((pf, plast), share)):
            put(msg2, 2 * k + i, jnp.where(ia == k // nb, own, joined))


def k_y3(f, xr, q1, mx, ey1, ez1, hx1, ex1, elo, m, hb, tp, bp, ts, bs, msg2, part2, v2, vn2, ex2, hy1, q2, r):
    n = y_size()
    gy = y_index()
    yon = jnp.where(gy < n - 1, 1.0, 0.0)
    yin = jnp.where(gy > 0, 1.0, 0.0)
    zeros = jnp.zeros((PY, PZ), F32)
    for x in range(PX + 2, YR):
        put(r, x, zeros)
    put(r, PX, zeros)
    for x in range(PX + 1):
        at = x * XR
        z = ez1[pl.ds(at, PY), :]
        zlo = ez1[pl.ds(at + PY, 1), :]
        zhi = yon * ez1[pl.ds(at + PY + 1, 1), :]
        fe = fz(plane(ey1, x))
        d = 32.0 * (y_next(z, zhi) - z) - fe
        k = x if x < PX else PX + 1
        dlo = yin * (32.0 * (z[:1] - zlo) - elo[pl.ds(k, 1), :])
        ez = fplane(f, EZ, x) if x < PX else plane(xr, 1)
        e = mx[pl.ds(at, PY), :] * 1024.0 if x < PX else plane(xr, 4)
        ie = 1.0 / e
        put(r, k, 2.0 * z - ez + (32.0 * ie) * (d - y_prev(d, dlo)))
        if x < PX:
            t = plane(q1, x) + 32.0 * (ez1[pl.ds(at + XR, PY), :] - z)
            put(hy1, x, t)
            put(ex2, x, 2.0 * plane(ex1, x) - fplane(f, EX, x) + (0.5 * ie) * bz(fplane(f, HY, x) - t))
            put(q2, x, plane(hx1, x) + 0.5 * fe)
    m_at = lambda j: plane(m, j, YR)
    last, vn = sweep(m_at, lambda j: r[pl.ds(j, YR, stride=PY), :], PY, v2, YR)
    vn2[...] = vn
    pf, plast = ends(last, vn, plane(hb, 0, YR), plane(hb, 2, YR))
    spread(msg2, 1, (pf, plast))
    nc, ic = lax.axis_size("gc"), lax.axis_index("gc")
    spread(part2, 1, shares(pf, plast, (tp, bp, ts, bs), nc, ic, YR, YR))


def k_y4(msg, h, b, v2, vn2, hb, *more):
    coi, coo, (ex2, hy1, q2, out, al, ga, w2, dw) = more[:6], more[6:12], more[12:]
    nz, nc = lax.axis_size("gz"), lax.axis_size("gc")
    iz, ic = lax.axis_index("gz"), lax.axis_index("gc")
    left, right = gathered(msg, nz, nc, iz, ic, YR, YR, coi, coo, al, ga)
    lw = left * plane(hb, 1, YR)
    rw = (right - vn2[...]) * plane(hb, 0, YR)
    later = right
    for j in range(PY - 1, -1, -1):
        w = plane(v2, j, YR) + plane(b, j, YR) * lw + plane(h, j, YR) * rw
        w2[pl.ds(j, YR, stride=PY), :] = w
        dw[pl.ds(j, YR, stride=PY), :] = later - w
        later = w
    xon = jnp.where(x_index() < x_size() - 1, 1.0, 0.0)
    for x in range(PX):
        w = plane(w2, x)
        nxt = plane(w2, x + 1) if x < PX - 1 else xon * plane(w2, PX + 1)
        e2 = plane(ex2, x)
        put(out, EX * PX + x, e2)
        put(out, EZ * PX + x, w)
        put(out, HX * PX + x, plane(q2, x) - 32.0 * plane(dw, x))
        put(out, HY * PX + x, plane(hy1, x) - 0.5 * fz(e2) + 32.0 * (nxt - w))


def k_x4(msg, h, b, v2, vn2, hb, *more):
    coi, coo, (p2, out, al, ga) = more[:6], more[6:12], more[12:]
    na, nb = lax.axis_size("ga"), lax.axis_size("gb")
    ia, ib = lax.axis_index("ga"), lax.axis_index("gb")
    left, right = gathered(msg, na, nb, ia, ib, PY, XR, coi, coo, al, ga)
    lw = left * hb[pl.ds(XR, PY), :]
    rw = (right - vn2[...]) * hb[pl.ds(0, PY), :]
    later = right
    for x in range(PX - 1, -1, -1):
        w = plane(v2, x) + b[pl.ds(x * XR, PY), :] * lw + h[pl.ds(x * XR, PY), :] * rw
        put(out, EY * PX + x, w)
        put(out, HZ * PX + x, plane(p2, x) - 32.0 * (later - w))
        later = w


def call(name, parts, args, outs, scratch=(), smem=(), into=(), flush=(), near=()):
    into, flush, scratch = dict(into), dict(flush), dict(scratch)
    moved = [k for k in args if k not in smem and (k not in near or k in into)]
    pieces = {k for group in flush.values() for k, _, _ in group}
    last = {k: max(i for i, (_, used) in enumerate(parts) if k in used) for k in outs}
    leave = [
        [(k, 0, outs[k]) for k in outs if last[k] == i and k not in pieces and k not in near]
        + list(flush.get(i, ()))
        for i in range(len(parts))
    ]
    own = [k for k in moved if k not in into]

    def body(*refs):
        take = iter(refs)
        hbm = {k: next(take) for k in args}
        results = {k: next(take) for k in outs}
        env = {k: next(take) for k in own}
        env.update({k: results[k] if k in near else next(take) for k in outs})
        env.update({k: next(take) for k in scratch})
        env.update({k: hbm[k] for k in args if k not in moved})
        sem_in, sem_out = next(take), next(take)
        pending = {}
        for i, k in enumerate(moved):
            where = env.get(k)
            if k in into:
                buffer, row = into[k]
                where = env[buffer].at[pl.ds(row(), args[k].shape[0]), :]
            copy = pltpu.make_async_copy(hbm[k], where, sem_in.at[i])
            copy.start()
            pending.setdefault(into[k][0] if k in into else k, []).append(copy)
        sent = []
        for i, (function, used) in enumerate(parts):
            for k in used:
                for copy in pending.pop(k, ()):
                    copy.wait()
            function(*[env[k] for k in used])
            for k, row, rows in leave[i]:
                window = pl.ds(row, rows)
                copy = pltpu.make_async_copy(
                    env[k].at[window, :], results[k].at[window, :], sem_out.at[len(sent)]
                )
                copy.start()
                sent.append(copy)
        for copy in sent:
            copy.wait()

    far, close, scalars = [
        pl.BlockSpec(memory_space=m) for m in (pltpu.HBM, pltpu.VMEM, pltpu.SMEM)
    ]
    got = pl.pallas_call(
        body,
        out_shape=[(pltpu.VMEM if k in near else pltpu.HBM)((c, PZ), F32) for k, c in outs.items()],
        in_specs=[scalars if k in smem else close if k in near else far for k in args],
        out_specs=[close if k in near else far for k in outs],
        scratch_shapes=[pltpu.VMEM(args[k].shape, args[k].dtype) for k in own]
        + [pltpu.VMEM((c, PZ), F32) for k, c in outs.items() if k not in near]
        + [pltpu.VMEM((c, PZ), F32) for c in scratch.values()]
        + [
            pltpu.SemaphoreType.DMA((len(moved),)),
            pltpu.SemaphoreType.DMA((max(1, sum(len(group) for group in leave)),)),
        ],
        compiler_params=pltpu.CompilerParams(vmem_limit_bytes=LIMIT * 1024 * 1024),
        cost_estimate=pl.CostEstimate(flops=1000, bytes_accessed=1000, transcendentals=0),
        name=name,
    )(*[a if k in smem else pltpu.with_memory_space_constraint(a, pltpu.VMEM if k in near else pltpu.HBM) for k, a in args.items()])
    return dict(zip(outs, got))


def ring(block, axis, step):
    n = lax.axis_size(axis)
    return lax.ppermute(block, axis, [(i, (i + step) % n) for i in range(n)])


def swap(msg, axis):
    n = lax.axis_size(axis)
    got = lax.all_to_all(msg.reshape(n, -1, PZ), axis, 0, 0, tiled=True)
    return got.reshape(-1, PZ)


def from_all(msg, axis, buffer):
    n = lax.axis_size(axis)
    rows = msg.shape[0]
    args, into = {}, {}
    for step in range(n):
        k = buffer + str(step)
        args[k] = ring(msg, axis, step) if step else msg

        def row(step=step):
            return pl.multiple_of(lax.rem(lax.axis_index(axis) - step + n, n) * rows, 8)

        into[k] = (buffer, row)
    return args, into


def from_groups(own, share, buffer):
    nz, nc = lax.axis_size("gz"), lax.axis_size("gc")
    rows = own.shape[0]
    args, into = {}, {}
    for z in range(nz):
        for c in range(nc):
            k = buffer + str(z * nc + c)
            route = [
                (i * nc + j, (i + z) % nz * nc + (j + c) % nc) for i in range(nz) for j in range(nc)
            ]
            sent = share if z else own
            args[k] = lax.ppermute(sent, ("gz", "gc"), route) if z or c else own

            def row(z=z, c=c):
                iz = lax.rem(lax.axis_index("gz") - z + nz, nz)
                ic = lax.rem(lax.axis_index("gc") - c + nc, nc)
                return pl.multiple_of((iz * nc + ic) * rows, 8)

            into[k] = (buffer, row)
    return args, into


def local(fields, region, eps_table):
    na, nb = lax.axis_size("ga"), lax.axis_size("gb")
    along_x, along_y = ("ga", "gb"), ("gz", "gc")
    nz, nc = lax.axis_size("gz"), lax.axis_size("gc")
    ny = nz * nc
    ey = (max(nz, nc) + 1) * YR
    cells = PX * PY
    nxl, nyl = PX * XR, PY * YR
    f = fields.reshape(6 * cells, PZ)
    reg = region.reshape(cells, PZ)
    xup, xdn, yup, ydn = edges(fields, region, eps_table)
    xl = ring(xup, along_x, 1)
    xr = ring(xdn, along_x, -1)
    yl = ring(yup, along_y, 1)
    yr = ring(ydn, along_y, -1)
    linex = ("mx", "hx", "bx", "vx", "hbx")
    liney = ("my", "hy", "by", "vy", "hby")
    one = call(
        "one",
        [
            (k_eps, ("reg", "table", "eps")),
            (k_x1, ("f", "eps", "xl", "xr", "yl", "yr", "msgx", "q1") + linex + ("r",)),
            (k_y1, ("f", "eps", "xl", "xr", "msgy", "p1", "ey1") + liney + ("rt", "ep")),
        ],
        dict(reg=reg, f=f, xl=xl, xr=xr, yl=yl, yr=yr, table=eps_table),
        dict(
            zip(
                ("msgx", "q1") + linex + ("msgy", "p1", "ey1") + liney,
                (nb * XB, cells, nxl, nxl, nxl, nxl, 4 * XR)
                + (7 * YR, cells + PY, cells + PY, nyl, nyl, nyl, nyl, 4 * YR),
            )
        ),
        dict(eps=cells, r=nxl, rt=YR * PY, ep=YR * PY),
        smem=("table",),
        near=("xl", "xr", "yl", "yr", "msgy"),
    )
    pair, into = from_all(one["msgy"], "gc", "gyi")
    group = call(
        "group",
        [
            (k_join_y, ("gyi", "msgyo")),
            (k_join_x, ("gi", "msgo", "inner")),
        ],
        dict(pair, gi=swap(one["msgx"], "gb")),
        dict(msgyo=YB, msgo=na * XB, inner=nb * XB),
        dict(gyi=nc * YB),
        into=into,
        near=("gi", "msgyo") + tuple(pair),
    )
    goto = swap(group["msgo"], "ga")
    argy, into_o = from_all(group["msgyo"], "gz", "gyo")
    argy.update(pair)
    into.update(into_o)
    chains = ("tp", "bp", "ts", "bs", "bet", "del")
    ci, co, cyi, cyo = [tuple(k + a for k in chains) for a in ("i", "o", "yi", "yo")]
    cx, cy = ci + co, cyi + cyo
    size = lambda n, rows: (n * rows,) * 4 + ((n + 1) * rows,) * 2
    keep = {k: one[k] for k in ("q1", "p1", "ey1") + linex + liney}
    two = call(
        "two",
        [
            (k_y2, ("gyi", "gyo", "p1", "hy", "by", "vy", "hby", "ex1", "p2", "elo") + cy + ("aly", "gay", "dex")),
            (
                k_x2,
                ("gi", "go", "f", "q1", "ey1", "p2", "hx", "bx", "vx", "mx", "hbx")
                + ("ez1", "hx1", "msgx2", "vx2", "vnx2")
                + cx
                + ("alx", "gax", "r"),
            ),
            (
                k_y3,
                ("f", "xr", "q1", "mx", "ey1", "ez1", "hx1", "ex1", "elo", "my", "hby")
                + cyi[:4] + ("msgy2", "party2", "vy2", "vny2", "ex2", "hy1", "q2", "rt"),
            ),
        ],
        dict(argy, gi=group["inner"], go=goto, xr=xr, f=f, **keep),
        dict(
            zip(
                ("p2",) + cy + ("msgx2", "vx2", "vnx2") + cx + ("msgy2", "party2", "vy2", "vny2", "ex2", "hy1", "q2"),
                (cells + PY,)
                + size(nc, YR)
                + size(nz, YR)
                + (na * nb * 2 * PY, cells, PY)
                + size(nb, XR)
                + size(na, XR)
                + (2 * YR, 2 * YR, nyl, YR, cells, cells, cells),
            )
        ),
        dict(
            gyi=nc * YB, gyo=nz * YB, ex1=YR * PY, elo=YR, aly=ey, gay=ey, dex=YR * PY,
            ez1=nxl + XR, hx1=cells, alx=(max(na, nb) + 1) * XR, gax=(max(na, nb) + 1) * XR, r=cells, rt=YR * PY,
        ),
        into=into,
        near=("go", "msgy2", "party2") + tuple(k for k in argy if k not in pair),
    )
    gotx = swap(two["msgx2"], along_x)
    argy, into = from_groups(two["msgy2"], two["party2"], "gy")
    need = {k: one[k] for k in ("hx", "bx", "hbx", "hy", "by", "hby")}
    need.update({k: two[k] for k in ("p2",) + cy + cx + ("vx2", "vnx2", "vy2", "vny2", "ex2", "hy1", "q2")})
    three = call(
        "three",
        [
            (
                k_y4,
                ("gy", "hy", "by", "vy2", "vny2", "hby") + cy + ("ex2", "hy1", "q2", "out")
                + ("aly", "gay", "w2", "dw"),
            ),
            (k_x4, ("gx", "hx", "bx", "vx2", "vnx2", "hbx") + cx + ("p2", "out", "alx", "gax")),
        ],
        dict(argy, gx=gotx, **need),
        dict(out=6 * cells),
        dict(
            gy=ny * 2 * YR, aly=ey, gay=ey, w2=YR * PY, dw=YR * PY,
            alx=(max(na, nb) + 1) * PY, gax=(max(na, nb) + 1) * PY,
        ),
        into=into,
        near=("gx",) + tuple(argy),
        flush={
            0: [("out", EX * cells, cells), ("out", EZ * cells, 3 * cells)],
            1: [("out", EY * cells, cells), ("out", HZ * cells, cells)],
        },
    )
    return three["out"].reshape(6, PX, PY, PZ)


def solution(mesh):
    nx, ny = mesh.devices.shape
    nb = max(d for d in range(1, nx + 1) if nx % d == 0 and d * d <= nx)
    shape = (nx // nb, nb, ny // 2, 2)
    grid = Mesh(mesh.devices.reshape(shape), ("ga", "gb", "gz", "gc"))
    columns = P(("ga", "gb"), ("gz", "gc"), None)
    return jax.shard_map(
        local,
        mesh=grid,
        in_specs=(P(None, *columns), columns, P()),
        out_specs=P(None, *columns),
        check_vma=False,
    )
```

```python
import functools

import jax
import jax.numpy as jnp
from jax import lax
from jax.experimental import pallas as pl
from jax.experimental.pallas import tpu as pltpu
from jax.sharding import Mesh
from jax.sharding import PartitionSpec as P

PX, PY, PZ = 16, 32, 128
XR = 40
YR = 24
F32 = jnp.float32
LIMIT = 30
NEAR = ()
EX, EY, EZ, HX, HY, HZ = range(6)


def x_index():
    return lax.axis_index("ga") * lax.axis_size("gb") + lax.axis_index("gb")


def y_index():
    return lax.axis_index("gz") * lax.axis_size("gc") + lax.axis_index("gc")


def y_size():
    return lax.axis_size("gz") * lax.axis_size("gc")


def x_size():
    return lax.axis_size("ga") * lax.axis_size("gb")


def sub():
    return lax.broadcasted_iota(jnp.int32, (PY, PZ), 0)


def lanes_of(v):
    return lax.broadcasted_iota(jnp.int32, v.shape, 1)


def z_next(v):
    return jnp.where(lanes_of(v) == PZ - 1, 0.0, pltpu.roll(v, PZ - 1, 1))


def z_prev(v):
    return jnp.where(lanes_of(v) == 0, 0.0, pltpu.roll(v, 1, 1))


def fz(v):
    return z_next(v) - v


def bz(v):
    return v - z_prev(v)


def y_prev(v, row):
    return jnp.where(sub() == 0, row, pltpu.roll(v, 1, 0))


def y_next(v, row):
    return jnp.where(sub() == PY - 1, row, pltpu.roll(v, PY - 1, 0))


def plane(ref, k, size=PY):
    return ref[pl.ds(k * size, size), :]


def put(ref, k, v, size=PY):
    ref[pl.ds(k * size, size), :] = v


def fplane(ref, f, x):
    return plane(ref, f * PX + x)


def lookup(region, table):
    level = [table[i] for i in range(16)]
    for bit in range(4):
        on = (region & (1 << bit)) != 0
        level = [jnp.where(on, level[2 * i + 1], level[2 * i]) for i in range(len(level) // 2)]
    return level[0]


def k_eps(reg, table, eps):
    tab = [table[i] for i in range(16)]
    for x in range(PX):
        put(eps, x, lookup(plane(reg, x), tab))


def k_edges(f, reg, table, xup, xdn, yup, ydn, tab, ends, low, high, rlow, rhigh, sems):
    up, down = (EX, EY, HY, HZ), (EY, EZ, HX, HZ)
    rows = (EX, HY, EZ, HX)
    top = pl.ds(PY - 8, 8)
    pairs = [(table, tab), (reg.at[PX - 1], ends.at[0]), (reg.at[0], ends.at[1])]
    pairs += [(reg.at[:, top, :], rhigh), (reg.at[:, pl.ds(0, 8), :], rlow)]
    for i in range(4):
        pairs += [
            (f.at[up[i], PX - 1], xup.at[pl.ds(i * PY, PY), :]),
            (f.at[down[i], 0], xdn.at[pl.ds(i * PY, PY), :]),
            (f.at[rows[i], :, top, :], high.at[i]),
            (f.at[rows[i], :, pl.ds(0, 8), :], low.at[i]),
        ]
    copies = [pltpu.make_async_copy(p, q, sems.at[i]) for i, (p, q) in enumerate(pairs)]
    for copy in copies:
        copy.start()
    for copy in copies:
        copy.wait()
    t = [tab[i] for i in range(16)]
    put(xup, 4, lookup(ends[0], t))
    put(xdn, 4, lookup(ends[1], t))
    for i in range(4):
        put(yup, i, high[i, :, 7, :], PX)
        put(ydn, i, low[i, :, 0, :], PX)
    put(yup, 4, high[3, :, 6, :], PX)
    put(yup, 5, lookup(rhigh[:, 7, :], t), PX)
    put(ydn, 4, lookup(rlow[:, 0, :], t), PX)


def edges(fields, region, eps_table):
    vmem, hbm = [pl.BlockSpec(memory_space=m) for m in (pltpu.VMEM, pltpu.HBM)]
    return pl.pallas_call(
        k_edges,
        out_shape=[pltpu.VMEM((c, PZ), F32) for c in (5 * PY, 5 * PY, 6 * PX, 6 * PX)],
        in_specs=[hbm] * 3,
        out_specs=[vmem] * 4,
        scratch_shapes=[
            pltpu.SMEM((16,), F32),
            pltpu.VMEM((2, PY, PZ), jnp.int32),
            pltpu.VMEM((4, PX, 8, PZ), F32),
            pltpu.VMEM((4, PX, 8, PZ), F32),
            pltpu.VMEM((PX, 8, PZ), jnp.int32),
            pltpu.VMEM((PX, 8, PZ), jnp.int32),
            pltpu.SemaphoreType.DMA((21,)),
        ],
        cost_estimate=pl.CostEstimate(flops=1000, bytes_accessed=1000, transcendentals=0),
        name="edges",
    )(*[pltpu.with_memory_space_constraint(v, pltpu.HBM) for v in (fields, region, eps_table)])


def factor(m_at, count, first, h, b, rows):
    hv = jnp.ones((rows, PZ), F32)
    hs = jnp.where(first, jnp.zeros_like(hv), jnp.ones_like(hv))
    bv = jnp.ones((rows, PZ), F32)
    bs = jnp.ones((rows, PZ), F32)
    for i in range(count):
        k = count - 1 - i
        put(h, i, hv, rows)
        put(b, k, bv, rows)
        hs = hs + m_at(i) * hv
        bs = bs + m_at(k) * bv
        hlast, blast = hv, bv
        hv = hv + hs
        bv = bv + bs
    hn = 1.0 / hv
    bn = 1.0 / bv
    return hn, bn, blast * bn, hn, hlast * hn


def sweep(m_at, r_at, count, v, rows):
    vv = jnp.zeros((rows, PZ), F32)
    vs = jnp.zeros((rows, PZ), F32)
    for i in range(count):
        put(v, i, vv, rows)
        vs = vs + m_at(i) * (vv - r_at(i))
        last = vv
        vv = vv + vs
    return last, vv


def ends(last, vn, hn, c):
    return -vn * hn, last - c * vn


def spread(msg, count, values):
    block = sum(v.shape[0] for v in values)
    for k in range(count):
        at = k * block
        for v in values:
            msg[pl.ds(at, v.shape[0]), :] = v
            at += v.shape[0]


def k_x1(f, eps, xl, xr, yl, yr, msg, q1, m, h, b, v, hb, r):
    gx = x_index()
    gy = y_index()
    xlo = gx > 0
    ylo = gy > 0
    yhi = gy < y_size() - 1
    yin = jnp.where(ylo, 1.0, 0.0)
    yon = jnp.where(yhi, 1.0, 0.0)
    q1lo = yin * (plane(yl, 1, PX) - 0.5 * fz(plane(yl, 0, PX)))
    q1hi = yon * (plane(yr, 1, PX) - 0.5 * fz(plane(yr, 0, PX)))
    hxlo = yin * plane(yl, 3, PX)
    epslo = plane(yl, 5, PX)
    epshi = plane(yr, 4, PX)
    hx31 = f[pl.ds(HX * PX * PY + PY - 1, PX, stride=PY), :]
    bxlo = jnp.concatenate([q1lo[:1], q1lo[1:] - q1lo[:-1]], 0)
    bxhi = jnp.concatenate([q1hi[:1], q1hi[1:] - q1hi[:-1]], 0)
    rlo = yin * plane(yl, 2, PX) + (32.0 / epslo) * (bxlo - (hxlo - yin * plane(yl, 4, PX)))
    rhi = yon * plane(yr, 2, PX) + (32.0 / epshi) * (bxhi - (yon * plane(yr, 3, PX) - hx31))
    pad = jnp.zeros((XR - PY - 2, PZ), F32)
    one = jnp.ones((XR - PY - 2, PZ), F32)
    before = jnp.where(xlo, plane(xl, 2) - 0.5 * fz(plane(xl, 0)), 0.0)
    for x in range(PX):
        q = fplane(f, HY, x) - 0.5 * fz(fplane(f, EX, x))
        put(q1, x, q)
        e = plane(eps, x)
        hx = fplane(f, HX, x)
        ce = 32.0 / e
        rr = fplane(f, EZ, x) + ce * ((q - before) - (hx - y_prev(hx, hxlo[x : x + 1])))
        before = q
        r[pl.ds(x * XR, PY), :] = rr
        r[pl.ds(x * XR + PY, 8), :] = jnp.concatenate([rlo[x : x + 1], rhi[x : x + 1], pad], 0)
        m[pl.ds(x * XR, PY), :] = e * (1.0 / 1024.0)
        m[pl.ds(x * XR + PY, 8), :] = (
            jnp.concatenate([epslo[x : x + 1], epshi[x : x + 1], one], 0) * (1.0 / 1024.0)
        )
    m_at = lambda i: plane(m, i, XR)
    hn, bn, a, bb, c = factor(m_at, PX, gx == 0, h, b, XR)
    last, vn = sweep(m_at, lambda i: plane(r, i, XR), PX, v, XR)
    pf, plast = ends(last, vn, hn, c)
    put(hb, 0, hn, XR)
    put(hb, 1, bn, XR)
    put(hb, 2, c, XR)
    put(hb, 3, vn, XR)
    zq = jnp.zeros((6, PZ), F32)
    qq = jnp.concatenate([q1lo[PX - 1 :], q1hi[PX - 1 :], zq], 0) * (-1.0 / 32.0)
    spread(msg, lax.axis_size("gb"), (pf, plast, a, bb, c, qq))


def k_y1(f, eps, xl, xr, msg, p1, ey1, m, h, b, v, hb, r, ep):
    gx = x_index()
    gy = y_index()
    n = y_size()
    xlo = gx > 0
    xin = jnp.where(xlo, 1.0, 0.0)
    xon = jnp.where(gx < x_size() - 1, 1.0, 0.0)
    zero = jnp.zeros((1, PZ), F32)
    zeros = jnp.zeros((PY, PZ), F32)
    exl, eyl, hyl, hzl = [xin * plane(xl, i) for i in range(4)]
    eyr, ezr, hxr, hzr = [xon * plane(xr, i) for i in range(4)]
    for x in range(PX):
        put(ep, x, plane(eps, x))
    put(ep, PX, plane(xl, 4))
    put(ep, PX + 1, plane(xr, 4))
    for x in range(PX + 2, YR):
        put(ep, x, zeros + 1.0)
        put(r, x, zeros)
    put(r, PX + 1, zeros)

    def rex(ex, hy, pp, e):
        ie = 1.0 / e
        return ex + (32.0 * ie) * (pp - y_prev(pp, zero)) - (0.5 * ie) * bz(hy)

    p = hzl - 32.0 * (fplane(f, EY, 0) - eyl)
    p = jnp.where(xlo, p, 0.0)
    put(p1, PX, p)
    put(r, PX, rex(exl, hyl, p, plane(ep, PX)))
    for x in range(PX):
        ey = fplane(f, EY, x)
        nxt = fplane(f, EY, x + 1) if x < PX - 1 else eyr
        hz = fplane(f, HZ, x)
        hzp = fplane(f, HZ, x - 1) if x > 0 else hzl
        e = plane(ep, x)
        p = hz - 32.0 * (nxt - ey)
        put(p1, x, p)
        put(r, x, rex(fplane(f, EX, x), fplane(f, HY, x), p, e))
        ie = 1.0 / e
        put(ey1, x, ey + (0.5 * ie) * bz(fplane(f, HX, x)) - (32.0 * ie) * (hz - hzp))
    ie = 1.0 / plane(ep, PX + 1)
    put(ey1, PX, eyr + (0.5 * ie) * bz(hxr) - (32.0 * ie) * (hzr - fplane(f, HZ, PX - 1)))

    def rows(ref, j):
        return ref[pl.ds(j, YR, stride=PY), :]

    for j in range(PY):
        put(m, j, rows(ep, j) * (1.0 / 1024.0), YR)
    m_at = lambda j: plane(m, j, YR)
    hn, bn, a, bb, c = factor(m_at, PY, gy == 0, h, b, YR)
    last, vn = sweep(m_at, lambda j: rows(r, j), PY, v, YR)
    pf, plast = ends(last, vn, hn, c)
    put(hb, 0, hn, YR)
    put(hb, 1, bn, YR)
    put(hb, 2, c, YR)
    put(hb, 3, vn, YR)
    lastrow = lambda ref, at, k: ref[pl.ds(at * PY + PY - 1, k, stride=PY), :]
    tail = jnp.zeros((7, PZ), F32)
    qq = jnp.concatenate([lastrow(p1, 0, PX), lastrow(p1, PX, 1), tail], 0) * (-1.0 / 32.0)
    tail = jnp.zeros((6, PZ), F32)
    ee = fz(jnp.concatenate([lastrow(ey1, 0, PX), zero, lastrow(ey1, PX, 1), tail], 0))
    spread(msg, 1, (pf, plast, a, bb, c, qq, ee))


def coefficients(part, n, rows, tp, bp, ts, bs, bet, dele):
    zero = jnp.zeros((rows, PZ), F32)
    beta = zero
    put(bet, 0, zero, rows)
    for j in range(n):
        a, b, c = part(j, 2), part(j, 3), part(j, 4)
        bd = b / (1.0 - a * beta)
        t = bd * beta
        put(tp, j, t, rows)
        put(bp, j, bd, rows)
        beta = c + t * b
        put(bet, j + 1, beta, rows)
    delta = zero
    put(dele, n, zero, rows)
    for j in range(n - 1, -1, -1):
        a, b, c = part(j, 2), part(j, 3), part(j, 4)
        bd = b / (1.0 - c * delta)
        t = bd * delta
        put(ts, j, t, rows)
        put(bs, j, bd, rows)
        delta = a + t * b
        put(dele, j, delta, rows)


def chain(part, n, rows, crows, tp, bp, ts, bs, al, ga, start, stop):
    take = lambda ref, j: ref[pl.ds(j * crows, rows), :]
    alpha, gamma = start, stop
    put(al, 0, alpha, rows)
    put(ga, n, gamma, rows)
    for j in range(n):
        k = n - 1 - j
        alpha = part(j, 1) + take(tp, j) * part(j, 0) + take(bp, j) * alpha
        gamma = part(k, 0) + take(ts, k) * part(k, 1) + take(bs, k) * gamma
        put(al, j + 1, alpha, rows)
        put(ga, k, gamma, rows)
    return gamma, alpha


def interface(part, n, me, rows, coefs, al, ga, start=None, stop=None, crows=None):
    crows = crows or rows
    tp, bp, ts, bs, bet, dele = coefs
    zero = jnp.zeros((rows, PZ), F32)
    start = zero if start is None else start
    stop = zero if stop is None else stop
    chain(part, n, rows, crows, tp, bp, ts, bs, al, ga, start, stop)
    at = lambda ref, d, size: ref[pl.ds(pl.multiple_of(d * size, 8), rows), :]
    a0, a1 = at(al, me, rows), at(al, me + 1, rows)
    g0, g1 = at(ga, me, rows), at(ga, me + 1, rows)
    b0, b1 = at(bet, me, crows), at(bet, me + 1, crows)
    d0, d1 = at(dele, me, crows), at(dele, me + 1, crows)
    left = a0 + b0 * ((g0 + d0 * a0) / (1.0 - d0 * b0))
    right = g1 + d1 * ((a1 + b1 * g1) / (1.0 - b1 * d1))
    return left, right


XB = 5 * XR + 8


def x_raw(msg):
    return lambda j, k: msg[pl.ds(j * XB + k * XR, XR), :]


def x_part(msg):
    def part(j, k):
        if j == 0:
            return x_raw(msg)(j, k)
        own = msg[pl.ds(j * XB + k * XR, PY), :]
        more = (
            msg[pl.ds(j * XB + k * XR + PY, 8), :]
            + msg[pl.ds(j * XB + (2 + k) * XR + PY, 8), :] * msg[pl.ds((j - 1) * XB + 5 * XR, 8), :]
        )
        return jnp.concatenate([own, more], 0)

    return part


def x_passed(msg, me):
    prev = pl.multiple_of(jnp.maximum(me - 1, 0) * XB, 8)
    return jnp.where(me > 0, msg[pl.ds(prev + 5 * XR, 8), :], 0.0)


YB = 7 * YR


def y_raw(msg):
    return lambda j, k: msg[pl.ds(j * YB + k * YR, YR), :]


def y_part(msg):
    raw = y_raw(msg)
    return lambda j, k: raw(j, k) + raw(j, 2 + k) * raw(j - 1, 5) if j else raw(j, k)


def y_passed(msg, me, k):
    prev = pl.multiple_of(jnp.maximum(me - 1, 0) * YB, 8)
    return jnp.where(me > 0, msg[pl.ds(prev + k * YR, YR), :], 0.0)


def k_y2(gi, go, p1, h, b, v, hb, ex1, p2, elo, *more):
    coi, coo, (al, ga, dex) = more[:6], more[6:12], more[12:]
    nz, nc = lax.axis_size("gz"), lax.axis_size("gc")
    iz, ic = lax.axis_index("gz"), lax.axis_index("gc")
    coefficients(y_raw(go), nz, YR, *coo)
    coefficients(y_raw(gi), nc, YR, *coi)
    left, right = interface(y_part(go), nz, iz, YR, coo, al, ga)
    left = left + y_passed(go, iz, 5)
    left, right = interface(y_part(gi), nc, ic, YR, coi, al, ga, left, right)
    left = left + y_passed(gi, ic, 5)
    elo[...] = jnp.where(ic > 0, y_passed(gi, ic, 6), y_passed(go, iz, 6))
    lw = left * plane(hb, 1, YR)
    rw = (right - plane(hb, 3, YR)) * plane(hb, 0, YR)
    later = right
    for j in range(PY - 1, -1, -1):
        w = plane(v, j, YR) + plane(b, j, YR) * lw + plane(h, j, YR) * rw
        ex1[pl.ds(j, YR, stride=PY), :] = w
        dex[pl.ds(j, YR, stride=PY), :] = later - w
        later = w
    live = jnp.where(x_index() > 0, 1.0, 0.0)
    for x in range(PX):
        put(p2, x, plane(p1, x) + 64.0 * plane(dex, x))
    put(p2, PX, live * (plane(p1, PX) + 64.0 * plane(dex, PX)))


def join(part, raw, count):
    pf, ph, a, b, c = part(0, 0), part(0, 1), raw(0, 2), raw(0, 3), raw(0, 4)
    for j in range(1, count):
        qf, qh, a2, b2, c2 = part(j, 0), part(j, 1), raw(j, 2), raw(j, 3), raw(j, 4)
        den = 1.0 / (1.0 - c * a2)
        low, high = b * den, b2 * den
        pf, ph = pf + low * (qf + a2 * ph), qh + high * (ph + c * qf)
        a, b, c = a + low * b * a2, low * b2, c2 + high * b2 * c
    return pf, ph, a, b, c


def k_join_y(gi, msg):
    nc = lax.axis_size("gc")
    raw = y_raw(gi)
    spread(msg, 1, join(y_part(gi), raw, nc) + (raw(nc - 1, 5), raw(nc - 1, 6)))


def k_join_x(gi, msg, inner):
    inner[...] = gi[...]
    nb = lax.axis_size("gb")
    last = gi[pl.ds((nb - 1) * XB + 5 * XR, 8), :]
    spread(msg, lax.axis_size("ga"), join(x_part(gi), x_raw(gi), nb) + (last,))


def shares(pf, ph, coefs, count, me, rows, crows):
    tp, bp, ts, bs = coefs[:4]
    low = high = jnp.ones((rows, PZ), F32)
    for k in range(count):
        low = jnp.where(k < me, low * bs[pl.ds(k * crows, rows), :], low)
        high = jnp.where(k > me, high * bp[pl.ds(k * crows, rows), :], high)
    mine = pl.ds(pl.multiple_of(me * crows, 8), rows)
    return low * (pf + ts[mine, :] * ph), high * (ph + tp[mine, :] * pf)


def gathered(msg, n, m, ia, ib, rows, crows, coi, coo, al, ga):
    zero = jnp.zeros((rows, PZ), F32)

    def inside(j, k):
        at = pl.multiple_of(((ia * m + j) * 2 + k) * rows, 8)
        return msg[pl.ds(at, rows), :]

    whole = chain(inside, m, rows, crows, *coi[:4], al, ga, zero, zero)

    def group(j, k):
        total = sum(msg[pl.ds(((j * m + i) * 2 + k) * rows, rows), :] for i in range(m))
        return jnp.where(ia == j, whole[k], total)

    left, right = interface(group, n, ia, rows, coo, al, ga, crows=crows)
    return interface(inside, m, ib, rows, coi, al, ga, left, right, crows)


def k_x2(gi, go, f, q1, ey1, p2, h, b, v, m, hb, ez1, hx1, msg2, v2, vn2, *more):
    coi, coo, (al, ga, r) = more[:6], more[6:12], more[12:]
    na, nb = lax.axis_size("ga"), lax.axis_size("gb")
    ia, ib = lax.axis_index("ga"), lax.axis_index("gb")
    gy = y_index()
    yon = jnp.where(gy < y_size() - 1, 1.0, 0.0)
    coefficients(x_raw(go), na, XR, *coo)
    coefficients(x_raw(gi), nb, XR, *coi)
    left, right = interface(x_part(go), na, ia, XR, coo, al, ga)
    left = jnp.concatenate([left[:PY], left[PY:] + x_passed(go, ia)], 0)
    left, right = interface(x_part(gi), nb, ib, XR, coi, al, ga, left, right)
    left = jnp.concatenate([left[:PY], left[PY:] + x_passed(gi, ib)], 0)
    lw = left * plane(hb, 1, XR)
    rw = (right - plane(hb, 3, XR)) * plane(hb, 0, XR)
    for x in range(PX):
        put(ez1, x, plane(v, x, XR) + plane(b, x, XR) * lw + plane(h, x, XR) * rw, XR)
    put(ez1, PX, right, XR)
    before = plane(p2, PX)
    for x in range(PX):
        z = ez1[pl.ds(x * XR, PY), :]
        z32 = yon * ez1[pl.ds(x * XR + PY + 1, 1), :]
        ey = plane(ey1, x)
        t = fplane(f, HX, x) - 32.0 * (y_next(z, z32) - z) + 0.5 * fz(ey)
        put(hx1, x, t)
        p = plane(p2, x)
        ie = 1.0 / (m[pl.ds(x * XR, PY), :] * 1024.0)
        put(r, x, ey + (0.5 * ie) * bz(t) - (32.0 * ie) * (p - before))
        before = p
    last, vn = sweep(lambda i: m[pl.ds(i * XR, PY), :], lambda i: plane(r, i), PX, v2, PY)
    vn2[...] = vn
    pf, plast = ends(last, vn, hb[pl.ds(0, PY), :], hb[pl.ds(2 * XR, PY), :])
    share = shares(pf, plast, coi, nb, ib, PY, XR)
    for k in range(na * nb):
        for i, (own, joined) in enumerate(zip((pf, plast), share)):
            put(msg2, 2 * k + i, jnp.where(ia == k // nb, own, joined))


def k_y3(f, xr, q1, mx, ey1, ez1, hx1, ex1, elo, ex2, hy1, q2, r):
    n = y_size()
    gy = y_index()
    yon = jnp.where(gy < n - 1, 1.0, 0.0)
    yin = jnp.where(gy > 0, 1.0, 0.0)
    zeros = jnp.zeros((PY, PZ), F32)
    for x in range(PX + 2, YR):
        put(r, x, zeros)
    put(r, PX, zeros)
    for x in range(PX + 1):
        at = x * XR
        z = ez1[pl.ds(at, PY), :]
        zlo = ez1[pl.ds(at + PY, 1), :]
        zhi = yon * ez1[pl.ds(at + PY + 1, 1), :]
        fe = fz(plane(ey1, x))
        d = 32.0 * (y_next(z, zhi) - z) - fe
        k = x if x < PX else PX + 1
        dlo = yin * (32.0 * (z[:1] - zlo) - elo[pl.ds(k, 1), :])
        ez = fplane(f, EZ, x) if x < PX else plane(xr, 1)
        e = mx[pl.ds(at, PY), :] * 1024.0 if x < PX else plane(xr, 4)
        ie = 1.0 / e
        put(r, k, 2.0 * z - ez + (32.0 * ie) * (d - y_prev(d, dlo)))
        if x < PX:
            t = plane(q1, x) + 32.0 * (ez1[pl.ds(at + XR, PY), :] - z)
            put(hy1, x, t)
            put(ex2, x, 2.0 * plane(ex1, x) - fplane(f, EX, x) + (0.5 * ie) * bz(fplane(f, HY, x) - t))
            put(q2, x, plane(hx1, x) + 0.5 * fe)


def k_y3_sweep(r, m, hb, msg2, v2, vn2):
    m_at = lambda j: plane(m, j, YR)
    last, vn = sweep(m_at, lambda j: r[pl.ds(j, YR, stride=PY), :], PY, v2, YR)
    vn2[...] = vn
    pf, plast = ends(last, vn, plane(hb, 0, YR), plane(hb, 2, YR))
    spread(msg2, 1, (pf, plast))


def y_ends(msg):
    return lambda j, k: msg[pl.ds((2 * j + k) * YR, YR), :]


def k_join_ends(gi, tp, bp, ts, bs, msg, al, ga):
    nc = lax.axis_size("gc")
    zero = jnp.zeros((YR, PZ), F32)
    spread(msg, 1, chain(y_ends(gi), nc, YR, YR, tp, bp, ts, bs, al, ga, zero, zero))


def k_y4(gi, go, h, b, v2, vn2, hb, *more):
    coi, coo, (ex2, hy1, q2, out, al, ga, w2, dw) = more[:6], more[6:12], more[12:]
    nz, nc = lax.axis_size("gz"), lax.axis_size("gc")
    iz, ic = lax.axis_index("gz"), lax.axis_index("gc")
    left, right = interface(y_ends(go), nz, iz, YR, coo, al, ga)
    left, right = interface(y_ends(gi), nc, ic, YR, coi, al, ga, left, right)
    lw = left * plane(hb, 1, YR)
    rw = (right - vn2[...]) * plane(hb, 0, YR)
    later = right
    for j in range(PY - 1, -1, -1):
        w = plane(v2, j, YR) + plane(b, j, YR) * lw + plane(h, j, YR) * rw
        w2[pl.ds(j, YR, stride=PY), :] = w
        dw[pl.ds(j, YR, stride=PY), :] = later - w
        later = w
    xon = jnp.where(x_index() < x_size() - 1, 1.0, 0.0)
    for x in range(PX):
        w = plane(w2, x)
        nxt = plane(w2, x + 1) if x < PX - 1 else xon * plane(w2, PX + 1)
        e2 = plane(ex2, x)
        put(out, EX * PX + x, e2)
        put(out, EZ * PX + x, w)
        put(out, HX * PX + x, plane(q2, x) - 32.0 * plane(dw, x))
        put(out, HY * PX + x, plane(hy1, x) - 0.5 * fz(e2) + 32.0 * (nxt - w))


def k_x4(msg, h, b, v2, vn2, hb, *more):
    coi, coo, (p2, out, al, ga) = more[:6], more[6:12], more[12:]
    na, nb = lax.axis_size("ga"), lax.axis_size("gb")
    ia, ib = lax.axis_index("ga"), lax.axis_index("gb")
    left, right = gathered(msg, na, nb, ia, ib, PY, XR, coi, coo, al, ga)
    lw = left * hb[pl.ds(XR, PY), :]
    rw = (right - vn2[...]) * hb[pl.ds(0, PY), :]
    later = right
    for x in range(PX - 1, -1, -1):
        w = plane(v2, x) + b[pl.ds(x * XR, PY), :] * lw + h[pl.ds(x * XR, PY), :] * rw
        put(out, EY * PX + x, w)
        put(out, HZ * PX + x, plane(p2, x) - 32.0 * (later - w))
        later = w


def call(name, parts, args, outs, scratch=(), smem=(), into=(), flush=(), near=(), only=()):
    into, flush, scratch, only = dict(into), dict(flush), dict(scratch), dict(only)
    moved = [k for k in args if k not in smem and (k not in near or k in into)]
    pieces = {k for group in flush.values() for k, _, _ in group}
    last = {k: max(i for i, (_, used) in enumerate(parts) if k in used) for k in outs}
    leave = [
        [(k, 0, outs[k]) for k in outs if last[k] == i and k not in pieces and k not in near]
        + list(flush.get(i, ()))
        for i in range(len(parts))
    ]
    own = [k for k in moved if k not in into]

    def body(*refs):
        take = iter(refs)
        hbm = {k: next(take) for k in args}
        results = {k: next(take) for k in outs}
        env = {k: next(take) for k in own}
        env.update({k: results[k] if k in near else next(take) for k in outs})
        env.update({k: next(take) for k in scratch})
        env.update({k: hbm[k] for k in args if k not in moved})
        sem_in, sem_out = next(take), next(take)
        pending = {}
        count = 0
        for k in moved:
            pairs = [(hbm[k], env.get(k))]
            if k in into:
                buffer, row = into[k]
                pairs = [(hbm[k], env[buffer].at[pl.ds(row(), args[k].shape[0]), :])]
            elif k in only:
                windows = [pl.ds(at, rows) for at, rows in only[k]]
                pairs = [(hbm[k].at[w, :], env[k].at[w, :]) for w in windows]
            for source, where in pairs:
                copy = pltpu.make_async_copy(source, where, sem_in.at[count])
                copy.start()
                count += 1
                pending.setdefault(into[k][0] if k in into else k, []).append(copy)
        sent = []
        for i, (function, used) in enumerate(parts):
            for k in used:
                for copy in pending.pop(k, ()):
                    copy.wait()
            function(*[env[k] for k in used])
            for k, row, rows in leave[i]:
                window = pl.ds(row, rows)
                copy = pltpu.make_async_copy(
                    env[k].at[window, :], results[k].at[window, :], sem_out.at[len(sent)]
                )
                copy.start()
                sent.append(copy)
        for copy in sent:
            copy.wait()

    far, close, scalars = [
        pl.BlockSpec(memory_space=m) for m in (pltpu.HBM, pltpu.VMEM, pltpu.SMEM)
    ]
    got = pl.pallas_call(
        body,
        out_shape=[(pltpu.VMEM if k in near else pltpu.HBM)((c, PZ), F32) for k, c in outs.items()],
        in_specs=[scalars if k in smem else close if k in near else far for k in args],
        out_specs=[close if k in near else far for k in outs],
        scratch_shapes=[pltpu.VMEM(args[k].shape, args[k].dtype) for k in own]
        + [pltpu.VMEM((c, PZ), F32) for k, c in outs.items() if k not in near]
        + [pltpu.VMEM((c, PZ), F32) for c in scratch.values()]
        + [
            pltpu.SemaphoreType.DMA((sum(len(only.get(k, (0,))) for k in moved),)),
            pltpu.SemaphoreType.DMA((max(1, sum(len(group) for group in leave)),)),
        ],
        compiler_params=pltpu.CompilerParams(vmem_limit_bytes=LIMIT * 1024 * 1024),
        cost_estimate=pl.CostEstimate(flops=1000, bytes_accessed=1000, transcendentals=0),
        name=name,
    )(*[a if k in smem else pltpu.with_memory_space_constraint(a, pltpu.VMEM if k in near else pltpu.HBM) for k, a in args.items()])
    return dict(zip(outs, got))


def ring(block, axis, step):
    n = lax.axis_size(axis)
    return lax.ppermute(block, axis, [(i, (i + step) % n) for i in range(n)])


def swap(msg, axis):
    n = lax.axis_size(axis)
    got = lax.all_to_all(msg.reshape(n, -1, PZ), axis, 0, 0, tiled=True)
    return got.reshape(-1, PZ)


def from_all(msg, axis, buffer):
    n = lax.axis_size(axis)
    rows = msg.shape[0]
    args, into = {}, {}
    for step in range(n):
        k = buffer + str(step)
        args[k] = ring(msg, axis, step) if step else msg

        def row(step=step):
            return pl.multiple_of(lax.rem(lax.axis_index(axis) - step + n, n) * rows, 8)

        into[k] = (buffer, row)
    return args, into


def local(fields, region, eps_table):
    na, nb = lax.axis_size("ga"), lax.axis_size("gb")
    along_x, along_y = ("ga", "gb"), ("gz", "gc")
    nz, nc = lax.axis_size("gz"), lax.axis_size("gc")
    ny = nz * nc
    ey = (max(nz, nc) + 1) * YR
    cells = PX * PY
    nxl, nyl = PX * XR, PY * YR
    f = fields.reshape(6 * cells, PZ)
    reg = region.reshape(cells, PZ)
    xup, xdn, yup, ydn = edges(fields, region, eps_table)
    xl = ring(xup, along_x, 1)
    xr = ring(xdn, along_x, -1)
    yl = ring(yup, along_y, 1)
    yr = ring(ydn, along_y, -1)
    linex = ("mx", "hx", "bx", "vx", "hbx")
    liney = ("my", "hy", "by", "vy", "hby")
    one = call(
        "onex",
        [
            (k_eps, ("reg", "table", "eps")),
            (k_x1, ("f", "eps", "xl", "xr", "yl", "yr", "msgx", "q1") + linex + ("r",)),
        ],
        dict(xl=xl, xr=xr, yl=yl, yr=yr, reg=reg, f=f, table=eps_table),
        dict(zip(("eps", "q1") + linex + ("msgx",), (cells, cells, nxl, nxl, nxl, nxl, 4 * XR, nb * XB))),
        dict(r=nxl),
        smem=("table",),
        near=("xl", "xr", "yl", "yr") + NEAR,
        flush={0: [("eps", 0, cells)]},
        only=dict(f=[(EX * cells, cells), (EZ * cells, 3 * cells)]),
    )
    oney = call(
        "oney",
        [(k_y1, ("f", "eps", "xl", "xr", "msgy", "p1", "ey1") + liney + ("rt", "ep"))],
        dict(f=f, eps=one["eps"], xl=xl, xr=xr),
        dict(
            zip(
                ("msgy", "p1", "ey1") + liney,
                (7 * YR, cells + PY, cells + PY, nyl, nyl, nyl, nyl, 4 * YR),
            )
        ),
        dict(rt=YR * PY, ep=YR * PY),
        near=("msgy",),
        only=dict(f=[(EX * cells, 2 * cells), (HX * cells, 3 * cells)]),
    )
    one.update(oney)
    pair, into = from_all(one["msgy"], "gc", "gyi")
    group = call(
        "group",
        [
            (k_join_y, ("gyi", "msgyo")),
            (k_join_x, ("gi", "msgo", "inner")),
        ],
        dict(pair, gi=swap(one["msgx"], "gb")),
        dict(msgyo=YB, msgo=na * XB, inner=nb * XB),
        dict(gyi=nc * YB),
        into=into,
        near=("gi", "msgyo") + NEAR + tuple(pair),
    )
    goto = swap(group["msgo"], "ga")
    argy, into_o = from_all(group["msgyo"], "gz", "gyo")
    argy.update(pair)
    into.update(into_o)
    chains = ("tp", "bp", "ts", "bs", "bet", "del")
    ci, co, cyi, cyo = [tuple(k + a for k in chains) for a in ("i", "o", "yi", "yo")]
    cx, cy = ci + co, cyi + cyo
    size = lambda n, rows: (n * rows,) * 4 + ((n + 1) * rows,) * 2
    keep = {k: one[k] for k in ("q1", "p1", "ey1") + linex + liney}
    two = call(
        "two",
        [
            (k_y2, ("gyi", "gyo", "p1", "hy", "by", "vy", "hby", "ex1", "p2", "elo") + cy + ("aly", "gay", "dex")),
            (
                k_x2,
                ("gi", "go", "f", "q1", "ey1", "p2", "hx", "bx", "vx", "mx", "hbx")
                + ("ez1", "hx1", "msgx2", "vx2", "vnx2")
                + cx
                + ("alx", "gax", "r"),
            ),
            (
                k_y3,
                ("f", "xr", "q1", "mx", "ey1", "ez1", "hx1", "ex1", "elo", "ex2", "hy1", "q2", "rt"),
            ),
            (k_y3_sweep, ("rt", "my", "hby", "msgy2", "vy2", "vny2")),
        ],
        dict(argy, **{k: keep[k] for k in ("hby", "vy", "by", "hy", "p1")}, gi=group["inner"], go=goto, f=f, xr=xr, **{k: keep[k] for k in linex + ("ey1", "q1", "my")}),
        dict(
            zip(
                ("p2",) + cy + ("msgx2", "vx2", "vnx2") + cx + ("msgy2", "vy2", "vny2", "ex2", "hy1", "q2"),
                (cells + PY,)
                + size(nc, YR)
                + size(nz, YR)
                + (na * nb * 2 * PY, cells, PY)
                + size(nb, XR)
                + size(na, XR)
                + (2 * YR, nyl, YR, cells, cells, cells),
            )
        ),
        dict(
            gyi=nc * YB, gyo=nz * YB, ex1=YR * PY, elo=YR, aly=ey, gay=ey, dex=YR * PY,
            ez1=nxl + XR, hx1=cells, alx=(max(na, nb) + 1) * XR, gax=(max(na, nb) + 1) * XR, r=cells, rt=YR * PY,
        ),
        into=into,
        near=("go", "msgy2", "party2") + NEAR + tuple(k for k in argy if k not in pair),
        flush={0: [("p2", 0, cells + PY)] + [(k, 0, c) for k, c in zip(cy, size(nc, YR) + size(nz, YR))]},
        only=dict(f=[(EX * cells, cells), (EZ * cells, 3 * cells)]),
    )
    gotx = swap(two["msgx2"], along_x)
    pair, into = from_all(two["msgy2"], "gc", "gyi")
    group = call(
        "ends",
        [(k_join_ends, ("gyi",) + cyi[:4] + ("msg", "aly", "gay"))],
        dict(pair, **{k: two[k] for k in cyi[:4]}),
        dict(msg=2 * YR),
        dict(gyi=nc * 2 * YR, aly=ey, gay=ey),
        into=into,
        near=tuple(pair) + ("msg",),
    )
    argy, into_o = from_all(group["msg"], "gz", "gyo")
    argy.update(pair)
    into.update(into_o)
    order = cy + ("hby", "vny2", "vy2", "by", "hy", "ex2", "q2", "hy1") + cx + ("hbx", "vnx2", "vx2", "bx", "hx", "p2")
    need = {k: two.get(k, one.get(k)) for k in order}
    three = call(
        "three",
        [
            (
                k_y4,
                ("gyi", "gyo", "hy", "by", "vy2", "vny2", "hby") + cy + ("ex2", "hy1", "q2", "out")
                + ("aly", "gay", "w2", "dw"),
            ),
            (k_x4, ("gx", "hx", "bx", "vx2", "vnx2", "hbx") + cx + ("p2", "out", "alx", "gax")),
        ],
        dict(argy, gx=gotx, **need),
        dict(out=6 * cells),
        dict(
            gyi=nc * 2 * YR, gyo=nz * 2 * YR, aly=ey, gay=ey, w2=YR * PY, dw=YR * PY,
            alx=(max(na, nb) + 1) * PY, gax=(max(na, nb) + 1) * PY,
        ),
        into=into,
        near=("gx",) + tuple(argy),
        flush={
            0: [("out", EX * cells, cells), ("out", EZ * cells, 3 * cells)],
            1: [("out", EY * cells, cells), ("out", HZ * cells, cells)],
        },
    )
    return three["out"].reshape(6, PX, PY, PZ)


def solution(mesh):
    nx, ny = mesh.devices.shape
    nb = max(d for d in range(1, nx + 1) if nx % d == 0 and d * d <= nx)
    shape = (nx // nb, nb, ny // 2, 2)
    grid = Mesh(mesh.devices.reshape(shape), ("ga", "gb", "gz", "gc"))
    columns = P(("ga", "gb"), ("gz", "gc"), None)
    return jax.shard_map(
        local,
        mesh=grid,
        in_specs=(P(None, *columns), columns, P()),
        out_specs=P(None, *columns),
        check_vma=False,
    )
```

```python
import functools

import jax
import jax.numpy as jnp
from jax import lax
from jax.experimental import pallas as pl
from jax.experimental.pallas import tpu as pltpu
from jax.sharding import Mesh
from jax.sharding import PartitionSpec as P

PX, PY, PZ = 16, 32, 128
XL, YL = PY + 2, PX + 2
XR = 40
YR = 24
F32 = jnp.float32
LIMIT = 30
NEAR = ()
EX, EY, EZ, HX, HY, HZ = range(6)
XB, YB = 5 * XL + 6, 7 * YL + 2


def x_index():
    return lax.axis_index("ga") * lax.axis_size("gb") + lax.axis_index("gb")


def y_index():
    return lax.axis_index("gz") * lax.axis_size("gc") + lax.axis_index("gc")


def y_size():
    return lax.axis_size("gz") * lax.axis_size("gc")


def x_size():
    return lax.axis_size("ga") * lax.axis_size("gb")


def sub():
    return lax.broadcasted_iota(jnp.int32, (PY, PZ), 0)


def lanes_of(v):
    return lax.broadcasted_iota(jnp.int32, v.shape, 1)


def z_next(v):
    return jnp.where(lanes_of(v) == PZ - 1, 0.0, pltpu.roll(v, PZ - 1, 1))


def z_prev(v):
    return jnp.where(lanes_of(v) == 0, 0.0, pltpu.roll(v, 1, 1))


def fz(v):
    return z_next(v) - v


def bz(v):
    return v - z_prev(v)


def y_prev(v, row):
    return jnp.where(sub() == 0, row, pltpu.roll(v, 1, 0))


def y_next(v, row):
    return jnp.where(sub() == PY - 1, row, pltpu.roll(v, PY - 1, 0))


def plane(ref, k, size=PY):
    return ref[pl.ds(k * size, size), :]


def put(ref, k, v, size=PY):
    ref[pl.ds(k * size, size), :] = v


def fplane(ref, f, x):
    return plane(ref, f * PX + x)


def lookup(region, table):
    level = [table[i] for i in range(16)]
    for bit in range(4):
        on = (region & (1 << bit)) != 0
        level = [jnp.where(on, level[2 * i + 1], level[2 * i]) for i in range(len(level) // 2)]
    return level[0]


def packed(values, lines, more, rows):
    parts = [v[:lines] for v in values] + list(more)
    pad = rows - sum(v.shape[0] for v in parts)
    return (jnp.concatenate(parts + [jnp.zeros((pad, PZ), F32)], 0),)


def k_eps(reg, table, eps):
    tab = [table[i] for i in range(16)]
    for x in range(PX):
        put(eps, x, lookup(plane(reg, x), tab))


def k_edges(f, reg, table, xup, xdn, yup, ydn, tab, ends, low, high, rlow, rhigh, sems):
    up, down = (EX, EY, HY, HZ), (EY, EZ, HX, HZ)
    rows = (EX, HY, EZ, HX)
    top = pl.ds(PY - 8, 8)
    pairs = [(table, tab), (reg.at[PX - 1], ends.at[0]), (reg.at[0], ends.at[1])]
    pairs += [(reg.at[:, top, :], rhigh), (reg.at[:, pl.ds(0, 8), :], rlow)]
    for i in range(4):
        pairs += [
            (f.at[up[i], PX - 1], xup.at[pl.ds(i * PY, PY), :]),
            (f.at[down[i], 0], xdn.at[pl.ds(i * PY, PY), :]),
            (f.at[rows[i], :, top, :], high.at[i]),
            (f.at[rows[i], :, pl.ds(0, 8), :], low.at[i]),
        ]
    copies = [pltpu.make_async_copy(p, q, sems.at[i]) for i, (p, q) in enumerate(pairs)]
    for copy in copies:
        copy.start()
    for copy in copies:
        copy.wait()
    t = [tab[i] for i in range(16)]
    put(xup, 4, lookup(ends[0], t))
    put(xdn, 4, lookup(ends[1], t))
    for i in range(4):
        put(yup, i, high[i, :, 7, :], PX)
        put(ydn, i, low[i, :, 0, :], PX)
    put(yup, 4, high[3, :, 6, :], PX)
    put(yup, 5, lookup(rhigh[:, 7, :], t), PX)
    put(ydn, 4, lookup(rlow[:, 0, :], t), PX)


def edges(fields, region, eps_table):
    vmem, hbm = [pl.BlockSpec(memory_space=m) for m in (pltpu.VMEM, pltpu.HBM)]
    return pl.pallas_call(
        k_edges,
        out_shape=[pltpu.VMEM((c, PZ), F32) for c in (5 * PY, 5 * PY, 6 * PX, 6 * PX)],
        in_specs=[hbm] * 3,
        out_specs=[vmem] * 4,
        scratch_shapes=[
            pltpu.SMEM((16,), F32),
            pltpu.VMEM((2, PY, PZ), jnp.int32),
            pltpu.VMEM((4, PX, 8, PZ), F32),
            pltpu.VMEM((4, PX, 8, PZ), F32),
            pltpu.VMEM((PX, 8, PZ), jnp.int32),
            pltpu.VMEM((PX, 8, PZ), jnp.int32),
            pltpu.SemaphoreType.DMA((21,)),
        ],
        cost_estimate=pl.CostEstimate(flops=1000, bytes_accessed=1000, transcendentals=0),
        name="edges",
    )(*[pltpu.with_memory_space_constraint(v, pltpu.HBM) for v in (fields, region, eps_table)])


def factor(m_at, count, first, h, b, rows):
    hv = jnp.ones((rows, PZ), F32)
    hs = jnp.where(first, jnp.zeros_like(hv), jnp.ones_like(hv))
    bv = jnp.ones((rows, PZ), F32)
    bs = jnp.ones((rows, PZ), F32)
    for i in range(count):
        k = count - 1 - i
        put(h, i, hv, rows)
        put(b, k, bv, rows)
        hs = hs + m_at(i) * hv
        bs = bs + m_at(k) * bv
        hlast, blast = hv, bv
        hv = hv + hs
        bv = bv + bs
    hn = 1.0 / hv
    bn = 1.0 / bv
    return hn, bn, blast * bn, hn, hlast * hn


def sweep(m_at, r_at, count, v, rows):
    vv = jnp.zeros((rows, PZ), F32)
    vs = jnp.zeros((rows, PZ), F32)
    for i in range(count):
        put(v, i, vv, rows)
        vs = vs + m_at(i) * (vv - r_at(i))
        last = vv
        vv = vv + vs
    return last, vv


def ends(last, vn, hn, c):
    return -vn * hn, last - c * vn


def spread(msg, count, values):
    block = sum(v.shape[0] for v in values)
    for k in range(count):
        at = k * block
        for v in values:
            msg[pl.ds(at, v.shape[0]), :] = v
            at += v.shape[0]


def k_x1(f, eps, xl, xr, yl, yr, msg, q1, m, h, b, v, hb, r):
    gx = x_index()
    gy = y_index()
    xlo = gx > 0
    ylo = gy > 0
    yhi = gy < y_size() - 1
    yin = jnp.where(ylo, 1.0, 0.0)
    yon = jnp.where(yhi, 1.0, 0.0)
    q1lo = yin * (plane(yl, 1, PX) - 0.5 * fz(plane(yl, 0, PX)))
    q1hi = yon * (plane(yr, 1, PX) - 0.5 * fz(plane(yr, 0, PX)))
    hxlo = yin * plane(yl, 3, PX)
    epslo = plane(yl, 5, PX)
    epshi = plane(yr, 4, PX)
    hx31 = f[pl.ds(HX * PX * PY + PY - 1, PX, stride=PY), :]
    bxlo = jnp.concatenate([q1lo[:1], q1lo[1:] - q1lo[:-1]], 0)
    bxhi = jnp.concatenate([q1hi[:1], q1hi[1:] - q1hi[:-1]], 0)
    rlo = yin * plane(yl, 2, PX) + (32.0 / epslo) * (bxlo - (hxlo - yin * plane(yl, 4, PX)))
    rhi = yon * plane(yr, 2, PX) + (32.0 / epshi) * (bxhi - (yon * plane(yr, 3, PX) - hx31))
    pad = jnp.zeros((XR - PY - 2, PZ), F32)
    one = jnp.ones((XR - PY - 2, PZ), F32)
    before = jnp.where(xlo, plane(xl, 2) - 0.5 * fz(plane(xl, 0)), 0.0)
    for x in range(PX):
        q = fplane(f, HY, x) - 0.5 * fz(fplane(f, EX, x))
        put(q1, x, q)
        e = plane(eps, x)
        hx = fplane(f, HX, x)
        ce = 32.0 / e
        rr = fplane(f, EZ, x) + ce * ((q - before) - (hx - y_prev(hx, hxlo[x : x + 1])))
        before = q
        r[pl.ds(x * XR, PY), :] = rr
        r[pl.ds(x * XR + PY, 8), :] = jnp.concatenate([rlo[x : x + 1], rhi[x : x + 1], pad], 0)
        m[pl.ds(x * XR, PY), :] = e * (1.0 / 1024.0)
        m[pl.ds(x * XR + PY, 8), :] = (
            jnp.concatenate([epslo[x : x + 1], epshi[x : x + 1], one], 0) * (1.0 / 1024.0)
        )
    m_at = lambda i: plane(m, i, XR)
    hn, bn, a, bb, c = factor(m_at, PX, gx == 0, h, b, XR)
    last, vn = sweep(m_at, lambda i: plane(r, i, XR), PX, v, XR)
    pf, plast = ends(last, vn, hn, c)
    put(hb, 0, hn, XR)
    put(hb, 1, bn, XR)
    put(hb, 2, c, XR)
    put(hb, 3, vn, XR)
    qq = jnp.concatenate([q1lo[PX - 1 :], q1hi[PX - 1 :]], 0) * (-1.0 / 32.0)
    spread(msg, lax.axis_size("gb"), packed((pf, plast, a, bb, c), XL, (qq,), XB))


def k_y1(f, eps, xl, xr, msg, p1, ey1, m, h, b, v, hb, r, ep):
    gx = x_index()
    gy = y_index()
    n = y_size()
    xlo = gx > 0
    xin = jnp.where(xlo, 1.0, 0.0)
    xon = jnp.where(gx < x_size() - 1, 1.0, 0.0)
    zero = jnp.zeros((1, PZ), F32)
    zeros = jnp.zeros((PY, PZ), F32)
    exl, eyl, hyl, hzl = [xin * plane(xl, i) for i in range(4)]
    eyr, ezr, hxr, hzr = [xon * plane(xr, i) for i in range(4)]
    for x in range(PX):
        put(ep, x, plane(eps, x))
    put(ep, PX, plane(xl, 4))
    put(ep, PX + 1, plane(xr, 4))
    for x in range(PX + 2, YR):
        put(ep, x, zeros + 1.0)
        put(r, x, zeros)
    put(r, PX + 1, zeros)

    def rex(ex, hy, pp, e):
        ie = 1.0 / e
        return ex + (32.0 * ie) * (pp - y_prev(pp, zero)) - (0.5 * ie) * bz(hy)

    p = hzl - 32.0 * (fplane(f, EY, 0) - eyl)
    p = jnp.where(xlo, p, 0.0)
    put(p1, PX, p)
    put(r, PX, rex(exl, hyl, p, plane(ep, PX)))
    for x in range(PX):
        ey = fplane(f, EY, x)
        nxt = fplane(f, EY, x + 1) if x < PX - 1 else eyr
        hz = fplane(f, HZ, x)
        hzp = fplane(f, HZ, x - 1) if x > 0 else hzl
        e = plane(ep, x)
        p = hz - 32.0 * (nxt - ey)
        put(p1, x, p)
        put(r, x, rex(fplane(f, EX, x), fplane(f, HY, x), p, e))
        ie = 1.0 / e
        put(ey1, x, ey + (0.5 * ie) * bz(fplane(f, HX, x)) - (32.0 * ie) * (hz - hzp))
    ie = 1.0 / plane(ep, PX + 1)
    put(ey1, PX, eyr + (0.5 * ie) * bz(hxr) - (32.0 * ie) * (hzr - fplane(f, HZ, PX - 1)))

    def rows(ref, j):
        return ref[pl.ds(j, YR, stride=PY), :]

    for j in range(PY):
        put(m, j, rows(ep, j) * (1.0 / 1024.0), YR)
    m_at = lambda j: plane(m, j, YR)
    hn, bn, a, bb, c = factor(m_at, PY, gy == 0, h, b, YR)
    last, vn = sweep(m_at, lambda j: rows(r, j), PY, v, YR)
    pf, plast = ends(last, vn, hn, c)
    put(hb, 0, hn, YR)
    put(hb, 1, bn, YR)
    put(hb, 2, c, YR)
    put(hb, 3, vn, YR)
    lastrow = lambda ref, at, k: ref[pl.ds(at * PY + PY - 1, k, stride=PY), :]
    tail = jnp.zeros((7, PZ), F32)
    qq = jnp.concatenate([lastrow(p1, 0, PX), lastrow(p1, PX, 1), tail], 0) * (-1.0 / 32.0)
    tail = jnp.zeros((6, PZ), F32)
    ee = fz(jnp.concatenate([lastrow(ey1, 0, PX), zero, lastrow(ey1, PX, 1), tail], 0))
    spread(msg, 1, packed((pf, plast, a, bb, c, qq, ee), YL, (), YB))


def coefficients(part, n, rows, tp, bp, ts, bs, bet, dele):
    zero = jnp.zeros((rows, PZ), F32)
    beta = zero
    put(bet, 0, zero, rows)
    for j in range(n):
        a, b, c = part(j, 2), part(j, 3), part(j, 4)
        bd = b / (1.0 - a * beta)
        t = bd * beta
        put(tp, j, t, rows)
        put(bp, j, bd, rows)
        beta = c + t * b
        put(bet, j + 1, beta, rows)
    delta = zero
    put(dele, n, zero, rows)
    for j in range(n - 1, -1, -1):
        a, b, c = part(j, 2), part(j, 3), part(j, 4)
        bd = b / (1.0 - c * delta)
        t = bd * delta
        put(ts, j, t, rows)
        put(bs, j, bd, rows)
        delta = a + t * b
        put(dele, j, delta, rows)


def chain(part, n, rows, crows, tp, bp, ts, bs, al, ga, start, stop):
    take = lambda ref, j: ref[pl.ds(j * crows, rows), :]
    alpha, gamma = start, stop
    put(al, 0, alpha, rows)
    put(ga, n, gamma, rows)
    for j in range(n):
        k = n - 1 - j
        alpha = part(j, 1) + take(tp, j) * part(j, 0) + take(bp, j) * alpha
        gamma = part(k, 0) + take(ts, k) * part(k, 1) + take(bs, k) * gamma
        put(al, j + 1, alpha, rows)
        put(ga, k, gamma, rows)
    return gamma, alpha


def interface(part, n, me, rows, coefs, al, ga, start=None, stop=None, crows=None):
    crows = crows or rows
    tp, bp, ts, bs, bet, dele = coefs
    zero = jnp.zeros((rows, PZ), F32)
    start = zero if start is None else start
    stop = zero if stop is None else stop
    chain(part, n, rows, crows, tp, bp, ts, bs, al, ga, start, stop)
    at = lambda ref, d, size: ref[pl.ds(pl.multiple_of(d * size, 8), rows), :]
    a0, a1 = at(al, me, rows), at(al, me + 1, rows)
    g0, g1 = at(ga, me, rows), at(ga, me + 1, rows)
    b0, b1 = at(bet, me, crows), at(bet, me + 1, crows)
    d0, d1 = at(dele, me, crows), at(dele, me + 1, crows)
    left = a0 + b0 * ((g0 + d0 * a0) / (1.0 - d0 * b0))
    right = g1 + d1 * ((a1 + b1 * g1) / (1.0 - b1 * d1))
    return left, right


def x_raw(msg):
    return lambda j, k: msg[pl.ds(j * XB + k * XL, XR), :]


def x_late(msg, at):
    return pltpu.roll(msg[pl.ds(at + XB - 8, 8), :], 6, 0)


def x_part(msg):
    def part(j, k):
        if j == 0:
            return x_raw(msg)(j, k)
        own = msg[pl.ds(j * XB + k * XL, PY), :]
        more = (
            msg[pl.ds(j * XB + k * XL + PY, 8), :]
            + msg[pl.ds(j * XB + (2 + k) * XL + PY, 8), :] * x_late(msg, (j - 1) * XB)
        )
        return jnp.concatenate([own, more], 0)

    return part


def x_passed(msg, me):
    prev = pl.multiple_of(jnp.maximum(me - 1, 0) * XB, 8)
    return jnp.where(me > 0, x_late(msg, prev), 0.0)


def y_raw(msg):
    return lambda j, k: msg[pl.ds(j * YB + k * YL, YR), :]


def y_part(msg):
    raw = y_raw(msg)
    return lambda j, k: raw(j, k) + raw(j, 2 + k) * raw(j - 1, 5) if j else raw(j, k)


def y_passed(msg, me, k):
    skip = k * YL % 8
    prev = pl.multiple_of(jnp.maximum(me - 1, 0) * YB + k * YL - skip, 8)
    return jnp.where(me > 0, pltpu.roll(msg[pl.ds(prev, YR), :], YR - skip, 0), 0.0)


def k_y2(gi, go, p1, h, b, v, hb, ex1, p2, elo, *more):
    coi, coo, (al, ga, dex) = more[:6], more[6:12], more[12:]
    nz, nc = lax.axis_size("gz"), lax.axis_size("gc")
    iz, ic = lax.axis_index("gz"), lax.axis_index("gc")
    coefficients(y_raw(go), nz, YR, *coo)
    coefficients(y_raw(gi), nc, YR, *coi)
    left, right = interface(y_part(go), nz, iz, YR, coo, al, ga)
    left = left + y_passed(go, iz, 5)
    left, right = interface(y_part(gi), nc, ic, YR, coi, al, ga, left, right)
    left = left + y_passed(gi, ic, 5)
    elo[...] = jnp.where(ic > 0, y_passed(gi, ic, 6), y_passed(go, iz, 6))
    lw = left * plane(hb, 1, YR)
    rw = (right - plane(hb, 3, YR)) * plane(hb, 0, YR)
    later = right
    for j in range(PY - 1, -1, -1):
        w = plane(v, j, YR) + plane(b, j, YR) * lw + plane(h, j, YR) * rw
        ex1[pl.ds(j, YR, stride=PY), :] = w
        dex[pl.ds(j, YR, stride=PY), :] = later - w
        later = w
    live = jnp.where(x_index() > 0, 1.0, 0.0)
    for x in range(PX):
        put(p2, x, plane(p1, x) + 64.0 * plane(dex, x))
    put(p2, PX, live * (plane(p1, PX) + 64.0 * plane(dex, PX)))


def join(part, raw, count):
    pf, ph, a, b, c = part(0, 0), part(0, 1), raw(0, 2), raw(0, 3), raw(0, 4)
    for j in range(1, count):
        qf, qh, a2, b2, c2 = part(j, 0), part(j, 1), raw(j, 2), raw(j, 3), raw(j, 4)
        den = 1.0 / (1.0 - c * a2)
        low, high = b * den, b2 * den
        pf, ph = pf + low * (qf + a2 * ph), qh + high * (ph + c * qf)
        a, b, c = a + low * b * a2, low * b2, c2 + high * b2 * c
    return pf, ph, a, b, c


def k_join_y(gi, msg):
    nc = lax.axis_size("gc")
    raw = y_raw(gi)
    values = join(y_part(gi), raw, nc)
    more = gi[pl.ds((nc - 1) * YB + 5 * YL, 2 * YL), :]
    spread(msg, 1, packed(values, YL, (more,), YB))


def k_join_x(gi, msg, inner):
    inner[...] = gi[...]
    nb = lax.axis_size("gb")
    last = x_late(gi, (nb - 1) * XB)[:2]
    spread(msg, lax.axis_size("ga"), packed(join(x_part(gi), x_raw(gi), nb), XL, (last,), XB))


def shares(pf, ph, coefs, count, me, rows, crows):
    tp, bp, ts, bs = coefs[:4]
    low = high = jnp.ones((rows, PZ), F32)
    for k in range(count):
        low = jnp.where(k < me, low * bs[pl.ds(k * crows, rows), :], low)
        high = jnp.where(k > me, high * bp[pl.ds(k * crows, rows), :], high)
    mine = pl.ds(pl.multiple_of(me * crows, 8), rows)
    return low * (pf + ts[mine, :] * ph), high * (ph + tp[mine, :] * pf)


def gathered(msg, n, m, ia, ib, rows, crows, coi, coo, al, ga):
    zero = jnp.zeros((rows, PZ), F32)

    def inside(j, k):
        at = pl.multiple_of(((ia * m + j) * 2 + k) * rows, 8)
        return msg[pl.ds(at, rows), :]

    whole = chain(inside, m, rows, crows, *coi[:4], al, ga, zero, zero)

    def group(j, k):
        total = sum(msg[pl.ds(((j * m + i) * 2 + k) * rows, rows), :] for i in range(m))
        return jnp.where(ia == j, whole[k], total)

    left, right = interface(group, n, ia, rows, coo, al, ga, crows=crows)
    return interface(inside, m, ib, rows, coi, al, ga, left, right, crows)


def k_x2(gi, go, f, q1, ey1, p2, h, b, v, m, hb, ez1, hx1, msg2, v2, vn2, *more):
    coi, coo, (al, ga, r) = more[:6], more[6:12], more[12:]
    na, nb = lax.axis_size("ga"), lax.axis_size("gb")
    ia, ib = lax.axis_index("ga"), lax.axis_index("gb")
    gy = y_index()
    yon = jnp.where(gy < y_size() - 1, 1.0, 0.0)
    coefficients(x_raw(go), na, XR, *coo)
    coefficients(x_raw(gi), nb, XR, *coi)
    left, right = interface(x_part(go), na, ia, XR, coo, al, ga)
    left = jnp.concatenate([left[:PY], left[PY:] + x_passed(go, ia)], 0)
    left, right = interface(x_part(gi), nb, ib, XR, coi, al, ga, left, right)
    left = jnp.concatenate([left[:PY], left[PY:] + x_passed(gi, ib)], 0)
    lw = left * plane(hb, 1, XR)
    rw = (right - plane(hb, 3, XR)) * plane(hb, 0, XR)
    for x in range(PX):
        put(ez1, x, plane(v, x, XR) + plane(b, x, XR) * lw + plane(h, x, XR) * rw, XR)
    put(ez1, PX, right, XR)
    before = plane(p2, PX)
    for x in range(PX):
        z = ez1[pl.ds(x * XR, PY), :]
        z32 = yon * ez1[pl.ds(x * XR + PY + 1, 1), :]
        ey = plane(ey1, x)
        t = fplane(f, HX, x) - 32.0 * (y_next(z, z32) - z) + 0.5 * fz(ey)
        put(hx1, x, t)
        p = plane(p2, x)
        ie = 1.0 / (m[pl.ds(x * XR, PY), :] * 1024.0)
        put(r, x, ey + (0.5 * ie) * bz(t) - (32.0 * ie) * (p - before))
        before = p
    last, vn = sweep(lambda i: m[pl.ds(i * XR, PY), :], lambda i: plane(r, i), PX, v2, PY)
    vn2[...] = vn
    pf, plast = ends(last, vn, hb[pl.ds(0, PY), :], hb[pl.ds(2 * XR, PY), :])
    share = shares(pf, plast, coi, nb, ib, PY, XR)
    for k in range(na * nb):
        for i, (own, joined) in enumerate(zip((pf, plast), share)):
            put(msg2, 2 * k + i, jnp.where(ia == k // nb, own, joined))


def k_y3(f, xr, q1, mx, ey1, ez1, hx1, ex1, elo, ex2, hy1, q2, r):
    n = y_size()
    gy = y_index()
    yon = jnp.where(gy < n - 1, 1.0, 0.0)
    yin = jnp.where(gy > 0, 1.0, 0.0)
    zeros = jnp.zeros((PY, PZ), F32)
    for x in range(PX + 2, YR):
        put(r, x, zeros)
    put(r, PX, zeros)
    for x in range(PX + 1):
        at = x * XR
        z = ez1[pl.ds(at, PY), :]
        zlo = ez1[pl.ds(at + PY, 1), :]
        zhi = yon * ez1[pl.ds(at + PY + 1, 1), :]
        fe = fz(plane(ey1, x))
        d = 32.0 * (y_next(z, zhi) - z) - fe
        k = x if x < PX else PX + 1
        dlo = yin * (32.0 * (z[:1] - zlo) - elo[pl.ds(k, 1), :])
        ez = fplane(f, EZ, x) if x < PX else plane(xr, 1)
        e = mx[pl.ds(at, PY), :] * 1024.0 if x < PX else plane(xr, 4)
        ie = 1.0 / e
        put(r, k, 2.0 * z - ez + (32.0 * ie) * (d - y_prev(d, dlo)))
        if x < PX:
            t = plane(q1, x) + 32.0 * (ez1[pl.ds(at + XR, PY), :] - z)
            put(hy1, x, t)
            put(ex2, x, 2.0 * plane(ex1, x) - fplane(f, EX, x) + (0.5 * ie) * bz(fplane(f, HY, x) - t))
            put(q2, x, plane(hx1, x) + 0.5 * fe)


def k_y3_sweep(r, m, hb, msg2, v2, vn2):
    m_at = lambda j: plane(m, j, YR)
    last, vn = sweep(m_at, lambda j: r[pl.ds(j, YR, stride=PY), :], PY, v2, YR)
    vn2[...] = vn
    pf, plast = ends(last, vn, plane(hb, 0, YR), plane(hb, 2, YR))
    spread(msg2, 1, (pf, plast))


def y_ends(msg):
    return lambda j, k: msg[pl.ds((2 * j + k) * YR, YR), :]


def k_join_ends(gi, tp, bp, ts, bs, msg, al, ga):
    nc = lax.axis_size("gc")
    zero = jnp.zeros((YR, PZ), F32)
    spread(msg, 1, chain(y_ends(gi), nc, YR, YR, tp, bp, ts, bs, al, ga, zero, zero))


def k_y4(gi, go, h, b, v2, vn2, hb, *more):
    coi, coo, (ex2, hy1, q2, out, al, ga, w2, dw) = more[:6], more[6:12], more[12:]
    nz, nc = lax.axis_size("gz"), lax.axis_size("gc")
    iz, ic = lax.axis_index("gz"), lax.axis_index("gc")
    left, right = interface(y_ends(go), nz, iz, YR, coo, al, ga)
    left, right = interface(y_ends(gi), nc, ic, YR, coi, al, ga, left, right)
    lw = left * plane(hb, 1, YR)
    rw = (right - vn2[...]) * plane(hb, 0, YR)
    later = right
    for j in range(PY - 1, -1, -1):
        w = plane(v2, j, YR) + plane(b, j, YR) * lw + plane(h, j, YR) * rw
        w2[pl.ds(j, YR, stride=PY), :] = w
        dw[pl.ds(j, YR, stride=PY), :] = later - w
        later = w
    xon = jnp.where(x_index() < x_size() - 1, 1.0, 0.0)
    for x in range(PX):
        w = plane(w2, x)
        nxt = plane(w2, x + 1) if x < PX - 1 else xon * plane(w2, PX + 1)
        e2 = plane(ex2, x)
        put(out, EX * PX + x, e2)
        put(out, EZ * PX + x, w)
        put(out, HX * PX + x, plane(q2, x) - 32.0 * plane(dw, x))
        put(out, HY * PX + x, plane(hy1, x) - 0.5 * fz(e2) + 32.0 * (nxt - w))


def k_x4(msg, h, b, v2, vn2, hb, *more):
    coi, coo, (p2, out, al, ga) = more[:6], more[6:12], more[12:]
    na, nb = lax.axis_size("ga"), lax.axis_size("gb")
    ia, ib = lax.axis_index("ga"), lax.axis_index("gb")
    left, right = gathered(msg, na, nb, ia, ib, PY, XR, coi, coo, al, ga)
    lw = left * hb[pl.ds(XR, PY), :]
    rw = (right - vn2[...]) * hb[pl.ds(0, PY), :]
    later = right
    for x in range(PX - 1, -1, -1):
        w = plane(v2, x) + b[pl.ds(x * XR, PY), :] * lw + h[pl.ds(x * XR, PY), :] * rw
        put(out, EY * PX + x, w)
        put(out, HZ * PX + x, plane(p2, x) - 32.0 * (later - w))
        later = w


def call(name, parts, args, outs, scratch=(), smem=(), into=(), flush=(), near=(), only=()):
    into, flush, scratch, only = dict(into), dict(flush), dict(scratch), dict(only)
    moved = [k for k in args if k not in smem and (k not in near or k in into)]
    pieces = {k for group in flush.values() for k, _, _ in group}
    last = {k: max(i for i, (_, used) in enumerate(parts) if k in used) for k in outs}
    leave = [
        [(k, 0, outs[k]) for k in outs if last[k] == i and k not in pieces and k not in near]
        + list(flush.get(i, ()))
        for i in range(len(parts))
    ]
    own = [k for k in moved if k not in into]

    def body(*refs):
        take = iter(refs)
        hbm = {k: next(take) for k in args}
        results = {k: next(take) for k in outs}
        env = {k: next(take) for k in own}
        env.update({k: results[k] if k in near else next(take) for k in outs})
        env.update({k: next(take) for k in scratch})
        env.update({k: hbm[k] for k in args if k not in moved})
        sem_in, sem_out = next(take), next(take)
        pending = {}
        count = 0
        for k in moved:
            pairs = [(hbm[k], env.get(k))]
            if k in into:
                buffer, row = into[k]
                pairs = [(hbm[k], env[buffer].at[pl.ds(row(), args[k].shape[0]), :])]
            elif k in only:
                windows = [pl.ds(at, rows) for at, rows in only[k]]
                pairs = [(hbm[k].at[w, :], env[k].at[w, :]) for w in windows]
            for source, where in pairs:
                copy = pltpu.make_async_copy(source, where, sem_in.at[count])
                copy.start()
                count += 1
                pending.setdefault(into[k][0] if k in into else k, []).append(copy)
        sent = []
        for i, (function, used) in enumerate(parts):
            for k in used:
                for copy in pending.pop(k, ()):
                    copy.wait()
            function(*[env[k] for k in used])
            for k, row, rows in leave[i]:
                window = pl.ds(row, rows)
                copy = pltpu.make_async_copy(
                    env[k].at[window, :], results[k].at[window, :], sem_out.at[len(sent)]
                )
                copy.start()
                sent.append(copy)
        for copy in sent:
            copy.wait()

    far, close, scalars = [
        pl.BlockSpec(memory_space=m) for m in (pltpu.HBM, pltpu.VMEM, pltpu.SMEM)
    ]
    got = pl.pallas_call(
        body,
        out_shape=[(pltpu.VMEM if k in near else pltpu.HBM)((c, PZ), F32) for k, c in outs.items()],
        in_specs=[scalars if k in smem else close if k in near else far for k in args],
        out_specs=[close if k in near else far for k in outs],
        scratch_shapes=[pltpu.VMEM(args[k].shape, args[k].dtype) for k in own]
        + [pltpu.VMEM((c, PZ), F32) for k, c in outs.items() if k not in near]
        + [pltpu.VMEM((c, PZ), F32) for c in scratch.values()]
        + [
            pltpu.SemaphoreType.DMA((sum(len(only.get(k, (0,))) for k in moved),)),
            pltpu.SemaphoreType.DMA((max(1, sum(len(group) for group in leave)),)),
        ],
        compiler_params=pltpu.CompilerParams(vmem_limit_bytes=LIMIT * 1024 * 1024),
        cost_estimate=pl.CostEstimate(flops=1000, bytes_accessed=1000, transcendentals=0),
        name=name,
    )(*[a if k in smem else pltpu.with_memory_space_constraint(a, pltpu.VMEM if k in near else pltpu.HBM) for k, a in args.items()])
    return dict(zip(outs, got))


def ring(block, axis, step):
    n = lax.axis_size(axis)
    return lax.ppermute(block, axis, [(i, (i + step) % n) for i in range(n)])


def swap(msg, axis):
    n = lax.axis_size(axis)
    got = lax.all_to_all(msg.reshape(n, -1, PZ), axis, 0, 0, tiled=True)
    return got.reshape(-1, PZ)


def from_all(msg, axis, buffer):
    n = lax.axis_size(axis)
    rows = msg.shape[0]
    args, into = {}, {}
    for step in range(n):
        k = buffer + str(step)
        args[k] = ring(msg, axis, step) if step else msg

        def row(step=step):
            return pl.multiple_of(lax.rem(lax.axis_index(axis) - step + n, n) * rows, 8)

        into[k] = (buffer, row)
    return args, into


def local(fields, region, eps_table):
    na, nb = lax.axis_size("ga"), lax.axis_size("gb")
    along_x, along_y = ("ga", "gb"), ("gz", "gc")
    nz, nc = lax.axis_size("gz"), lax.axis_size("gc")
    ny = nz * nc
    ey = (max(nz, nc) + 1) * YR
    cells = PX * PY
    nxl, nyl = PX * XR, PY * YR
    f = fields.reshape(6 * cells, PZ)
    reg = region.reshape(cells, PZ)
    xup, xdn, yup, ydn = edges(fields, region, eps_table)
    xl = ring(xup, along_x, 1)
    xr = ring(xdn, along_x, -1)
    yl = ring(yup, along_y, 1)
    yr = ring(ydn, along_y, -1)
    linex = ("mx", "hx", "bx", "vx", "hbx")
    liney = ("my", "hy", "by", "vy", "hby")
    one = call(
        "onex",
        [
            (k_eps, ("reg", "table", "eps")),
            (k_x1, ("f", "eps", "xl", "xr", "yl", "yr", "msgx", "q1") + linex + ("r",)),
        ],
        dict(xl=xl, xr=xr, yl=yl, yr=yr, reg=reg, f=f, table=eps_table),
        dict(zip(("eps", "q1") + linex + ("msgx",), (cells, cells, nxl, nxl, nxl, nxl, 4 * XR, nb * XB))),
        dict(r=nxl),
        smem=("table",),
        near=("xl", "xr", "yl", "yr") + NEAR,
        flush={0: [("eps", 0, cells)]},
        only=dict(f=[(EX * cells, cells), (EZ * cells, 3 * cells)]),
    )
    oney = call(
        "oney",
        [(k_y1, ("f", "eps", "xl", "xr", "msgy", "p1", "ey1") + liney + ("rt", "ep"))],
        dict(f=f, eps=one["eps"], xl=xl, xr=xr),
        dict(
            zip(
                ("msgy", "p1", "ey1") + liney,
                (YB, cells + PY, cells + PY, nyl, nyl, nyl, nyl, 4 * YR),
            )
        ),
        dict(rt=YR * PY, ep=YR * PY),
        near=("msgy",),
        only=dict(f=[(EX * cells, 2 * cells), (HX * cells, 3 * cells)]),
    )
    one.update(oney)
    pair, into = from_all(one["msgy"], "gc", "gyi")
    group = call(
        "group",
        [
            (k_join_y, ("gyi", "msgyo")),
            (k_join_x, ("gi", "msgo", "inner")),
        ],
        dict(pair, gi=swap(one["msgx"], "gb")),
        dict(msgyo=YB, msgo=na * XB, inner=nb * XB),
        dict(gyi=nc * YB),
        into=into,
        near=("gi", "msgyo") + NEAR + tuple(pair),
    )
    goto = swap(group["msgo"], "ga")
    argy, into_o = from_all(group["msgyo"], "gz", "gyo")
    argy.update(pair)
    into.update(into_o)
    chains = ("tp", "bp", "ts", "bs", "bet", "del")
    ci, co, cyi, cyo = [tuple(k + a for k in chains) for a in ("i", "o", "yi", "yo")]
    cx, cy = ci + co, cyi + cyo
    size = lambda n, rows: (n * rows,) * 4 + ((n + 1) * rows,) * 2
    keep = {k: one[k] for k in ("q1", "p1", "ey1") + linex + liney}
    two = call(
        "two",
        [
            (k_y2, ("gyi", "gyo", "p1", "hy", "by", "vy", "hby", "ex1", "p2", "elo") + cy + ("aly", "gay", "dex")),
            (
                k_x2,
                ("gi", "go", "f", "q1", "ey1", "p2", "hx", "bx", "vx", "mx", "hbx")
                + ("ez1", "hx1", "msgx2", "vx2", "vnx2")
                + cx
                + ("alx", "gax", "r"),
            ),
            (
                k_y3,
                ("f", "xr", "q1", "mx", "ey1", "ez1", "hx1", "ex1", "elo", "ex2", "hy1", "q2", "rt"),
            ),
            (k_y3_sweep, ("rt", "my", "hby", "msgy2", "vy2", "vny2")),
        ],
        dict(argy, **{k: keep[k] for k in ("hby", "vy", "by", "hy", "p1")}, gi=group["inner"], go=goto, f=f, xr=xr, **{k: keep[k] for k in linex + ("ey1", "q1", "my")}),
        dict(
            zip(
                ("p2",) + cy + ("msgx2", "vx2", "vnx2") + cx + ("msgy2", "vy2", "vny2", "ex2", "hy1", "q2"),
                (cells + PY,)
                + size(nc, YR)
                + size(nz, YR)
                + (na * nb * 2 * PY, cells, PY)
                + size(nb, XR)
                + size(na, XR)
                + (2 * YR, nyl, YR, cells, cells, cells),
            )
        ),
        dict(
            gyi=nc * YB, gyo=nz * YB, ex1=YR * PY, elo=YR, aly=ey, gay=ey, dex=YR * PY,
            ez1=nxl + XR, hx1=cells, alx=(max(na, nb) + 1) * XR, gax=(max(na, nb) + 1) * XR, r=cells, rt=YR * PY,
        ),
        into=into,
        near=("go", "msgy2", "party2") + NEAR + tuple(k for k in argy if k not in pair),
        flush={0: [("p2", 0, cells + PY)] + [(k, 0, c) for k, c in zip(cy, size(nc, YR) + size(nz, YR))]},
        only=dict(f=[(EX * cells, cells), (EZ * cells, 3 * cells)]),
    )
    gotx = swap(two["msgx2"], along_x)
    pair, into = from_all(two["msgy2"], "gc", "gyi")
    group = call(
        "ends",
        [(k_join_ends, ("gyi",) + cyi[:4] + ("msg", "aly", "gay"))],
        dict(pair, **{k: two[k] for k in cyi[:4]}),
        dict(msg=2 * YR),
        dict(gyi=nc * 2 * YR, aly=ey, gay=ey),
        into=into,
        near=tuple(pair) + ("msg",),
    )
    argy, into_o = from_all(group["msg"], "gz", "gyo")
    argy.update(pair)
    into.update(into_o)
    order = cy + ("hby", "vny2", "vy2", "by", "hy", "ex2", "q2", "hy1") + cx + ("hbx", "vnx2", "vx2", "bx", "hx", "p2")
    need = {k: two.get(k, one.get(k)) for k in order}
    three = call(
        "three",
        [
            (
                k_y4,
                ("gyi", "gyo", "hy", "by", "vy2", "vny2", "hby") + cy + ("ex2", "hy1", "q2", "out")
                + ("aly", "gay", "w2", "dw"),
            ),
            (k_x4, ("gx", "hx", "bx", "vx2", "vnx2", "hbx") + cx + ("p2", "out", "alx", "gax")),
        ],
        dict(argy, gx=gotx, **need),
        dict(out=6 * cells),
        dict(
            gyi=nc * 2 * YR, gyo=nz * 2 * YR, aly=ey, gay=ey, w2=YR * PY, dw=YR * PY,
            alx=(max(na, nb) + 1) * PY, gax=(max(na, nb) + 1) * PY,
        ),
        into=into,
        near=("gx",) + tuple(argy),
        flush={
            0: [("out", EX * cells, cells), ("out", EZ * cells, 3 * cells)],
            1: [("out", EY * cells, cells), ("out", HZ * cells, cells)],
        },
    )
    return three["out"].reshape(6, PX, PY, PZ)


def solution(mesh):
    nx, ny = mesh.devices.shape
    nb = max(d for d in range(1, nx + 1) if nx % d == 0 and d * d <= nx)
    shape = (nx // nb, nb, ny // 2, 2)
    grid = Mesh(mesh.devices.reshape(shape), ("ga", "gb", "gz", "gc"))
    columns = P(("ga", "gb"), ("gz", "gc"), None)
    return jax.shard_map(
        local,
        mesh=grid,
        in_specs=(P(None, *columns), columns, P()),
        out_specs=P(None, *columns),
        check_vma=False,
    )
```

```python
import functools

import jax
import jax.numpy as jnp
from jax import lax
from jax.experimental import pallas as pl
from jax.experimental.pallas import tpu as pltpu
from jax.sharding import Mesh
from jax.sharding import PartitionSpec as P

PX, PY, PZ = 16, 32, 128
XL, YL = PY + 2, PX + 2
XR = 40
YR = 24
F32 = jnp.float32
LIMIT = 30
NEAR = ()
EX, EY, EZ, HX, HY, HZ = range(6)
XB, YB = 5 * XL + 6, 7 * YL + 2


def x_index():
    return lax.axis_index("ga") * lax.axis_size("gb") + lax.axis_index("gb")


def y_index():
    return lax.axis_index("gz") * lax.axis_size("gc") + lax.axis_index("gc")


def y_size():
    return lax.axis_size("gz") * lax.axis_size("gc")


def x_size():
    return lax.axis_size("ga") * lax.axis_size("gb")


def sub():
    return lax.broadcasted_iota(jnp.int32, (PY, PZ), 0)


def lanes_of(v):
    return lax.broadcasted_iota(jnp.int32, v.shape, 1)


def z_next(v):
    return jnp.where(lanes_of(v) == PZ - 1, 0.0, pltpu.roll(v, PZ - 1, 1))


def z_prev(v):
    return jnp.where(lanes_of(v) == 0, 0.0, pltpu.roll(v, 1, 1))


def fz(v):
    return z_next(v) - v


def bz(v):
    return v - z_prev(v)


def y_prev(v, row):
    return jnp.where(sub() == 0, row, pltpu.roll(v, 1, 0))


def y_next(v, row):
    return jnp.where(sub() == PY - 1, row, pltpu.roll(v, PY - 1, 0))


def plane(ref, k, size=PY):
    return ref[pl.ds(k * size, size), :]


def put(ref, k, v, size=PY):
    ref[pl.ds(k * size, size), :] = v


def fplane(ref, f, x):
    return plane(ref, f * PX + x)


def lookup(region, table):
    level = [table[i] for i in range(16)]
    for bit in range(4):
        on = (region & (1 << bit)) != 0
        level = [jnp.where(on, level[2 * i + 1], level[2 * i]) for i in range(len(level) // 2)]
    return level[0]


def packed(values, lines, more, rows):
    parts = [v[:lines] for v in values] + list(more)
    pad = rows - sum(v.shape[0] for v in parts)
    return (jnp.concatenate(parts + [jnp.zeros((pad, PZ), F32)], 0),)


def k_eps(reg, table, eps):
    tab = [table[i] for i in range(16)]
    for x in range(PX):
        put(eps, x, lookup(plane(reg, x), tab))


def k_edges(f, reg, table, xup, xdn, yup, ydn, tab, ends, low, high, rlow, rhigh, sems):
    up, down = (EX, EY, HY, HZ), (EY, EZ, HX, HZ)
    rows = (EX, HY, EZ, HX)
    top = pl.ds(PY - 8, 8)
    pairs = [(table, tab), (reg.at[PX - 1], ends.at[0]), (reg.at[0], ends.at[1])]
    pairs += [(reg.at[:, top, :], rhigh), (reg.at[:, pl.ds(0, 8), :], rlow)]
    for i in range(4):
        pairs += [
            (f.at[up[i], PX - 1], xup.at[pl.ds(i * PY, PY), :]),
            (f.at[down[i], 0], xdn.at[pl.ds(i * PY, PY), :]),
            (f.at[rows[i], :, top, :], high.at[i]),
            (f.at[rows[i], :, pl.ds(0, 8), :], low.at[i]),
        ]
    copies = [pltpu.make_async_copy(p, q, sems.at[i]) for i, (p, q) in enumerate(pairs)]
    for copy in copies:
        copy.start()
    for copy in copies:
        copy.wait()
    t = [tab[i] for i in range(16)]
    put(xup, 4, lookup(ends[0], t))
    put(xdn, 4, lookup(ends[1], t))
    for i in range(4):
        put(yup, i, high[i, :, 7, :], PX)
        put(ydn, i, low[i, :, 0, :], PX)
    put(yup, 4, high[3, :, 6, :], PX)
    put(yup, 5, lookup(rhigh[:, 7, :], t), PX)
    put(ydn, 4, lookup(rlow[:, 0, :], t), PX)


def edges(fields, region, eps_table):
    vmem, hbm = [pl.BlockSpec(memory_space=m) for m in (pltpu.VMEM, pltpu.HBM)]
    return pl.pallas_call(
        k_edges,
        out_shape=[pltpu.VMEM((c, PZ), F32) for c in (5 * PY, 5 * PY, 6 * PX, 6 * PX)],
        in_specs=[hbm] * 3,
        out_specs=[vmem] * 4,
        scratch_shapes=[
            pltpu.SMEM((16,), F32),
            pltpu.VMEM((2, PY, PZ), jnp.int32),
            pltpu.VMEM((4, PX, 8, PZ), F32),
            pltpu.VMEM((4, PX, 8, PZ), F32),
            pltpu.VMEM((PX, 8, PZ), jnp.int32),
            pltpu.VMEM((PX, 8, PZ), jnp.int32),
            pltpu.SemaphoreType.DMA((21,)),
        ],
        cost_estimate=pl.CostEstimate(flops=1000, bytes_accessed=1000, transcendentals=0),
        name="edges",
    )(*[pltpu.with_memory_space_constraint(v, pltpu.HBM) for v in (fields, region, eps_table)])


def factor(m_at, count, first, h, b, rows):
    hv = jnp.ones((rows, PZ), F32)
    hs = jnp.where(first, jnp.zeros_like(hv), jnp.ones_like(hv))
    bv = jnp.ones((rows, PZ), F32)
    bs = jnp.ones((rows, PZ), F32)
    for i in range(count):
        k = count - 1 - i
        put(h, i, hv, rows)
        put(b, k, bv, rows)
        hs = hs + m_at(i) * hv
        bs = bs + m_at(k) * bv
        hlast, blast = hv, bv
        hv = hv + hs
        bv = bv + bs
    hn = 1.0 / hv
    bn = 1.0 / bv
    return hn, bn, blast * bn, hn, hlast * hn


def sweep(m_at, r_at, count, v, rows):
    vv = jnp.zeros((rows, PZ), F32)
    vs = jnp.zeros((rows, PZ), F32)
    for i in range(count):
        put(v, i, vv, rows)
        vs = vs + m_at(i) * (vv - r_at(i))
        last = vv
        vv = vv + vs
    return last, vv


def ends(last, vn, hn, c):
    return -vn * hn, last - c * vn


def spread(msg, count, values):
    block = sum(v.shape[0] for v in values)
    for k in range(count):
        at = k * block
        for v in values:
            msg[pl.ds(at, v.shape[0]), :] = v
            at += v.shape[0]


def k_x1(f, eps, xl, xr, yl, yr, msg, q1, m, h, b, v, hb, r):
    gx = x_index()
    gy = y_index()
    xlo = gx > 0
    ylo = gy > 0
    yhi = gy < y_size() - 1
    yin = jnp.where(ylo, 1.0, 0.0)
    yon = jnp.where(yhi, 1.0, 0.0)
    q1lo = yin * (plane(yl, 1, PX) - 0.5 * fz(plane(yl, 0, PX)))
    q1hi = yon * (plane(yr, 1, PX) - 0.5 * fz(plane(yr, 0, PX)))
    hxlo = yin * plane(yl, 3, PX)
    epslo = plane(yl, 5, PX)
    epshi = plane(yr, 4, PX)
    hx31 = f[pl.ds(HX * PX * PY + PY - 1, PX, stride=PY), :]
    bxlo = jnp.concatenate([q1lo[:1], q1lo[1:] - q1lo[:-1]], 0)
    bxhi = jnp.concatenate([q1hi[:1], q1hi[1:] - q1hi[:-1]], 0)
    rlo = yin * plane(yl, 2, PX) + (32.0 / epslo) * (bxlo - (hxlo - yin * plane(yl, 4, PX)))
    rhi = yon * plane(yr, 2, PX) + (32.0 / epshi) * (bxhi - (yon * plane(yr, 3, PX) - hx31))
    pad = jnp.zeros((XR - PY - 2, PZ), F32)
    one = jnp.ones((XR - PY - 2, PZ), F32)
    before = jnp.where(xlo, plane(xl, 2) - 0.5 * fz(plane(xl, 0)), 0.0)
    for x in range(PX):
        q = fplane(f, HY, x) - 0.5 * fz(fplane(f, EX, x))
        put(q1, x, q)
        e = plane(eps, x)
        hx = fplane(f, HX, x)
        ce = 32.0 / e
        rr = fplane(f, EZ, x) + ce * ((q - before) - (hx - y_prev(hx, hxlo[x : x + 1])))
        before = q
        r[pl.ds(x * XR, PY), :] = rr
        r[pl.ds(x * XR + PY, 8), :] = jnp.concatenate([rlo[x : x + 1], rhi[x : x + 1], pad], 0)
        m[pl.ds(x * XR, PY), :] = e * (1.0 / 1024.0)
        m[pl.ds(x * XR + PY, 8), :] = (
            jnp.concatenate([epslo[x : x + 1], epshi[x : x + 1], one], 0) * (1.0 / 1024.0)
        )
    m_at = lambda i: plane(m, i, XR)
    hn, bn, a, bb, c = factor(m_at, PX, gx == 0, h, b, XR)
    last, vn = sweep(m_at, lambda i: plane(r, i, XR), PX, v, XR)
    pf, plast = ends(last, vn, hn, c)
    put(hb, 0, hn, XR)
    put(hb, 1, bn, XR)
    put(hb, 2, c, XR)
    put(hb, 3, vn, XR)
    qq = jnp.concatenate([q1lo[PX - 1 :], q1hi[PX - 1 :]], 0) * (-1.0 / 32.0)
    spread(msg, lax.axis_size("gb"), packed((pf, plast, a, bb, c), XL, (qq,), XB))


def k_y1(f, eps, xl, xr, msg, p1, ey1, m, h, b, v, hb, r, ep):
    gx = x_index()
    gy = y_index()
    n = y_size()
    xlo = gx > 0
    xin = jnp.where(xlo, 1.0, 0.0)
    xon = jnp.where(gx < x_size() - 1, 1.0, 0.0)
    zero = jnp.zeros((1, PZ), F32)
    zeros = jnp.zeros((PY, PZ), F32)
    exl, eyl, hyl, hzl = [xin * plane(xl, i) for i in range(4)]
    eyr, ezr, hxr, hzr = [xon * plane(xr, i) for i in range(4)]
    for x in range(PX):
        put(ep, x, plane(eps, x))
    put(ep, PX, plane(xl, 4))
    put(ep, PX + 1, plane(xr, 4))
    for x in range(PX + 2, YR):
        put(ep, x, zeros + 1.0)
        put(r, x, zeros)
    put(r, PX + 1, zeros)

    def rex(ex, hy, pp, e):
        ie = 1.0 / e
        return ex + (32.0 * ie) * (pp - y_prev(pp, zero)) - (0.5 * ie) * bz(hy)

    p = hzl - 32.0 * (fplane(f, EY, 0) - eyl)
    p = jnp.where(xlo, p, 0.0)
    put(p1, PX, p)
    put(r, PX, rex(exl, hyl, p, plane(ep, PX)))
    for x in range(PX):
        ey = fplane(f, EY, x)
        nxt = fplane(f, EY, x + 1) if x < PX - 1 else eyr
        hz = fplane(f, HZ, x)
        hzp = fplane(f, HZ, x - 1) if x > 0 else hzl
        e = plane(ep, x)
        p = hz - 32.0 * (nxt - ey)
        put(p1, x, p)
        put(r, x, rex(fplane(f, EX, x), fplane(f, HY, x), p, e))
        ie = 1.0 / e
        put(ey1, x, ey + (0.5 * ie) * bz(fplane(f, HX, x)) - (32.0 * ie) * (hz - hzp))
    ie = 1.0 / plane(ep, PX + 1)
    put(ey1, PX, eyr + (0.5 * ie) * bz(hxr) - (32.0 * ie) * (hzr - fplane(f, HZ, PX - 1)))

    def rows(ref, j):
        return ref[pl.ds(j, YR, stride=PY), :]

    for j in range(PY):
        put(m, j, rows(ep, j) * (1.0 / 1024.0), YR)
    m_at = lambda j: plane(m, j, YR)
    hn, bn, a, bb, c = factor(m_at, PY, gy == 0, h, b, YR)
    last, vn = sweep(m_at, lambda j: rows(r, j), PY, v, YR)
    pf, plast = ends(last, vn, hn, c)
    put(hb, 0, hn, YR)
    put(hb, 1, bn, YR)
    put(hb, 2, c, YR)
    put(hb, 3, vn, YR)
    lastrow = lambda ref, at, k: ref[pl.ds(at * PY + PY - 1, k, stride=PY), :]
    tail = jnp.zeros((7, PZ), F32)
    qq = jnp.concatenate([lastrow(p1, 0, PX), lastrow(p1, PX, 1), tail], 0) * (-1.0 / 32.0)
    tail = jnp.zeros((6, PZ), F32)
    ee = fz(jnp.concatenate([lastrow(ey1, 0, PX), zero, lastrow(ey1, PX, 1), tail], 0))
    spread(msg, 1, packed((pf, plast, a, bb, c, qq, ee), YL, (), YB))


def coefficients(part, n, rows, tp, bp, ts, bs, bet, dele):
    zero = jnp.zeros((rows, PZ), F32)
    beta = zero
    put(bet, 0, zero, rows)
    for j in range(n):
        a, b, c = part(j, 2), part(j, 3), part(j, 4)
        bd = b / (1.0 - a * beta)
        t = bd * beta
        put(tp, j, t, rows)
        put(bp, j, bd, rows)
        beta = c + t * b
        put(bet, j + 1, beta, rows)
    delta = zero
    put(dele, n, zero, rows)
    for j in range(n - 1, -1, -1):
        a, b, c = part(j, 2), part(j, 3), part(j, 4)
        bd = b / (1.0 - c * delta)
        t = bd * delta
        put(ts, j, t, rows)
        put(bs, j, bd, rows)
        delta = a + t * b
        put(dele, j, delta, rows)


def chain(part, n, rows, crows, tp, bp, ts, bs, al, ga, start, stop):
    take = lambda ref, j: ref[pl.ds(j * crows, rows), :]
    alpha, gamma = start, stop
    put(al, 0, alpha, rows)
    put(ga, n, gamma, rows)
    for j in range(n):
        k = n - 1 - j
        alpha = part(j, 1) + take(tp, j) * part(j, 0) + take(bp, j) * alpha
        gamma = part(k, 0) + take(ts, k) * part(k, 1) + take(bs, k) * gamma
        put(al, j + 1, alpha, rows)
        put(ga, k, gamma, rows)
    return gamma, alpha


def interface(part, n, me, rows, coefs, al, ga, start=None, stop=None, crows=None):
    crows = crows or rows
    tp, bp, ts, bs, bet, dele = coefs
    zero = jnp.zeros((rows, PZ), F32)
    start = zero if start is None else start
    stop = zero if stop is None else stop
    chain(part, n, rows, crows, tp, bp, ts, bs, al, ga, start, stop)
    at = lambda ref, d, size: ref[pl.ds(pl.multiple_of(d * size, 8), rows), :]
    a0, a1 = at(al, me, rows), at(al, me + 1, rows)
    g0, g1 = at(ga, me, rows), at(ga, me + 1, rows)
    b0, b1 = at(bet, me, crows), at(bet, me + 1, crows)
    d0, d1 = at(dele, me, crows), at(dele, me + 1, crows)
    left = a0 + b0 * ((g0 + d0 * a0) / (1.0 - d0 * b0))
    right = g1 + d1 * ((a1 + b1 * g1) / (1.0 - b1 * d1))
    return left, right


def x_raw(msg):
    return lambda j, k: msg[pl.ds(j * XB + k * XL, XR), :]


def x_late(msg, at):
    return pltpu.roll(msg[pl.ds(at + XB - 8, 8), :], 6, 0)


def x_part(msg):
    def part(j, k):
        if j == 0:
            return x_raw(msg)(j, k)
        own = msg[pl.ds(j * XB + k * XL, PY), :]
        more = (
            msg[pl.ds(j * XB + k * XL + PY, 8), :]
            + msg[pl.ds(j * XB + (2 + k) * XL + PY, 8), :] * x_late(msg, (j - 1) * XB)
        )
        return jnp.concatenate([own, more], 0)

    return part


def x_passed(msg, me):
    prev = pl.multiple_of(jnp.maximum(me - 1, 0) * XB, 8)
    return jnp.where(me > 0, x_late(msg, prev), 0.0)


def y_raw(msg):
    return lambda j, k: msg[pl.ds(j * YB + k * YL, YR), :]


def y_part(msg):
    raw = y_raw(msg)
    return lambda j, k: raw(j, k) + raw(j, 2 + k) * raw(j - 1, 5) if j else raw(j, k)


def y_passed(msg, me, k):
    skip = k * YL % 8
    prev = pl.multiple_of(jnp.maximum(me - 1, 0) * YB + k * YL - skip, 8)
    return jnp.where(me > 0, pltpu.roll(msg[pl.ds(prev, YR), :], YR - skip, 0), 0.0)


def k_y2(gi, go, p1, h, b, v, hb, ex1, p2, elo, *more):
    coi, coo, (al, ga, dex) = more[:6], more[6:12], more[12:]
    nz, nc = lax.axis_size("gz"), lax.axis_size("gc")
    iz, ic = lax.axis_index("gz"), lax.axis_index("gc")
    coefficients(y_raw(go), nz, YR, *coo)
    coefficients(y_raw(gi), nc, YR, *coi)
    left, right = interface(y_part(go), nz, iz, YR, coo, al, ga)
    left = left + y_passed(go, iz, 5)
    left, right = interface(y_part(gi), nc, ic, YR, coi, al, ga, left, right)
    left = left + y_passed(gi, ic, 5)
    elo[...] = jnp.where(ic > 0, y_passed(gi, ic, 6), y_passed(go, iz, 6))
    lw = left * plane(hb, 1, YR)
    rw = (right - plane(hb, 3, YR)) * plane(hb, 0, YR)
    later = right
    for j in range(PY - 1, -1, -1):
        w = plane(v, j, YR) + plane(b, j, YR) * lw + plane(h, j, YR) * rw
        ex1[pl.ds(j, YR, stride=PY), :] = w
        dex[pl.ds(j, YR, stride=PY), :] = later - w
        later = w
    live = jnp.where(x_index() > 0, 1.0, 0.0)
    for x in range(PX):
        put(p2, x, plane(p1, x) + 64.0 * plane(dex, x))
    put(p2, PX, live * (plane(p1, PX) + 64.0 * plane(dex, PX)))


def join(part, raw, count):
    pf, ph, a, b, c = part(0, 0), part(0, 1), raw(0, 2), raw(0, 3), raw(0, 4)
    for j in range(1, count):
        qf, qh, a2, b2, c2 = part(j, 0), part(j, 1), raw(j, 2), raw(j, 3), raw(j, 4)
        den = 1.0 / (1.0 - c * a2)
        low, high = b * den, b2 * den
        pf, ph = pf + low * (qf + a2 * ph), qh + high * (ph + c * qf)
        a, b, c = a + low * b * a2, low * b2, c2 + high * b2 * c
    return pf, ph, a, b, c


def k_join_y(gi, msg):
    nc = lax.axis_size("gc")
    raw = y_raw(gi)
    values = join(y_part(gi), raw, nc)
    more = gi[pl.ds((nc - 1) * YB + 5 * YL, 2 * YL), :]
    spread(msg, 1, packed(values, YL, (more,), YB))


def k_join_x(gi, msg, inner):
    inner[...] = gi[...]
    nb = lax.axis_size("gb")
    last = x_late(gi, (nb - 1) * XB)[:2]
    spread(msg, lax.axis_size("ga"), packed(join(x_part(gi), x_raw(gi), nb), XL, (last,), XB))


def shares(pf, ph, coefs, count, me, rows, crows):
    tp, bp, ts, bs = coefs[:4]
    low = high = jnp.ones((rows, PZ), F32)
    for k in range(count):
        low = jnp.where(k < me, low * bs[pl.ds(k * crows, rows), :], low)
        high = jnp.where(k > me, high * bp[pl.ds(k * crows, rows), :], high)
    mine = pl.ds(pl.multiple_of(me * crows, 8), rows)
    return low * (pf + ts[mine, :] * ph), high * (ph + tp[mine, :] * pf)


def gathered(msg, n, m, ia, ib, rows, crows, coi, coo, al, ga):
    zero = jnp.zeros((rows, PZ), F32)

    def inside(j, k):
        at = pl.multiple_of(((ia * m + j) * 2 + k) * rows, 8)
        return msg[pl.ds(at, rows), :]

    whole = chain(inside, m, rows, crows, *coi[:4], al, ga, zero, zero)

    def group(j, k):
        total = sum(msg[pl.ds(((j * m + i) * 2 + k) * rows, rows), :] for i in range(m))
        return jnp.where(ia == j, whole[k], total)

    left, right = interface(group, n, ia, rows, coo, al, ga, crows=crows)
    return interface(inside, m, ib, rows, coi, al, ga, left, right, crows)


def k_x2(gi, go, f, q1, ey1, p2, h, b, v, m, hb, ez1, hx1, msg2, v2, vn2, *more):
    coi, coo, (al, ga, r) = more[:6], more[6:12], more[12:]
    na, nb = lax.axis_size("ga"), lax.axis_size("gb")
    ia, ib = lax.axis_index("ga"), lax.axis_index("gb")
    gy = y_index()
    yon = jnp.where(gy < y_size() - 1, 1.0, 0.0)
    coefficients(x_raw(go), na, XR, *coo)
    coefficients(x_raw(gi), nb, XR, *coi)
    left, right = interface(x_part(go), na, ia, XR, coo, al, ga)
    left = jnp.concatenate([left[:PY], left[PY:] + x_passed(go, ia)], 0)
    left, right = interface(x_part(gi), nb, ib, XR, coi, al, ga, left, right)
    left = jnp.concatenate([left[:PY], left[PY:] + x_passed(gi, ib)], 0)
    lw = left * plane(hb, 1, XR)
    rw = (right - plane(hb, 3, XR)) * plane(hb, 0, XR)
    for x in range(PX):
        put(ez1, x, plane(v, x, XR) + plane(b, x, XR) * lw + plane(h, x, XR) * rw, XR)
    put(ez1, PX, right, XR)
    before = plane(p2, PX)
    for x in range(PX):
        z = ez1[pl.ds(x * XR, PY), :]
        z32 = yon * ez1[pl.ds(x * XR + PY + 1, 1), :]
        ey = plane(ey1, x)
        t = fplane(f, HX, x) - 32.0 * (y_next(z, z32) - z) + 0.5 * fz(ey)
        put(hx1, x, t)
        p = plane(p2, x)
        ie = 1.0 / (m[pl.ds(x * XR, PY), :] * 1024.0)
        put(r, x, ey + (0.5 * ie) * bz(t) - (32.0 * ie) * (p - before))
        before = p
    last, vn = sweep(lambda i: m[pl.ds(i * XR, PY), :], lambda i: plane(r, i), PX, v2, PY)
    vn2[...] = vn
    pf, plast = ends(last, vn, hb[pl.ds(0, PY), :], hb[pl.ds(2 * XR, PY), :])
    share = shares(pf, plast, coi, nb, ib, PY, XR)
    for k in range(na * nb):
        for i, (own, joined) in enumerate(zip((pf, plast), share)):
            put(msg2, 2 * k + i, jnp.where(ia == k // nb, own, joined))


def k_y3(f, xr, q1, mx, ey1, ez1, hx1, ex1, elo, ex2, hy1, q2, r):
    n = y_size()
    gy = y_index()
    yon = jnp.where(gy < n - 1, 1.0, 0.0)
    yin = jnp.where(gy > 0, 1.0, 0.0)
    zeros = jnp.zeros((PY, PZ), F32)
    for x in range(PX + 2, YR):
        put(r, x, zeros)
    put(r, PX, zeros)
    for x in range(PX + 1):
        at = x * XR
        z = ez1[pl.ds(at, PY), :]
        zlo = ez1[pl.ds(at + PY, 1), :]
        zhi = yon * ez1[pl.ds(at + PY + 1, 1), :]
        fe = fz(plane(ey1, x))
        d = 32.0 * (y_next(z, zhi) - z) - fe
        k = x if x < PX else PX + 1
        dlo = yin * (32.0 * (z[:1] - zlo) - elo[pl.ds(k, 1), :])
        ez = fplane(f, EZ, x) if x < PX else plane(xr, 1)
        e = mx[pl.ds(at, PY), :] * 1024.0 if x < PX else plane(xr, 4)
        ie = 1.0 / e
        put(r, k, 2.0 * z - ez + (32.0 * ie) * (d - y_prev(d, dlo)))
        if x < PX:
            t = plane(q1, x) + 32.0 * (ez1[pl.ds(at + XR, PY), :] - z)
            put(hy1, x, t)
            put(ex2, x, 2.0 * plane(ex1, x) - fplane(f, EX, x) + (0.5 * ie) * bz(fplane(f, HY, x) - t))
            put(q2, x, plane(hx1, x) + 0.5 * fe)


def k_y3_sweep(r, m, hb, msg2, v2, vn2):
    m_at = lambda j: plane(m, j, YR)
    last, vn = sweep(m_at, lambda j: r[pl.ds(j, YR, stride=PY), :], PY, v2, YR)
    vn2[...] = vn
    pf, plast = ends(last, vn, plane(hb, 0, YR), plane(hb, 2, YR))
    spread(msg2, 1, (pf, plast))


def y_ends(msg):
    return lambda j, k: msg[pl.ds((2 * j + k) * YR, YR), :]


def k_join_ends(gi, tp, bp, ts, bs, msg, al, ga):
    nc = lax.axis_size("gc")
    zero = jnp.zeros((YR, PZ), F32)
    spread(msg, 1, chain(y_ends(gi), nc, YR, YR, tp, bp, ts, bs, al, ga, zero, zero))


def k_y4(gi, go, h, b, v2, vn2, hb, *more):
    coi, coo, (ex2, hy1, q2, out, al, ga, w2, dw) = more[:6], more[6:12], more[12:]
    nz, nc = lax.axis_size("gz"), lax.axis_size("gc")
    iz, ic = lax.axis_index("gz"), lax.axis_index("gc")
    left, right = interface(y_ends(go), nz, iz, YR, coo, al, ga)
    left, right = interface(y_ends(gi), nc, ic, YR, coi, al, ga, left, right)
    lw = left * plane(hb, 1, YR)
    rw = (right - vn2[...]) * plane(hb, 0, YR)
    later = right
    for j in range(PY - 1, -1, -1):
        w = plane(v2, j, YR) + plane(b, j, YR) * lw + plane(h, j, YR) * rw
        w2[pl.ds(j, YR, stride=PY), :] = w
        dw[pl.ds(j, YR, stride=PY), :] = later - w
        later = w
    xon = jnp.where(x_index() < x_size() - 1, 1.0, 0.0)
    for x in range(PX):
        w = plane(w2, x)
        nxt = plane(w2, x + 1) if x < PX - 1 else xon * plane(w2, PX + 1)
        e2 = plane(ex2, x)
        put(out, EX * PX + x, e2)
        put(out, EZ * PX + x, w)
        put(out, HX * PX + x, plane(q2, x) - 32.0 * plane(dw, x))
        put(out, HY * PX + x, plane(hy1, x) - 0.5 * fz(e2) + 32.0 * (nxt - w))


def k_x4(msg, h, b, v2, vn2, hb, *more):
    coi, coo, (p2, out, al, ga) = more[:6], more[6:12], more[12:]
    na, nb = lax.axis_size("ga"), lax.axis_size("gb")
    ia, ib = lax.axis_index("ga"), lax.axis_index("gb")
    left, right = gathered(msg, na, nb, ia, ib, PY, XR, coi, coo, al, ga)
    lw = left * hb[pl.ds(XR, PY), :]
    rw = (right - vn2[...]) * hb[pl.ds(0, PY), :]
    later = right
    for x in range(PX - 1, -1, -1):
        w = plane(v2, x) + b[pl.ds(x * XR, PY), :] * lw + h[pl.ds(x * XR, PY), :] * rw
        put(out, EY * PX + x, w)
        put(out, HZ * PX + x, plane(p2, x) - 32.0 * (later - w))
        later = w


def call(name, parts, args, outs, scratch=(), smem=(), into=(), flush=(), near=(), only=(), views=()):
    into, flush, scratch, only = dict(into), dict(flush), dict(scratch), dict(only)
    views = dict(views)
    touched = [list(used) + [views[k][0] for k in used if k in views] for _, used in parts]
    moved = [k for k in args if k not in smem and (k not in near or k in into)]
    pieces = {k for group in flush.values() for k, _, _ in group}
    last = {k: max(i for i, used in enumerate(touched) if k in used) for k in outs}
    leave = [
        [(k, 0, outs[k]) for k in outs if last[k] == i and k not in pieces and k not in near]
        + list(flush.get(i, ()))
        for i in range(len(parts))
    ]
    own = [k for k in moved if k not in into]

    def body(*refs):
        take = iter(refs)
        hbm = {k: next(take) for k in args}
        results = {k: next(take) for k in outs}
        env = {k: next(take) for k in own}
        env.update({k: results[k] if k in near else next(take) for k in outs})
        env.update({k: next(take) for k in scratch})
        env.update({k: hbm[k] for k in args if k not in moved})
        env.update({k: env[b].at[pl.ds(at, rows), :] for k, (b, at, rows) in views.items()})
        sem_in, sem_out = next(take), next(take)
        pending = {}
        count = 0
        for k in moved:
            pairs = [(hbm[k], env.get(k))]
            if k in into:
                buffer, row = into[k]
                pairs = [(hbm[k], env[buffer].at[pl.ds(row(), args[k].shape[0]), :])]
            elif k in only:
                windows = [pl.ds(at, rows) for at, rows in only[k]]
                pairs = [(hbm[k].at[w, :], env[k].at[w, :]) for w in windows]
            for source, where in pairs:
                copy = pltpu.make_async_copy(source, where, sem_in.at[count])
                copy.start()
                count += 1
                pending.setdefault(into[k][0] if k in into else k, []).append(copy)
        sent = []
        for i, (function, used) in enumerate(parts):
            for k in touched[i]:
                for copy in pending.pop(k, ()):
                    copy.wait()
            function(*[env[k] for k in used])
            for k, row, rows in leave[i]:
                window = pl.ds(row, rows)
                copy = pltpu.make_async_copy(
                    env[k].at[window, :], results[k].at[window, :], sem_out.at[len(sent)]
                )
                copy.start()
                sent.append(copy)
        for copy in sent:
            copy.wait()

    far, close, scalars = [
        pl.BlockSpec(memory_space=m) for m in (pltpu.HBM, pltpu.VMEM, pltpu.SMEM)
    ]
    got = pl.pallas_call(
        body,
        out_shape=[(pltpu.VMEM if k in near else pltpu.HBM)((c, PZ), F32) for k, c in outs.items()],
        in_specs=[scalars if k in smem else close if k in near else far for k in args],
        out_specs=[close if k in near else far for k in outs],
        scratch_shapes=[pltpu.VMEM(args[k].shape, args[k].dtype) for k in own]
        + [pltpu.VMEM((c, PZ), F32) for k, c in outs.items() if k not in near]
        + [pltpu.VMEM((c, PZ), F32) for c in scratch.values()]
        + [
            pltpu.SemaphoreType.DMA((sum(len(only.get(k, (0,))) for k in moved),)),
            pltpu.SemaphoreType.DMA((max(1, sum(len(group) for group in leave)),)),
        ],
        compiler_params=pltpu.CompilerParams(vmem_limit_bytes=LIMIT * 1024 * 1024),
        cost_estimate=pl.CostEstimate(flops=1000, bytes_accessed=1000, transcendentals=0),
        name=name,
    )(*[a if k in smem else pltpu.with_memory_space_constraint(a, pltpu.VMEM if k in near else pltpu.HBM) for k, a in args.items()])
    return dict(zip(outs, got))


def stacked(buffer, names, rows):
    return {k: (buffer, sum(rows[:i]), rows[i]) for i, k in enumerate(names)}


def ring(block, axis, step):
    n = lax.axis_size(axis)
    return lax.ppermute(block, axis, [(i, (i + step) % n) for i in range(n)])


def swap(msg, axis):
    n = lax.axis_size(axis)
    got = lax.all_to_all(msg.reshape(n, -1, PZ), axis, 0, 0, tiled=True)
    return got.reshape(-1, PZ)


def from_all(msg, axis, buffer):
    n = lax.axis_size(axis)
    rows = msg.shape[0]
    args, into = {}, {}
    for step in range(n):
        k = buffer + str(step)
        args[k] = ring(msg, axis, step) if step else msg

        def row(step=step):
            return pl.multiple_of(lax.rem(lax.axis_index(axis) - step + n, n) * rows, 8)

        into[k] = (buffer, row)
    return args, into


def local(fields, region, eps_table):
    na, nb = lax.axis_size("ga"), lax.axis_size("gb")
    along_x, along_y = ("ga", "gb"), ("gz", "gc")
    nz, nc = lax.axis_size("gz"), lax.axis_size("gc")
    ny = nz * nc
    ey = (max(nz, nc) + 1) * YR
    cells = PX * PY
    nxl, nyl = PX * XR, PY * YR
    f = fields.reshape(6 * cells, PZ)
    reg = region.reshape(cells, PZ)
    xup, xdn, yup, ydn = edges(fields, region, eps_table)
    xl = ring(xup, along_x, 1)
    xr = ring(xdn, along_x, -1)
    yl = ring(yup, along_y, 1)
    yr = ring(ydn, along_y, -1)
    linex = ("mx", "hx", "bx", "vx", "hbx")
    liney = ("my", "hy", "by", "vy", "hby")
    lines_x, lines_y = 4 * nxl + 4 * XR, 4 * nyl + 4 * YR
    lines = {
        **stacked("lx", ("mx", "vx", "hx", "bx", "hbx"), (nxl,) * 4 + (4 * XR,)),
        **stacked("ly", ("my", "vy", "hy", "by", "hby"), (nyl,) * 4 + (4 * YR,)),
    }
    of = lambda names: {k: lines[k] for k in names}
    one = call(
        "onex",
        [
            (k_eps, ("reg", "table", "eps")),
            (k_x1, ("f", "eps", "xl", "xr", "yl", "yr", "msgx", "q1") + linex + ("r",)),
        ],
        dict(xl=xl, xr=xr, yl=yl, yr=yr, reg=reg, f=f, table=eps_table),
        dict(eps=cells, q1=cells, lx=lines_x, msgx=nb * XB),
        dict(r=nxl),
        smem=("table",),
        near=("xl", "xr", "yl", "yr") + NEAR,
        flush={0: [("eps", 0, cells)]},
        views=of(linex),
        only=dict(f=[(EX * cells, cells), (EZ * cells, 3 * cells)]),
    )
    oney = call(
        "oney",
        [(k_y1, ("f", "eps", "xl", "xr", "msgy", "p1", "ey1") + liney + ("rt", "ep"))],
        dict(f=f, eps=one["eps"], xl=xl, xr=xr),
        dict(msgy=YB, p1=cells + PY, ey1=cells + PY, ly=lines_y),
        dict(rt=YR * PY, ep=YR * PY),
        near=("msgy",),
        views=of(liney),
        only=dict(f=[(EX * cells, 2 * cells), (HX * cells, 3 * cells)]),
    )
    one.update(oney)
    pair, into = from_all(one["msgy"], "gc", "gyi")
    group = call(
        "group",
        [
            (k_join_y, ("gyi", "msgyo")),
            (k_join_x, ("gi", "msgo", "inner")),
        ],
        dict(pair, gi=swap(one["msgx"], "gb")),
        dict(msgyo=YB, msgo=na * XB, inner=nb * XB),
        dict(gyi=nc * YB),
        into=into,
        near=("gi", "msgyo") + NEAR + tuple(pair),
    )
    goto = swap(group["msgo"], "ga")
    argy, into_o = from_all(group["msgyo"], "gz", "gyo")
    argy.update(pair)
    into.update(into_o)
    chains = ("tp", "bp", "ts", "bs", "bet", "del")
    ci, co, cyi, cyo = [tuple(k + a for k in chains) for a in ("i", "o", "yi", "yo")]
    cx, cy = ci + co, cyi + cyo
    size = lambda n, rows: (n * rows,) * 4 + ((n + 1) * rows,) * 2
    keep = {k: one[k] for k in ("q1", "p1", "ey1", "lx", "ly")}
    rows_y, rows_x = size(nc, YR) + size(nz, YR), size(nb, XR) + size(na, XR)
    views = {**stacked("cy", cy, rows_y), **stacked("cx", cx, rows_x)}
    two = call(
        "two",
        [
            (k_y2, ("gyi", "gyo", "p1", "hy", "by", "vy", "hby", "ex1", "p2", "elo") + cy + ("aly", "gay", "dex")),
            (
                k_x2,
                ("gi", "go", "f", "q1", "ey1", "p2", "hx", "bx", "vx", "mx", "hbx")
                + ("ez1", "hx1", "msgx2", "vx2", "vnx2")
                + cx
                + ("alx", "gax", "r"),
            ),
            (
                k_y3,
                ("f", "xr", "q1", "mx", "ey1", "ez1", "hx1", "ex1", "elo", "ex2", "hy1", "q2", "rt"),
            ),
            (k_y3_sweep, ("rt", "my", "hby", "msgy2", "vy2", "vny2")),
        ],
        dict(argy, **{k: keep[k] for k in ("ly", "p1")}, gi=group["inner"], go=goto, f=f, xr=xr, **{k: keep[k] for k in ("lx", "ey1", "q1")}),
        dict(
            zip(
                ("p2", "cy", "msgx2", "vx2", "vnx2", "cx", "msgy2", "vy2", "vny2", "ex2", "hy1", "q2"),
                (cells + PY, sum(rows_y), na * nb * 2 * PY, cells, PY, sum(rows_x))
                + (2 * YR, nyl, YR, cells, cells, cells),
            )
        ),
        dict(
            gyi=nc * YB, gyo=nz * YB, ex1=YR * PY, elo=YR, aly=ey, gay=ey, dex=YR * PY,
            ez1=nxl + XR, hx1=cells, alx=(max(na, nb) + 1) * XR, gax=(max(na, nb) + 1) * XR, r=cells, rt=YR * PY,
        ),
        into=into,
        near=("go", "msgy2", "party2") + NEAR + tuple(k for k in argy if k not in pair),
        flush={0: [("p2", 0, cells + PY), ("cy", 0, sum(rows_y))]},
        views={**views, **lines},
        only=dict(f=[(EX * cells, cells), (EZ * cells, 3 * cells)]),
    )
    gotx = swap(two["msgx2"], along_x)
    pair, into = from_all(two["msgy2"], "gc", "gyi")
    group = call(
        "ends",
        [(k_join_ends, ("gyi",) + cyi[:4] + ("msg", "aly", "gay"))],
        dict(pair, cy=two["cy"]),
        dict(msg=2 * YR),
        dict(gyi=nc * 2 * YR, aly=ey, gay=ey),
        into=into,
        near=tuple(pair) + ("msg",),
        views={k: views[k] for k in cyi[:4]},
        only=dict(cy=[(0, sum(rows_y[:4]))]),
    )
    argy, into_o = from_all(group["msg"], "gz", "gyo")
    argy.update(pair)
    into.update(into_o)
    order = ("cy", "ly", "vny2", "vy2", "ex2", "q2", "hy1", "cx", "lx", "vnx2", "vx2", "p2")
    need = {k: two.get(k, one.get(k)) for k in order}
    three = call(
        "three",
        [
            (
                k_y4,
                ("gyi", "gyo", "hy", "by", "vy2", "vny2", "hby") + cy + ("ex2", "hy1", "q2", "out")
                + ("aly", "gay", "w2", "dw"),
            ),
            (k_x4, ("gx", "hx", "bx", "vx2", "vnx2", "hbx") + cx + ("p2", "out", "alx", "gax")),
        ],
        dict(argy, gx=gotx, **need),
        dict(out=6 * cells),
        dict(
            gyi=nc * 2 * YR, gyo=nz * 2 * YR, aly=ey, gay=ey, w2=YR * PY, dw=YR * PY,
            alx=(max(na, nb) + 1) * PY, gax=(max(na, nb) + 1) * PY,
        ),
        into=into,
        near=("gx",) + tuple(argy),
        views={**views, **of(("hx", "bx", "hbx", "hy", "by", "hby"))},
        only=dict(lx=[(2 * nxl, lines_x - 2 * nxl)], ly=[(2 * nyl, lines_y - 2 * nyl)]),
        flush={
            0: [("out", EX * cells, cells), ("out", EZ * cells, 3 * cells)],
            1: [("out", EY * cells, cells), ("out", HZ * cells, cells)],
        },
    )
    return three["out"].reshape(6, PX, PY, PZ)


def solution(mesh):
    nx, ny = mesh.devices.shape
    nb = max(d for d in range(1, nx + 1) if nx % d == 0 and d * d <= nx)
    shape = (nx // nb, nb, ny // 2, 2)
    grid = Mesh(mesh.devices.reshape(shape), ("ga", "gb", "gz", "gc"))
    columns = P(("ga", "gb"), ("gz", "gc"), None)
    return jax.shard_map(
        local,
        mesh=grid,
        in_specs=(P(None, *columns), columns, P()),
        out_specs=P(None, *columns),
        check_vma=False,
    )
```

```python
import functools

import jax
import jax.numpy as jnp
from jax import lax
from jax.experimental import pallas as pl
from jax.experimental.pallas import tpu as pltpu
from jax.sharding import Mesh
from jax.sharding import PartitionSpec as P

PX, PY, PZ = 16, 32, 128
XL, YL = PY + 2, PX + 2
XR = 40
YR = 24
F32 = jnp.float32
LIMIT = 30
NEAR = ()
EX, EY, EZ, HX, HY, HZ = range(6)
XB, YB = 5 * XL + 6, 7 * YL + 2


def x_index():
    return lax.axis_index("ga") * lax.axis_size("gb") + lax.axis_index("gb")


def y_index():
    return lax.axis_index("gz") * lax.axis_size("gc") + lax.axis_index("gc")


def y_size():
    return lax.axis_size("gz") * lax.axis_size("gc")


def x_size():
    return lax.axis_size("ga") * lax.axis_size("gb")


def sub():
    return lax.broadcasted_iota(jnp.int32, (PY, PZ), 0)


def lanes_of(v):
    return lax.broadcasted_iota(jnp.int32, v.shape, 1)


def z_next(v):
    return jnp.where(lanes_of(v) == PZ - 1, 0.0, pltpu.roll(v, PZ - 1, 1))


def z_prev(v):
    return jnp.where(lanes_of(v) == 0, 0.0, pltpu.roll(v, 1, 1))


def fz(v):
    return z_next(v) - v


def bz(v):
    return v - z_prev(v)


def y_prev(v, row):
    return jnp.where(sub() == 0, row, pltpu.roll(v, 1, 0))


def y_next(v, row):
    return jnp.where(sub() == PY - 1, row, pltpu.roll(v, PY - 1, 0))


def plane(ref, k, size=PY):
    return ref[pl.ds(k * size, size), :]


def put(ref, k, v, size=PY):
    ref[pl.ds(k * size, size), :] = v


def fplane(ref, f, x):
    return plane(ref, f * PX + x)


def lookup(region, table):
    level = [table[i] for i in range(16)]
    for bit in range(4):
        on = (region & (1 << bit)) != 0
        level = [jnp.where(on, level[2 * i + 1], level[2 * i]) for i in range(len(level) // 2)]
    return level[0]


def packed(values, lines, more, rows):
    parts = [v[:lines] for v in values] + list(more)
    pad = rows - sum(v.shape[0] for v in parts)
    return (jnp.concatenate(parts + [jnp.zeros((pad, PZ), F32)], 0),)


def k_eps(reg, table, eps):
    tab = [table[i] for i in range(16)]
    for x in range(PX):
        put(eps, x, lookup(plane(reg, x), tab))


def k_edges(f, reg, table, xup, xdn, yup, ydn, tab, ends, low, high, rlow, rhigh, sems):
    up, down = (EX, EY, HY, HZ), (EY, EZ, HX, HZ)
    rows = (EX, HY, EZ, HX)
    top = pl.ds(PY - 8, 8)
    pairs = [(table, tab), (reg.at[PX - 1], ends.at[0]), (reg.at[0], ends.at[1])]
    pairs += [(reg.at[:, top, :], rhigh), (reg.at[:, pl.ds(0, 8), :], rlow)]
    for i in range(4):
        pairs += [
            (f.at[up[i], PX - 1], xup.at[pl.ds(i * PY, PY), :]),
            (f.at[down[i], 0], xdn.at[pl.ds(i * PY, PY), :]),
            (f.at[rows[i], :, top, :], high.at[i]),
            (f.at[rows[i], :, pl.ds(0, 8), :], low.at[i]),
        ]
    copies = [pltpu.make_async_copy(p, q, sems.at[i]) for i, (p, q) in enumerate(pairs)]
    for copy in copies:
        copy.start()
    for copy in copies:
        copy.wait()
    t = [tab[i] for i in range(16)]
    put(xup, 4, lookup(ends[0], t))
    put(xdn, 4, lookup(ends[1], t))
    for i in range(4):
        put(yup, i, high[i, :, 7, :], PX)
        put(ydn, i, low[i, :, 0, :], PX)
    put(yup, 4, high[3, :, 6, :], PX)
    put(yup, 5, lookup(rhigh[:, 7, :], t), PX)
    put(ydn, 4, lookup(rlow[:, 0, :], t), PX)


def edges(fields, region, eps_table):
    vmem, hbm = [pl.BlockSpec(memory_space=m) for m in (pltpu.VMEM, pltpu.HBM)]
    return pl.pallas_call(
        k_edges,
        out_shape=[pltpu.VMEM((c, PZ), F32) for c in (5 * PY, 5 * PY, 6 * PX, 6 * PX)],
        in_specs=[hbm] * 3,
        out_specs=[vmem] * 4,
        scratch_shapes=[
            pltpu.SMEM((16,), F32),
            pltpu.VMEM((2, PY, PZ), jnp.int32),
            pltpu.VMEM((4, PX, 8, PZ), F32),
            pltpu.VMEM((4, PX, 8, PZ), F32),
            pltpu.VMEM((PX, 8, PZ), jnp.int32),
            pltpu.VMEM((PX, 8, PZ), jnp.int32),
            pltpu.SemaphoreType.DMA((21,)),
        ],
        cost_estimate=pl.CostEstimate(flops=1000, bytes_accessed=1000, transcendentals=0),
        name="edges",
    )(*[pltpu.with_memory_space_constraint(v, pltpu.HBM) for v in (fields, region, eps_table)])


def factor(m_at, count, first, h, b, rows):
    hv = jnp.ones((rows, PZ), F32)
    hs = jnp.where(first, jnp.zeros_like(hv), jnp.ones_like(hv))
    bv = jnp.ones((rows, PZ), F32)
    bs = jnp.ones((rows, PZ), F32)
    for i in range(count):
        k = count - 1 - i
        put(h, i, hv, rows)
        put(b, k, bv, rows)
        hs = hs + m_at(i) * hv
        bs = bs + m_at(k) * bv
        hlast, blast = hv, bv
        hv = hv + hs
        bv = bv + bs
    hn = 1.0 / hv
    bn = 1.0 / bv
    return hn, bn, blast * bn, hn, hlast * hn


def sweep(m_at, r_at, count, v, rows):
    vv = jnp.zeros((rows, PZ), F32)
    vs = jnp.zeros((rows, PZ), F32)
    for i in range(count):
        put(v, i, vv, rows)
        vs = vs + m_at(i) * (vv - r_at(i))
        last = vv
        vv = vv + vs
    return last, vv


def ends(last, vn, hn, c):
    return -vn * hn, last - c * vn


def spread(msg, count, values):
    block = sum(v.shape[0] for v in values)
    for k in range(count):
        at = k * block
        for v in values:
            msg[pl.ds(at, v.shape[0]), :] = v
            at += v.shape[0]


def k_x1(f, eps, xl, xr, yl, yr, msg, q1, m, h, b, v, hb, r):
    gx = x_index()
    gy = y_index()
    xlo = gx > 0
    ylo = gy > 0
    yhi = gy < y_size() - 1
    yin = jnp.where(ylo, 1.0, 0.0)
    yon = jnp.where(yhi, 1.0, 0.0)
    q1lo = yin * (plane(yl, 1, PX) - 0.5 * fz(plane(yl, 0, PX)))
    q1hi = yon * (plane(yr, 1, PX) - 0.5 * fz(plane(yr, 0, PX)))
    hxlo = yin * plane(yl, 3, PX)
    epslo = plane(yl, 5, PX)
    epshi = plane(yr, 4, PX)
    hx31 = f[pl.ds(HX * PX * PY + PY - 1, PX, stride=PY), :]
    bxlo = jnp.concatenate([q1lo[:1], q1lo[1:] - q1lo[:-1]], 0)
    bxhi = jnp.concatenate([q1hi[:1], q1hi[1:] - q1hi[:-1]], 0)
    rlo = yin * plane(yl, 2, PX) + (32.0 / epslo) * (bxlo - (hxlo - yin * plane(yl, 4, PX)))
    rhi = yon * plane(yr, 2, PX) + (32.0 / epshi) * (bxhi - (yon * plane(yr, 3, PX) - hx31))
    pad = jnp.zeros((XR - PY - 2, PZ), F32)
    one = jnp.ones((XR - PY - 2, PZ), F32)
    before = jnp.where(xlo, plane(xl, 2) - 0.5 * fz(plane(xl, 0)), 0.0)
    for x in range(PX):
        q = fplane(f, HY, x) - 0.5 * fz(fplane(f, EX, x))
        put(q1, x, q)
        e = plane(eps, x)
        hx = fplane(f, HX, x)
        ce = 32.0 / e
        rr = fplane(f, EZ, x) + ce * ((q - before) - (hx - y_prev(hx, hxlo[x : x + 1])))
        before = q
        r[pl.ds(x * XR, PY), :] = rr
        r[pl.ds(x * XR + PY, 8), :] = jnp.concatenate([rlo[x : x + 1], rhi[x : x + 1], pad], 0)
        m[pl.ds(x * XR, PY), :] = e * (1.0 / 1024.0)
        m[pl.ds(x * XR + PY, 8), :] = (
            jnp.concatenate([epslo[x : x + 1], epshi[x : x + 1], one], 0) * (1.0 / 1024.0)
        )
    m_at = lambda i: plane(m, i, XR)
    hn, bn, a, bb, c = factor(m_at, PX, gx == 0, h, b, XR)
    last, vn = sweep(m_at, lambda i: plane(r, i, XR), PX, v, XR)
    pf, plast = ends(last, vn, hn, c)
    put(hb, 0, hn, XR)
    put(hb, 1, bn, XR)
    put(hb, 2, c, XR)
    put(hb, 3, vn, XR)
    qq = jnp.concatenate([q1lo[PX - 1 :], q1hi[PX - 1 :]], 0) * (-1.0 / 32.0)
    spread(msg, lax.axis_size("gb"), packed((pf, plast, a, bb, c), XL, (qq,), XB))


def k_y1(f, eps, xl, xr, msg, p1, ey1, m, h, b, v, hb, r, ep):
    gx = x_index()
    gy = y_index()
    n = y_size()
    xlo = gx > 0
    xin = jnp.where(xlo, 1.0, 0.0)
    xon = jnp.where(gx < x_size() - 1, 1.0, 0.0)
    zero = jnp.zeros((1, PZ), F32)
    zeros = jnp.zeros((PY, PZ), F32)
    exl, eyl, hyl, hzl = [xin * plane(xl, i) for i in range(4)]
    eyr, ezr, hxr, hzr = [xon * plane(xr, i) for i in range(4)]
    for x in range(PX):
        put(ep, x, plane(eps, x))
    put(ep, PX, plane(xl, 4))
    put(ep, PX + 1, plane(xr, 4))
    for x in range(PX + 2, YR):
        put(ep, x, zeros + 1.0)
        put(r, x, zeros)
    put(r, PX + 1, zeros)

    def rex(ex, hy, pp, e):
        ie = 1.0 / e
        return ex + (32.0 * ie) * (pp - y_prev(pp, zero)) - (0.5 * ie) * bz(hy)

    p = hzl - 32.0 * (fplane(f, EY, 0) - eyl)
    p = jnp.where(xlo, p, 0.0)
    put(p1, PX, p)
    put(r, PX, rex(exl, hyl, p, plane(ep, PX)))
    for x in range(PX):
        ey = fplane(f, EY, x)
        nxt = fplane(f, EY, x + 1) if x < PX - 1 else eyr
        hz = fplane(f, HZ, x)
        hzp = fplane(f, HZ, x - 1) if x > 0 else hzl
        e = plane(ep, x)
        p = hz - 32.0 * (nxt - ey)
        put(p1, x, p)
        put(r, x, rex(fplane(f, EX, x), fplane(f, HY, x), p, e))
        ie = 1.0 / e
        put(ey1, x, ey + (0.5 * ie) * bz(fplane(f, HX, x)) - (32.0 * ie) * (hz - hzp))
    ie = 1.0 / plane(ep, PX + 1)
    put(ey1, PX, eyr + (0.5 * ie) * bz(hxr) - (32.0 * ie) * (hzr - fplane(f, HZ, PX - 1)))

    def rows(ref, j):
        return ref[pl.ds(j, YR, stride=PY), :]

    for j in range(PY):
        put(m, j, rows(ep, j) * (1.0 / 1024.0), YR)
    m_at = lambda j: plane(m, j, YR)
    hn, bn, a, bb, c = factor(m_at, PY, gy == 0, h, b, YR)
    last, vn = sweep(m_at, lambda j: rows(r, j), PY, v, YR)
    pf, plast = ends(last, vn, hn, c)
    put(hb, 0, hn, YR)
    put(hb, 1, bn, YR)
    put(hb, 2, c, YR)
    put(hb, 3, vn, YR)
    lastrow = lambda ref, at, k: ref[pl.ds(at * PY + PY - 1, k, stride=PY), :]
    tail = jnp.zeros((7, PZ), F32)
    qq = jnp.concatenate([lastrow(p1, 0, PX), lastrow(p1, PX, 1), tail], 0) * (-1.0 / 32.0)
    tail = jnp.zeros((6, PZ), F32)
    ee = fz(jnp.concatenate([lastrow(ey1, 0, PX), zero, lastrow(ey1, PX, 1), tail], 0))
    spread(msg, 1, packed((pf, plast, a, bb, c, qq, ee), YL, (), YB))


def coefficients(part, n, rows, tp, bp, ts, bs, bet, dele):
    zero = jnp.zeros((rows, PZ), F32)
    beta = zero
    put(bet, 0, zero, rows)
    for j in range(n):
        a, b, c = part(j, 2), part(j, 3), part(j, 4)
        bd = b / (1.0 - a * beta)
        t = bd * beta
        put(tp, j, t, rows)
        put(bp, j, bd, rows)
        beta = c + t * b
        put(bet, j + 1, beta, rows)
    delta = zero
    put(dele, n, zero, rows)
    for j in range(n - 1, -1, -1):
        a, b, c = part(j, 2), part(j, 3), part(j, 4)
        bd = b / (1.0 - c * delta)
        t = bd * delta
        put(ts, j, t, rows)
        put(bs, j, bd, rows)
        delta = a + t * b
        put(dele, j, delta, rows)


def chain(part, n, rows, crows, tp, bp, ts, bs, al, ga, start, stop):
    take = lambda ref, j: ref[pl.ds(j * crows, rows), :]
    alpha, gamma = start, stop
    put(al, 0, alpha, rows)
    put(ga, n, gamma, rows)
    for j in range(n):
        k = n - 1 - j
        alpha = part(j, 1) + take(tp, j) * part(j, 0) + take(bp, j) * alpha
        gamma = part(k, 0) + take(ts, k) * part(k, 1) + take(bs, k) * gamma
        put(al, j + 1, alpha, rows)
        put(ga, k, gamma, rows)
    return gamma, alpha


def interface(part, n, me, rows, coefs, al, ga, start=None, stop=None, crows=None):
    crows = crows or rows
    tp, bp, ts, bs, bet, dele = coefs
    zero = jnp.zeros((rows, PZ), F32)
    start = zero if start is None else start
    stop = zero if stop is None else stop
    chain(part, n, rows, crows, tp, bp, ts, bs, al, ga, start, stop)
    at = lambda ref, d, size: ref[pl.ds(pl.multiple_of(d * size, 8), rows), :]
    a0, a1 = at(al, me, rows), at(al, me + 1, rows)
    g0, g1 = at(ga, me, rows), at(ga, me + 1, rows)
    b0, b1 = at(bet, me, crows), at(bet, me + 1, crows)
    d0, d1 = at(dele, me, crows), at(dele, me + 1, crows)
    left = a0 + b0 * ((g0 + d0 * a0) / (1.0 - d0 * b0))
    right = g1 + d1 * ((a1 + b1 * g1) / (1.0 - b1 * d1))
    return left, right


def x_raw(msg):
    return lambda j, k: msg[pl.ds(j * XB + k * XL, XR), :]


def x_late(msg, at):
    return pltpu.roll(msg[pl.ds(at + XB - 8, 8), :], 6, 0)


def x_part(msg):
    def part(j, k):
        if j == 0:
            return x_raw(msg)(j, k)
        own = msg[pl.ds(j * XB + k * XL, PY), :]
        more = (
            msg[pl.ds(j * XB + k * XL + PY, 8), :]
            + msg[pl.ds(j * XB + (2 + k) * XL + PY, 8), :] * x_late(msg, (j - 1) * XB)
        )
        return jnp.concatenate([own, more], 0)

    return part


def x_passed(msg, me):
    prev = pl.multiple_of(jnp.maximum(me - 1, 0) * XB, 8)
    return jnp.where(me > 0, x_late(msg, prev), 0.0)


def y_raw(msg):
    return lambda j, k: msg[pl.ds(j * YB + k * YL, YR), :]


def y_part(msg):
    raw = y_raw(msg)
    return lambda j, k: raw(j, k) + raw(j, 2 + k) * raw(j - 1, 5) if j else raw(j, k)


def y_passed(msg, me, k):
    skip = k * YL % 8
    prev = pl.multiple_of(jnp.maximum(me - 1, 0) * YB + k * YL - skip, 8)
    return jnp.where(me > 0, pltpu.roll(msg[pl.ds(prev, YR), :], YR - skip, 0), 0.0)


def k_y2(gi, go, p1, h, b, v, hb, ex1, p2, elo, *more):
    coi, coo, (al, ga, dex) = more[:6], more[6:12], more[12:]
    nz, nc = lax.axis_size("gz"), lax.axis_size("gc")
    iz, ic = lax.axis_index("gz"), lax.axis_index("gc")
    coefficients(y_raw(go), nz, YR, *coo)
    coefficients(y_raw(gi), nc, YR, *coi)
    left, right = interface(y_part(go), nz, iz, YR, coo, al, ga)
    left = left + y_passed(go, iz, 5)
    left, right = interface(y_part(gi), nc, ic, YR, coi, al, ga, left, right)
    left = left + y_passed(gi, ic, 5)
    elo[...] = jnp.where(ic > 0, y_passed(gi, ic, 6), y_passed(go, iz, 6))
    lw = left * plane(hb, 1, YR)
    rw = (right - plane(hb, 3, YR)) * plane(hb, 0, YR)
    later = right
    for j in range(PY - 1, -1, -1):
        w = plane(v, j, YR) + plane(b, j, YR) * lw + plane(h, j, YR) * rw
        ex1[pl.ds(j, YR, stride=PY), :] = w
        dex[pl.ds(j, YR, stride=PY), :] = later - w
        later = w
    live = jnp.where(x_index() > 0, 1.0, 0.0)
    for x in range(PX):
        put(p2, x, plane(p1, x) + 64.0 * plane(dex, x))
    put(p2, PX, live * (plane(p1, PX) + 64.0 * plane(dex, PX)))


def join(part, raw, count):
    pf, ph, a, b, c = part(0, 0), part(0, 1), raw(0, 2), raw(0, 3), raw(0, 4)
    for j in range(1, count):
        qf, qh, a2, b2, c2 = part(j, 0), part(j, 1), raw(j, 2), raw(j, 3), raw(j, 4)
        den = 1.0 / (1.0 - c * a2)
        low, high = b * den, b2 * den
        pf, ph = pf + low * (qf + a2 * ph), qh + high * (ph + c * qf)
        a, b, c = a + low * b * a2, low * b2, c2 + high * b2 * c
    return pf, ph, a, b, c


def k_join_y(gi, msg):
    nc = lax.axis_size("gc")
    raw = y_raw(gi)
    values = join(y_part(gi), raw, nc)
    more = gi[pl.ds((nc - 1) * YB + 5 * YL, 2 * YL), :]
    spread(msg, 1, packed(values, YL, (more,), YB))


def k_join_x(gi, msg, inner):
    inner[...] = gi[...]
    nb = lax.axis_size("gb")
    last = x_late(gi, (nb - 1) * XB)[:2]
    spread(msg, lax.axis_size("ga"), packed(join(x_part(gi), x_raw(gi), nb), XL, (last,), XB))


def shares(pf, ph, coefs, count, me, rows, crows):
    tp, bp, ts, bs = coefs[:4]
    low = high = jnp.ones((rows, PZ), F32)
    for k in range(count):
        low = jnp.where(k < me, low * bs[pl.ds(k * crows, rows), :], low)
        high = jnp.where(k > me, high * bp[pl.ds(k * crows, rows), :], high)
    mine = pl.ds(pl.multiple_of(me * crows, 8), rows)
    return low * (pf + ts[mine, :] * ph), high * (ph + tp[mine, :] * pf)


def gathered(msg, n, m, ia, ib, rows, crows, coi, coo, al, ga):
    zero = jnp.zeros((rows, PZ), F32)

    def inside(j, k):
        at = pl.multiple_of(((ia * m + j) * 2 + k) * rows, 8)
        return msg[pl.ds(at, rows), :]

    whole = chain(inside, m, rows, crows, *coi[:4], al, ga, zero, zero)

    def group(j, k):
        total = sum(msg[pl.ds(((j * m + i) * 2 + k) * rows, rows), :] for i in range(m))
        return jnp.where(ia == j, whole[k], total)

    left, right = interface(group, n, ia, rows, coo, al, ga, crows=crows)
    return interface(inside, m, ib, rows, coi, al, ga, left, right, crows)


def k_x2(gi, go, f, q1, ey1, p2, h, b, v, m, hb, ez1, hx1, msg2, v2, vn2, *more):
    coi, coo, (al, ga, r) = more[:6], more[6:12], more[12:]
    na, nb = lax.axis_size("ga"), lax.axis_size("gb")
    ia, ib = lax.axis_index("ga"), lax.axis_index("gb")
    gy = y_index()
    yon = jnp.where(gy < y_size() - 1, 1.0, 0.0)
    coefficients(x_raw(go), na, XR, *coo)
    coefficients(x_raw(gi), nb, XR, *coi)
    left, right = interface(x_part(go), na, ia, XR, coo, al, ga)
    left = jnp.concatenate([left[:PY], left[PY:] + x_passed(go, ia)], 0)
    left, right = interface(x_part(gi), nb, ib, XR, coi, al, ga, left, right)
    left = jnp.concatenate([left[:PY], left[PY:] + x_passed(gi, ib)], 0)
    lw = left * plane(hb, 1, XR)
    rw = (right - plane(hb, 3, XR)) * plane(hb, 0, XR)
    for x in range(PX):
        put(ez1, x, plane(v, x, XR) + plane(b, x, XR) * lw + plane(h, x, XR) * rw, XR)
    put(ez1, PX, right, XR)
    before = plane(p2, PX)
    for x in range(PX):
        z = ez1[pl.ds(x * XR, PY), :]
        z32 = yon * ez1[pl.ds(x * XR + PY + 1, 1), :]
        ey = plane(ey1, x)
        t = fplane(f, HX, x) - 32.0 * (y_next(z, z32) - z) + 0.5 * fz(ey)
        put(hx1, x, t)
        p = plane(p2, x)
        ie = 1.0 / (m[pl.ds(x * XR, PY), :] * 1024.0)
        put(r, x, ey + (0.5 * ie) * bz(t) - (32.0 * ie) * (p - before))
        before = p
    last, vn = sweep(lambda i: m[pl.ds(i * XR, PY), :], lambda i: plane(r, i), PX, v2, PY)
    vn2[...] = vn
    pf, plast = ends(last, vn, hb[pl.ds(0, PY), :], hb[pl.ds(2 * XR, PY), :])
    share = shares(pf, plast, coi, nb, ib, PY, XR)
    for k in range(na * nb):
        for i, (own, joined) in enumerate(zip((pf, plast), share)):
            put(msg2, 2 * k + i, jnp.where(ia == k // nb, own, joined))


def k_y3(f, xr, q1, mx, ey1, ez1, hx1, ex1, elo, ex2, hy1, q2, r):
    n = y_size()
    gy = y_index()
    yon = jnp.where(gy < n - 1, 1.0, 0.0)
    yin = jnp.where(gy > 0, 1.0, 0.0)
    zeros = jnp.zeros((PY, PZ), F32)
    for x in range(PX + 2, YR):
        put(r, x, zeros)
    put(r, PX, zeros)
    for x in range(PX + 1):
        at = x * XR
        z = ez1[pl.ds(at, PY), :]
        zlo = ez1[pl.ds(at + PY, 1), :]
        zhi = yon * ez1[pl.ds(at + PY + 1, 1), :]
        fe = fz(plane(ey1, x))
        d = 32.0 * (y_next(z, zhi) - z) - fe
        k = x if x < PX else PX + 1
        dlo = yin * (32.0 * (z[:1] - zlo) - elo[pl.ds(k, 1), :])
        ez = fplane(f, EZ, x) if x < PX else plane(xr, 1)
        e = mx[pl.ds(at, PY), :] * 1024.0 if x < PX else plane(xr, 4)
        ie = 1.0 / e
        put(r, k, 2.0 * z - ez + (32.0 * ie) * (d - y_prev(d, dlo)))
        if x < PX:
            t = plane(q1, x) + 32.0 * (ez1[pl.ds(at + XR, PY), :] - z)
            put(hy1, x, t)
            put(ex2, x, 2.0 * plane(ex1, x) - fplane(f, EX, x) + (0.5 * ie) * bz(fplane(f, HY, x) - t))
            put(q2, x, plane(hx1, x) + 0.5 * fe)


def k_y3_sweep(r, m, hb, msg2, v2, vn2):
    m_at = lambda j: plane(m, j, YR)
    last, vn = sweep(m_at, lambda j: r[pl.ds(j, YR, stride=PY), :], PY, v2, YR)
    vn2[...] = vn
    pf, plast = ends(last, vn, plane(hb, 0, YR), plane(hb, 2, YR))
    spread(msg2, 1, (pf, plast))


def y_ends(msg):
    return lambda j, k: msg[pl.ds((2 * j + k) * YR, YR), :]


def k_join_ends(gi, tp, bp, ts, bs, msg, al, ga):
    nc = lax.axis_size("gc")
    zero = jnp.zeros((YR, PZ), F32)
    spread(msg, 1, chain(y_ends(gi), nc, YR, YR, tp, bp, ts, bs, al, ga, zero, zero))


def k_y4(gi, go, h, b, v2, vn2, hb, *more):
    coi, coo, (ex2, hy1, q2, out, al, ga, w2, dw) = more[:6], more[6:12], more[12:]
    nz, nc = lax.axis_size("gz"), lax.axis_size("gc")
    iz, ic = lax.axis_index("gz"), lax.axis_index("gc")
    left, right = interface(y_ends(go), nz, iz, YR, coo, al, ga)
    left, right = interface(y_ends(gi), nc, ic, YR, coi, al, ga, left, right)
    lw = left * plane(hb, 1, YR)
    rw = (right - vn2[...]) * plane(hb, 0, YR)
    later = right
    for j in range(PY - 1, -1, -1):
        w = plane(v2, j, YR) + plane(b, j, YR) * lw + plane(h, j, YR) * rw
        w2[pl.ds(j, YR, stride=PY), :] = w
        dw[pl.ds(j, YR, stride=PY), :] = later - w
        later = w
    xon = jnp.where(x_index() < x_size() - 1, 1.0, 0.0)
    for x in range(PX):
        w = plane(w2, x)
        nxt = plane(w2, x + 1) if x < PX - 1 else xon * plane(w2, PX + 1)
        e2 = plane(ex2, x)
        put(out, EX * PX + x, e2)
        put(out, EZ * PX + x, w)
        put(out, HX * PX + x, plane(q2, x) - 32.0 * plane(dw, x))
        put(out, HY * PX + x, plane(hy1, x) - 0.5 * fz(e2) + 32.0 * (nxt - w))


def k_x4(msg, h, b, v2, vn2, hb, *more):
    coi, coo, (p2, out, al, ga) = more[:6], more[6:12], more[12:]
    na, nb = lax.axis_size("ga"), lax.axis_size("gb")
    ia, ib = lax.axis_index("ga"), lax.axis_index("gb")
    left, right = gathered(msg, na, nb, ia, ib, PY, XR, coi, coo, al, ga)
    lw = left * hb[pl.ds(XR, PY), :]
    rw = (right - vn2[...]) * hb[pl.ds(0, PY), :]
    later = right
    for x in range(PX - 1, -1, -1):
        w = plane(v2, x) + b[pl.ds(x * XR, PY), :] * lw + h[pl.ds(x * XR, PY), :] * rw
        put(out, EY * PX + x, w)
        put(out, HZ * PX + x, plane(p2, x) - 32.0 * (later - w))
        later = w


def call(name, parts, args, outs, scratch=(), smem=(), into=(), flush=(), near=(), only=(), views=()):
    into, flush, scratch, only = dict(into), dict(flush), dict(scratch), dict(only)
    views = dict(views)
    touched = [list(used) + [views[k][0] for k in used if k in views] for _, used in parts]
    moved = [k for k in args if k not in smem and (k not in near or k in into)]
    pieces = {k for group in flush.values() for k, _, _ in group}
    last = {k: max(i for i, used in enumerate(touched) if k in used) for k in outs}
    leave = [
        [(k, 0, outs[k]) for k in outs if last[k] == i and k not in pieces and k not in near]
        + list(flush.get(i, ()))
        for i in range(len(parts))
    ]
    own = [k for k in moved if k not in into]

    def body(*refs):
        take = iter(refs)
        hbm = {k: next(take) for k in args}
        results = {k: next(take) for k in outs}
        env = {k: next(take) for k in own}
        env.update({k: results[k] if k in near else next(take) for k in outs})
        env.update({k: next(take) for k in scratch})
        env.update({k: hbm[k] for k in args if k not in moved})
        env.update({k: env[b].at[pl.ds(at, rows), :] for k, (b, at, rows) in views.items()})
        sem_in, sem_out = next(take), next(take)
        pending = {}
        count = 0
        for k in moved:
            pairs = [(hbm[k], env.get(k))]
            if k in into:
                buffer, row = into[k]
                pairs = [(hbm[k], env[buffer].at[pl.ds(row(), args[k].shape[0]), :])]
            elif k in only:
                windows = [pl.ds(at, rows) for at, rows in only[k]]
                pairs = [(hbm[k].at[w, :], env[k].at[w, :]) for w in windows]
            for source, where in pairs:
                copy = pltpu.make_async_copy(source, where, sem_in.at[count])
                copy.start()
                count += 1
                pending.setdefault(into[k][0] if k in into else k, []).append(copy)
        sent = []
        for i, (function, used) in enumerate(parts):
            for k in touched[i]:
                for copy in pending.pop(k, ()):
                    copy.wait()
            function(*[env[k] for k in used])
            for k, row, rows in leave[i]:
                window = pl.ds(row, rows)
                copy = pltpu.make_async_copy(
                    env[k].at[window, :], results[k].at[window, :], sem_out.at[len(sent)]
                )
                copy.start()
                sent.append(copy)
        for copy in sent:
            copy.wait()

    far, close, scalars = [
        pl.BlockSpec(memory_space=m) for m in (pltpu.HBM, pltpu.VMEM, pltpu.SMEM)
    ]
    got = pl.pallas_call(
        body,
        out_shape=[(pltpu.VMEM if k in near else pltpu.HBM)((c, PZ), F32) for k, c in outs.items()],
        in_specs=[scalars if k in smem else close if k in near else far for k in args],
        out_specs=[close if k in near else far for k in outs],
        scratch_shapes=[pltpu.VMEM(args[k].shape, args[k].dtype) for k in own]
        + [pltpu.VMEM((c, PZ), F32) for k, c in outs.items() if k not in near]
        + [pltpu.VMEM((c, PZ), F32) for c in scratch.values()]
        + [
            pltpu.SemaphoreType.DMA((sum(len(only.get(k, (0,))) for k in moved),)),
            pltpu.SemaphoreType.DMA((max(1, sum(len(group) for group in leave)),)),
        ],
        compiler_params=pltpu.CompilerParams(vmem_limit_bytes=LIMIT * 1024 * 1024),
        cost_estimate=pl.CostEstimate(flops=1000, bytes_accessed=1000, transcendentals=0),
        name=name,
    )(*[a if k in smem else pltpu.with_memory_space_constraint(a, pltpu.VMEM if k in near else pltpu.HBM) for k, a in args.items()])
    return dict(zip(outs, got))


def stacked(buffer, names, rows):
    return {k: (buffer, sum(rows[:i]), rows[i]) for i, k in enumerate(names)}


def ring(block, axis, step):
    n = lax.axis_size(axis)
    return lax.ppermute(block, axis, [(i, (i + step) % n) for i in range(n)])


def swap(msg, axis):
    n = lax.axis_size(axis)
    got = lax.all_to_all(msg.reshape(n, -1, PZ), axis, 0, 0, tiled=True)
    return got.reshape(-1, PZ)


def from_all(msg, axis, buffer):
    n = lax.axis_size(axis)
    rows = msg.shape[0]
    args, into = {}, {}
    for step in range(n):
        k = buffer + str(step)
        args[k] = ring(msg, axis, step) if step else msg

        def row(step=step):
            return pl.multiple_of(lax.rem(lax.axis_index(axis) - step + n, n) * rows, 8)

        into[k] = (buffer, row)
    return args, into


def local(fields, region, eps_table):
    na, nb = lax.axis_size("ga"), lax.axis_size("gb")
    along_x, along_y = ("ga", "gb"), ("gz", "gc")
    nz, nc = lax.axis_size("gz"), lax.axis_size("gc")
    ny = nz * nc
    ey = (max(nz, nc) + 1) * YR
    cells = PX * PY
    nxl, nyl = PX * XR, PY * YR
    f = fields.reshape(6 * cells, PZ)
    reg = region.reshape(cells, PZ)
    xup, xdn, yup, ydn = edges(fields, region, eps_table)
    xl = ring(xup, along_x, 1)
    xr = ring(xdn, along_x, -1)
    yl = ring(yup, along_y, 1)
    yr = ring(ydn, along_y, -1)
    linex = ("mx", "hx", "bx", "vx", "hbx")
    liney = ("my", "hy", "by", "vy", "hby")
    lines_x, lines_y = 4 * nxl + 4 * XR, 4 * nyl + 4 * YR
    lines = {
        **stacked("lx", ("mx", "vx", "hx", "bx", "hbx"), (nxl,) * 4 + (4 * XR,)),
        **stacked("ly", ("my", "vy", "hy", "by", "hby"), (nyl,) * 4 + (4 * YR,)),
    }
    of = lambda names: {k: lines[k] for k in names}
    pre = call(
        "eps",
        [(k_eps, ("reg", "table", "eps"))],
        dict(reg=reg, table=eps_table),
        dict(eps=cells),
        smem=("table",),
    )
    one = call(
        "onex",
        [
            (k_x1, ("f", "eps", "xl", "xr", "yl", "yr", "msgx", "q1") + linex + ("r",)),
        ],
        dict(xl=xl, xr=xr, yl=yl, yr=yr, eps=pre["eps"], f=f),
        dict(q1=cells, lx=lines_x, msgx=nb * XB),
        dict(r=nxl),
        near=("xl", "xr", "yl", "yr") + NEAR,
        views=of(linex),
        only=dict(f=[(EX * cells, cells), (EZ * cells, 3 * cells)]),
    )
    oney = call(
        "oney",
        [(k_y1, ("f", "eps", "xl", "xr", "msgy", "p1", "ey1") + liney + ("rt", "ep"))],
        dict(f=f, eps=pre["eps"], xl=xl, xr=xr),
        dict(msgy=YB, p1=cells + PY, ey1=cells + PY, ly=lines_y),
        dict(rt=YR * PY, ep=YR * PY),
        near=("msgy",),
        views=of(liney),
        only=dict(f=[(EX * cells, 2 * cells), (HX * cells, 3 * cells)]),
    )
    one.update(oney)
    pair, into = from_all(one["msgy"], "gc", "gyi")
    group = call(
        "group",
        [
            (k_join_y, ("gyi", "msgyo")),
            (k_join_x, ("gi", "msgo", "inner")),
        ],
        dict(pair, gi=swap(one["msgx"], "gb")),
        dict(msgyo=YB, msgo=na * XB, inner=nb * XB),
        dict(gyi=nc * YB),
        into=into,
        near=("gi", "msgyo") + NEAR + tuple(pair),
    )
    goto = swap(group["msgo"], "ga")
    argy, into_o = from_all(group["msgyo"], "gz", "gyo")
    argy.update(pair)
    into.update(into_o)
    chains = ("tp", "bp", "ts", "bs", "bet", "del")
    ci, co, cyi, cyo = [tuple(k + a for k in chains) for a in ("i", "o", "yi", "yo")]
    cx, cy = ci + co, cyi + cyo
    size = lambda n, rows: (n * rows,) * 4 + ((n + 1) * rows,) * 2
    keep = {k: one[k] for k in ("q1", "p1", "ey1", "lx", "ly")}
    rows_y, rows_x = size(nc, YR) + size(nz, YR), size(nb, XR) + size(na, XR)
    views = {**stacked("cy", cy, rows_y), **stacked("cx", cx, rows_x)}
    two = call(
        "two",
        [
            (k_y2, ("gyi", "gyo", "p1", "hy", "by", "vy", "hby", "ex1", "p2", "elo") + cy + ("aly", "gay", "dex")),
            (
                k_x2,
                ("gi", "go", "f", "q1", "ey1", "p2", "hx", "bx", "vx", "mx", "hbx")
                + ("ez1", "hx1", "msgx2", "vx2", "vnx2")
                + cx
                + ("alx", "gax", "r"),
            ),
            (
                k_y3,
                ("f", "xr", "q1", "mx", "ey1", "ez1", "hx1", "ex1", "elo", "ex2", "hy1", "q2", "rt"),
            ),
            (k_y3_sweep, ("rt", "my", "hby", "msgy2", "vy2", "vny2")),
        ],
        dict(argy, **{k: keep[k] for k in ("ly", "p1")}, gi=group["inner"], go=goto, f=f, xr=xr, **{k: keep[k] for k in ("lx", "ey1", "q1")}),
        dict(
            zip(
                ("p2", "cy", "msgx2", "vx2", "vnx2", "cx", "msgy2", "vy2", "vny2", "ex2", "hy1", "q2"),
                (cells + PY, sum(rows_y), na * nb * 2 * PY, cells, PY, sum(rows_x))
                + (2 * YR, nyl, YR, cells, cells, cells),
            )
        ),
        dict(
            gyi=nc * YB, gyo=nz * YB, ex1=YR * PY, elo=YR, aly=ey, gay=ey, dex=YR * PY,
            ez1=nxl + XR, hx1=cells, alx=(max(na, nb) + 1) * XR, gax=(max(na, nb) + 1) * XR, r=cells, rt=YR * PY,
        ),
        into=into,
        near=("go", "msgy2", "party2") + NEAR + tuple(k for k in argy if k not in pair),
        flush={0: [("p2", 0, cells + PY), ("cy", 0, sum(rows_y))]},
        views={**views, **lines},
        only=dict(f=[(EX * cells, cells), (EZ * cells, 3 * cells)]),
    )
    gotx = swap(two["msgx2"], along_x)
    pair, into = from_all(two["msgy2"], "gc", "gyi")
    group = call(
        "ends",
        [(k_join_ends, ("gyi",) + cyi[:4] + ("msg", "aly", "gay"))],
        dict(pair, cy=two["cy"]),
        dict(msg=2 * YR),
        dict(gyi=nc * 2 * YR, aly=ey, gay=ey),
        into=into,
        near=tuple(pair) + ("msg",),
        views={k: views[k] for k in cyi[:4]},
        only=dict(cy=[(0, sum(rows_y[:4]))]),
    )
    argy, into_o = from_all(group["msg"], "gz", "gyo")
    argy.update(pair)
    into.update(into_o)
    order = ("cy", "ly", "vny2", "vy2", "ex2", "q2", "hy1", "cx", "lx", "vnx2", "vx2", "p2")
    need = {k: two.get(k, one.get(k)) for k in order}
    three = call(
        "three",
        [
            (
                k_y4,
                ("gyi", "gyo", "hy", "by", "vy2", "vny2", "hby") + cy + ("ex2", "hy1", "q2", "out")
                + ("aly", "gay", "w2", "dw"),
            ),
            (k_x4, ("gx", "hx", "bx", "vx2", "vnx2", "hbx") + cx + ("p2", "out", "alx", "gax")),
        ],
        dict(argy, gx=gotx, **need),
        dict(out=6 * cells),
        dict(
            gyi=nc * 2 * YR, gyo=nz * 2 * YR, aly=ey, gay=ey, w2=YR * PY, dw=YR * PY,
            alx=(max(na, nb) + 1) * PY, gax=(max(na, nb) + 1) * PY,
        ),
        into=into,
        near=("gx",) + tuple(argy),
        views={**views, **of(("hx", "bx", "hbx", "hy", "by", "hby"))},
        only=dict(lx=[(2 * nxl, lines_x - 2 * nxl)], ly=[(2 * nyl, lines_y - 2 * nyl)]),
        flush={
            0: [("out", EX * cells, cells), ("out", EZ * cells, 3 * cells)],
            1: [("out", EY * cells, cells), ("out", HZ * cells, cells)],
        },
    )
    return three["out"].reshape(6, PX, PY, PZ)


def solution(mesh):
    nx, ny = mesh.devices.shape
    nb = max(d for d in range(1, nx + 1) if nx % d == 0 and d * d <= nx)
    shape = (nx // nb, nb, ny // 2, 2)
    grid = Mesh(mesh.devices.reshape(shape), ("ga", "gb", "gz", "gc"))
    columns = P(("ga", "gb"), ("gz", "gc"), None)
    return jax.shard_map(
        local,
        mesh=grid,
        in_specs=(P(None, *columns), columns, P()),
        out_specs=P(None, *columns),
        check_vma=False,
    )
```

```python
import functools

import jax
import jax.numpy as jnp
from jax import lax
from jax.experimental import pallas as pl
from jax.experimental.pallas import tpu as pltpu
from jax.sharding import Mesh
from jax.sharding import PartitionSpec as P

PX, PY, PZ = 16, 32, 128
XL, YL = PY + 2, PX + 2
XR = 40
YR = 24
F32 = jnp.float32
LIMIT = 30
NEAR = ()
EX, EY, EZ, HX, HY, HZ = range(6)
XB, YB = 5 * XL + 6, 7 * YL + 2


def x_index():
    return lax.axis_index("ga") * lax.axis_size("gb") + lax.axis_index("gb")


def y_index():
    return lax.axis_index("gz") * lax.axis_size("gc") + lax.axis_index("gc")


def y_size():
    return lax.axis_size("gz") * lax.axis_size("gc")


def x_size():
    return lax.axis_size("ga") * lax.axis_size("gb")


def sub():
    return lax.broadcasted_iota(jnp.int32, (PY, PZ), 0)


def lanes_of(v):
    return lax.broadcasted_iota(jnp.int32, v.shape, 1)


def z_next(v):
    return jnp.where(lanes_of(v) == PZ - 1, 0.0, pltpu.roll(v, PZ - 1, 1))


def z_prev(v):
    return jnp.where(lanes_of(v) == 0, 0.0, pltpu.roll(v, 1, 1))


def fz(v):
    return z_next(v) - v


def bz(v):
    return v - z_prev(v)


def y_prev(v, row):
    return jnp.where(sub() == 0, row, pltpu.roll(v, 1, 0))


def y_next(v, row):
    return jnp.where(sub() == PY - 1, row, pltpu.roll(v, PY - 1, 0))


def plane(ref, k, size=PY):
    return ref[pl.ds(k * size, size), :]


def put(ref, k, v, size=PY):
    ref[pl.ds(k * size, size), :] = v


def fplane(ref, f, x):
    return plane(ref, f * PX + x)


def lookup(region, table):
    level = [table[i] for i in range(16)]
    for bit in range(4):
        on = (region & (1 << bit)) != 0
        level = [jnp.where(on, level[2 * i + 1], level[2 * i]) for i in range(len(level) // 2)]
    return level[0]


def packed(values, lines, more, rows):
    parts = [v[:lines] for v in values] + list(more)
    pad = rows - sum(v.shape[0] for v in parts)
    return (jnp.concatenate(parts + [jnp.zeros((pad, PZ), F32)], 0),)


def k_eps(reg, table, eps):
    tab = [table[i] for i in range(16)]
    for x in range(PX):
        put(eps, x, lookup(plane(reg, x), tab))


def k_q1(f, q1):
    for x in range(PX):
        put(q1, x, fplane(f, HY, x) - 0.5 * fz(fplane(f, EX, x)))


def k_edges(f, reg, table, xup, xdn, yup, ydn, tab, ends, low, high, rlow, rhigh, sems):
    up, down = (EX, EY, HY, HZ), (EY, EZ, HX, HZ)
    rows = (EX, HY, EZ, HX)
    top = pl.ds(PY - 8, 8)
    pairs = [(table, tab), (reg.at[PX - 1], ends.at[0]), (reg.at[0], ends.at[1])]
    pairs += [(reg.at[:, top, :], rhigh), (reg.at[:, pl.ds(0, 8), :], rlow)]
    for i in range(4):
        pairs += [
            (f.at[up[i], PX - 1], xup.at[pl.ds(i * PY, PY), :]),
            (f.at[down[i], 0], xdn.at[pl.ds(i * PY, PY), :]),
            (f.at[rows[i], :, top, :], high.at[i]),
            (f.at[rows[i], :, pl.ds(0, 8), :], low.at[i]),
        ]
    copies = [pltpu.make_async_copy(p, q, sems.at[i]) for i, (p, q) in enumerate(pairs)]
    for copy in copies:
        copy.start()
    for copy in copies:
        copy.wait()
    t = [tab[i] for i in range(16)]
    put(xup, 4, lookup(ends[0], t))
    put(xdn, 4, lookup(ends[1], t))
    for i in range(4):
        put(yup, i, high[i, :, 7, :], PX)
        put(ydn, i, low[i, :, 0, :], PX)
    put(yup, 4, high[3, :, 6, :], PX)
    put(yup, 5, lookup(rhigh[:, 7, :], t), PX)
    put(ydn, 4, lookup(rlow[:, 0, :], t), PX)


def edges(fields, region, eps_table):
    vmem, hbm = [pl.BlockSpec(memory_space=m) for m in (pltpu.VMEM, pltpu.HBM)]
    return pl.pallas_call(
        k_edges,
        out_shape=[pltpu.VMEM((c, PZ), F32) for c in (5 * PY, 5 * PY, 6 * PX, 6 * PX)],
        in_specs=[hbm] * 3,
        out_specs=[vmem] * 4,
        scratch_shapes=[
            pltpu.SMEM((16,), F32),
            pltpu.VMEM((2, PY, PZ), jnp.int32),
            pltpu.VMEM((4, PX, 8, PZ), F32),
            pltpu.VMEM((4, PX, 8, PZ), F32),
            pltpu.VMEM((PX, 8, PZ), jnp.int32),
            pltpu.VMEM((PX, 8, PZ), jnp.int32),
            pltpu.SemaphoreType.DMA((21,)),
        ],
        cost_estimate=pl.CostEstimate(flops=1000, bytes_accessed=1000, transcendentals=0),
        name="edges",
    )(*[pltpu.with_memory_space_constraint(v, pltpu.HBM) for v in (fields, region, eps_table)])


def factor(m_at, count, first, h, b, rows):
    hv = jnp.ones((rows, PZ), F32)
    hs = jnp.where(first, jnp.zeros_like(hv), jnp.ones_like(hv))
    bv = jnp.ones((rows, PZ), F32)
    bs = jnp.ones((rows, PZ), F32)
    for i in range(count):
        k = count - 1 - i
        put(h, i, hv, rows)
        put(b, k, bv, rows)
        hs = hs + m_at(i) * hv
        bs = bs + m_at(k) * bv
        hlast, blast = hv, bv
        hv = hv + hs
        bv = bv + bs
    hn = 1.0 / hv
    bn = 1.0 / bv
    return hn, bn, blast * bn, hn, hlast * hn


def sweep(m_at, r_at, count, v, rows):
    vv = jnp.zeros((rows, PZ), F32)
    vs = jnp.zeros((rows, PZ), F32)
    for i in range(count):
        put(v, i, vv, rows)
        vs = vs + m_at(i) * (vv - r_at(i))
        last = vv
        vv = vv + vs
    return last, vv


def ends(last, vn, hn, c):
    return -vn * hn, last - c * vn


def spread(msg, count, values):
    block = sum(v.shape[0] for v in values)
    for k in range(count):
        at = k * block
        for v in values:
            msg[pl.ds(at, v.shape[0]), :] = v
            at += v.shape[0]


def k_x1(f, eps, q1, xl, xr, yl, yr, msg, m, h, b, v, hb, r):
    gx = x_index()
    gy = y_index()
    xlo = gx > 0
    ylo = gy > 0
    yhi = gy < y_size() - 1
    yin = jnp.where(ylo, 1.0, 0.0)
    yon = jnp.where(yhi, 1.0, 0.0)
    q1lo = yin * (plane(yl, 1, PX) - 0.5 * fz(plane(yl, 0, PX)))
    q1hi = yon * (plane(yr, 1, PX) - 0.5 * fz(plane(yr, 0, PX)))
    hxlo = yin * plane(yl, 3, PX)
    epslo = plane(yl, 5, PX)
    epshi = plane(yr, 4, PX)
    hx31 = f[pl.ds(HX * PX * PY + PY - 1, PX, stride=PY), :]
    bxlo = jnp.concatenate([q1lo[:1], q1lo[1:] - q1lo[:-1]], 0)
    bxhi = jnp.concatenate([q1hi[:1], q1hi[1:] - q1hi[:-1]], 0)
    rlo = yin * plane(yl, 2, PX) + (32.0 / epslo) * (bxlo - (hxlo - yin * plane(yl, 4, PX)))
    rhi = yon * plane(yr, 2, PX) + (32.0 / epshi) * (bxhi - (yon * plane(yr, 3, PX) - hx31))
    pad = jnp.zeros((XR - PY - 2, PZ), F32)
    one = jnp.ones((XR - PY - 2, PZ), F32)
    before = jnp.where(xlo, plane(xl, 2) - 0.5 * fz(plane(xl, 0)), 0.0)
    for x in range(PX):
        q = plane(q1, x)
        e = plane(eps, x)
        hx = fplane(f, HX, x)
        ce = 32.0 / e
        rr = fplane(f, EZ, x) + ce * ((q - before) - (hx - y_prev(hx, hxlo[x : x + 1])))
        before = q
        r[pl.ds(x * XR, PY), :] = rr
        r[pl.ds(x * XR + PY, 8), :] = jnp.concatenate([rlo[x : x + 1], rhi[x : x + 1], pad], 0)
        m[pl.ds(x * XR, PY), :] = e * (1.0 / 1024.0)
        m[pl.ds(x * XR + PY, 8), :] = (
            jnp.concatenate([epslo[x : x + 1], epshi[x : x + 1], one], 0) * (1.0 / 1024.0)
        )
    m_at = lambda i: plane(m, i, XR)
    hn, bn, a, bb, c = factor(m_at, PX, gx == 0, h, b, XR)
    last, vn = sweep(m_at, lambda i: plane(r, i, XR), PX, v, XR)
    pf, plast = ends(last, vn, hn, c)
    put(hb, 0, hn, XR)
    put(hb, 1, bn, XR)
    put(hb, 2, c, XR)
    put(hb, 3, vn, XR)
    qq = jnp.concatenate([q1lo[PX - 1 :], q1hi[PX - 1 :]], 0) * (-1.0 / 32.0)
    spread(msg, lax.axis_size("gb"), packed((pf, plast, a, bb, c), XL, (qq,), XB))


def k_y1(f, eps, xl, xr, msg, p1, ey1, m, h, b, v, hb, r, ep):
    gx = x_index()
    gy = y_index()
    n = y_size()
    xlo = gx > 0
    xin = jnp.where(xlo, 1.0, 0.0)
    xon = jnp.where(gx < x_size() - 1, 1.0, 0.0)
    zero = jnp.zeros((1, PZ), F32)
    zeros = jnp.zeros((PY, PZ), F32)
    exl, eyl, hyl, hzl = [xin * plane(xl, i) for i in range(4)]
    eyr, ezr, hxr, hzr = [xon * plane(xr, i) for i in range(4)]
    for x in range(PX):
        put(ep, x, plane(eps, x))
    put(ep, PX, plane(xl, 4))
    put(ep, PX + 1, plane(xr, 4))
    for x in range(PX + 2, YR):
        put(ep, x, zeros + 1.0)
        put(r, x, zeros)
    put(r, PX + 1, zeros)

    def rex(ex, hy, pp, e):
        ie = 1.0 / e
        return ex + (32.0 * ie) * (pp - y_prev(pp, zero)) - (0.5 * ie) * bz(hy)

    p = hzl - 32.0 * (fplane(f, EY, 0) - eyl)
    p = jnp.where(xlo, p, 0.0)
    put(p1, PX, p)
    put(r, PX, rex(exl, hyl, p, plane(ep, PX)))
    for x in range(PX):
        ey = fplane(f, EY, x)
        nxt = fplane(f, EY, x + 1) if x < PX - 1 else eyr
        hz = fplane(f, HZ, x)
        hzp = fplane(f, HZ, x - 1) if x > 0 else hzl
        e = plane(ep, x)
        p = hz - 32.0 * (nxt - ey)
        put(p1, x, p)
        put(r, x, rex(fplane(f, EX, x), fplane(f, HY, x), p, e))
        ie = 1.0 / e
        put(ey1, x, ey + (0.5 * ie) * bz(fplane(f, HX, x)) - (32.0 * ie) * (hz - hzp))
    ie = 1.0 / plane(ep, PX + 1)
    put(ey1, PX, eyr + (0.5 * ie) * bz(hxr) - (32.0 * ie) * (hzr - fplane(f, HZ, PX - 1)))

    def rows(ref, j):
        return ref[pl.ds(j, YR, stride=PY), :]

    for j in range(PY):
        put(m, j, rows(ep, j) * (1.0 / 1024.0), YR)
    m_at = lambda j: plane(m, j, YR)
    hn, bn, a, bb, c = factor(m_at, PY, gy == 0, h, b, YR)
    last, vn = sweep(m_at, lambda j: rows(r, j), PY, v, YR)
    pf, plast = ends(last, vn, hn, c)
    put(hb, 0, hn, YR)
    put(hb, 1, bn, YR)
    put(hb, 2, c, YR)
    put(hb, 3, vn, YR)
    lastrow = lambda ref, at, k: ref[pl.ds(at * PY + PY - 1, k, stride=PY), :]
    tail = jnp.zeros((7, PZ), F32)
    qq = jnp.concatenate([lastrow(p1, 0, PX), lastrow(p1, PX, 1), tail], 0) * (-1.0 / 32.0)
    tail = jnp.zeros((6, PZ), F32)
    ee = fz(jnp.concatenate([lastrow(ey1, 0, PX), zero, lastrow(ey1, PX, 1), tail], 0))
    spread(msg, 1, packed((pf, plast, a, bb, c, qq, ee), YL, (), YB))


def coefficients(part, n, rows, tp, bp, ts, bs, bet, dele):
    zero = jnp.zeros((rows, PZ), F32)
    beta = zero
    put(bet, 0, zero, rows)
    for j in range(n):
        a, b, c = part(j, 2), part(j, 3), part(j, 4)
        bd = b / (1.0 - a * beta)
        t = bd * beta
        put(tp, j, t, rows)
        put(bp, j, bd, rows)
        beta = c + t * b
        put(bet, j + 1, beta, rows)
    delta = zero
    put(dele, n, zero, rows)
    for j in range(n - 1, -1, -1):
        a, b, c = part(j, 2), part(j, 3), part(j, 4)
        bd = b / (1.0 - c * delta)
        t = bd * delta
        put(ts, j, t, rows)
        put(bs, j, bd, rows)
        delta = a + t * b
        put(dele, j, delta, rows)


def chain(part, n, rows, crows, tp, bp, ts, bs, al, ga, start, stop):
    take = lambda ref, j: ref[pl.ds(j * crows, rows), :]
    alpha, gamma = start, stop
    put(al, 0, alpha, rows)
    put(ga, n, gamma, rows)
    for j in range(n):
        k = n - 1 - j
        alpha = part(j, 1) + take(tp, j) * part(j, 0) + take(bp, j) * alpha
        gamma = part(k, 0) + take(ts, k) * part(k, 1) + take(bs, k) * gamma
        put(al, j + 1, alpha, rows)
        put(ga, k, gamma, rows)
    return gamma, alpha


def interface(part, n, me, rows, coefs, al, ga, start=None, stop=None, crows=None):
    crows = crows or rows
    tp, bp, ts, bs, bet, dele = coefs
    zero = jnp.zeros((rows, PZ), F32)
    start = zero if start is None else start
    stop = zero if stop is None else stop
    chain(part, n, rows, crows, tp, bp, ts, bs, al, ga, start, stop)
    at = lambda ref, d, size: ref[pl.ds(pl.multiple_of(d * size, 8), rows), :]
    a0, a1 = at(al, me, rows), at(al, me + 1, rows)
    g0, g1 = at(ga, me, rows), at(ga, me + 1, rows)
    b0, b1 = at(bet, me, crows), at(bet, me + 1, crows)
    d0, d1 = at(dele, me, crows), at(dele, me + 1, crows)
    left = a0 + b0 * ((g0 + d0 * a0) / (1.0 - d0 * b0))
    right = g1 + d1 * ((a1 + b1 * g1) / (1.0 - b1 * d1))
    return left, right


def x_raw(msg):
    return lambda j, k: msg[pl.ds(j * XB + k * XL, XR), :]


def x_late(msg, at):
    return pltpu.roll(msg[pl.ds(at + XB - 8, 8), :], 6, 0)


def x_part(msg):
    def part(j, k):
        if j == 0:
            return x_raw(msg)(j, k)
        own = msg[pl.ds(j * XB + k * XL, PY), :]
        more = (
            msg[pl.ds(j * XB + k * XL + PY, 8), :]
            + msg[pl.ds(j * XB + (2 + k) * XL + PY, 8), :] * x_late(msg, (j - 1) * XB)
        )
        return jnp.concatenate([own, more], 0)

    return part


def x_passed(msg, me):
    prev = pl.multiple_of(jnp.maximum(me - 1, 0) * XB, 8)
    return jnp.where(me > 0, x_late(msg, prev), 0.0)


def y_raw(msg):
    return lambda j, k: msg[pl.ds(j * YB + k * YL, YR), :]


def y_part(msg):
    raw = y_raw(msg)
    return lambda j, k: raw(j, k) + raw(j, 2 + k) * raw(j - 1, 5) if j else raw(j, k)


def y_passed(msg, me, k):
    skip = k * YL % 8
    prev = pl.multiple_of(jnp.maximum(me - 1, 0) * YB + k * YL - skip, 8)
    return jnp.where(me > 0, pltpu.roll(msg[pl.ds(prev, YR), :], YR - skip, 0), 0.0)


def k_y2(gi, go, p1, h, b, v, hb, ex1, p2, elo, *more):
    coi, coo, (al, ga, dex) = more[:6], more[6:12], more[12:]
    nz, nc = lax.axis_size("gz"), lax.axis_size("gc")
    iz, ic = lax.axis_index("gz"), lax.axis_index("gc")
    coefficients(y_raw(go), nz, YR, *coo)
    coefficients(y_raw(gi), nc, YR, *coi)
    left, right = interface(y_part(go), nz, iz, YR, coo, al, ga)
    left = left + y_passed(go, iz, 5)
    left, right = interface(y_part(gi), nc, ic, YR, coi, al, ga, left, right)
    left = left + y_passed(gi, ic, 5)
    elo[...] = jnp.where(ic > 0, y_passed(gi, ic, 6), y_passed(go, iz, 6))
    lw = left * plane(hb, 1, YR)
    rw = (right - plane(hb, 3, YR)) * plane(hb, 0, YR)
    later = right
    for j in range(PY - 1, -1, -1):
        w = plane(v, j, YR) + plane(b, j, YR) * lw + plane(h, j, YR) * rw
        ex1[pl.ds(j, YR, stride=PY), :] = w
        dex[pl.ds(j, YR, stride=PY), :] = later - w
        later = w
    live = jnp.where(x_index() > 0, 1.0, 0.0)
    for x in range(PX):
        put(p2, x, plane(p1, x) + 64.0 * plane(dex, x))
    put(p2, PX, live * (plane(p1, PX) + 64.0 * plane(dex, PX)))


def join(part, raw, count):
    pf, ph, a, b, c = part(0, 0), part(0, 1), raw(0, 2), raw(0, 3), raw(0, 4)
    for j in range(1, count):
        qf, qh, a2, b2, c2 = part(j, 0), part(j, 1), raw(j, 2), raw(j, 3), raw(j, 4)
        den = 1.0 / (1.0 - c * a2)
        low, high = b * den, b2 * den
        pf, ph = pf + low * (qf + a2 * ph), qh + high * (ph + c * qf)
        a, b, c = a + low * b * a2, low * b2, c2 + high * b2 * c
    return pf, ph, a, b, c


def k_join_y(gi, msg):
    nc = lax.axis_size("gc")
    raw = y_raw(gi)
    values = join(y_part(gi), raw, nc)
    more = gi[pl.ds((nc - 1) * YB + 5 * YL, 2 * YL), :]
    spread(msg, 1, packed(values, YL, (more,), YB))


def k_join_x(gi, msg, inner):
    inner[...] = gi[...]
    nb = lax.axis_size("gb")
    last = x_late(gi, (nb - 1) * XB)[:2]
    spread(msg, lax.axis_size("ga"), packed(join(x_part(gi), x_raw(gi), nb), XL, (last,), XB))


def shares(pf, ph, coefs, count, me, rows, crows):
    tp, bp, ts, bs = coefs[:4]
    low = high = jnp.ones((rows, PZ), F32)
    for k in range(count):
        low = jnp.where(k < me, low * bs[pl.ds(k * crows, rows), :], low)
        high = jnp.where(k > me, high * bp[pl.ds(k * crows, rows), :], high)
    mine = pl.ds(pl.multiple_of(me * crows, 8), rows)
    return low * (pf + ts[mine, :] * ph), high * (ph + tp[mine, :] * pf)


def gathered(msg, n, m, ia, ib, rows, crows, coi, coo, al, ga):
    zero = jnp.zeros((rows, PZ), F32)

    def inside(j, k):
        at = pl.multiple_of(((ia * m + j) * 2 + k) * rows, 8)
        return msg[pl.ds(at, rows), :]

    whole = chain(inside, m, rows, crows, *coi[:4], al, ga, zero, zero)

    def group(j, k):
        total = sum(msg[pl.ds(((j * m + i) * 2 + k) * rows, rows), :] for i in range(m))
        return jnp.where(ia == j, whole[k], total)

    left, right = interface(group, n, ia, rows, coo, al, ga, crows=crows)
    return interface(inside, m, ib, rows, coi, al, ga, left, right, crows)


def k_x2(gi, go, f, q1, ey1, p2, h, b, v, m, hb, ez1, hx1, msg2, v2, vn2, *more):
    coi, coo, (al, ga, r) = more[:6], more[6:12], more[12:]
    na, nb = lax.axis_size("ga"), lax.axis_size("gb")
    ia, ib = lax.axis_index("ga"), lax.axis_index("gb")
    gy = y_index()
    yon = jnp.where(gy < y_size() - 1, 1.0, 0.0)
    coefficients(x_raw(go), na, XR, *coo)
    coefficients(x_raw(gi), nb, XR, *coi)
    left, right = interface(x_part(go), na, ia, XR, coo, al, ga)
    left = jnp.concatenate([left[:PY], left[PY:] + x_passed(go, ia)], 0)
    left, right = interface(x_part(gi), nb, ib, XR, coi, al, ga, left, right)
    left = jnp.concatenate([left[:PY], left[PY:] + x_passed(gi, ib)], 0)
    lw = left * plane(hb, 1, XR)
    rw = (right - plane(hb, 3, XR)) * plane(hb, 0, XR)
    for x in range(PX):
        put(ez1, x, plane(v, x, XR) + plane(b, x, XR) * lw + plane(h, x, XR) * rw, XR)
    put(ez1, PX, right, XR)
    before = plane(p2, PX)
    for x in range(PX):
        z = ez1[pl.ds(x * XR, PY), :]
        z32 = yon * ez1[pl.ds(x * XR + PY + 1, 1), :]
        ey = plane(ey1, x)
        t = fplane(f, HX, x) - 32.0 * (y_next(z, z32) - z) + 0.5 * fz(ey)
        put(hx1, x, t)
        p = plane(p2, x)
        ie = 1.0 / (m[pl.ds(x * XR, PY), :] * 1024.0)
        put(r, x, ey + (0.5 * ie) * bz(t) - (32.0 * ie) * (p - before))
        before = p
    last, vn = sweep(lambda i: m[pl.ds(i * XR, PY), :], lambda i: plane(r, i), PX, v2, PY)
    vn2[...] = vn
    pf, plast = ends(last, vn, hb[pl.ds(0, PY), :], hb[pl.ds(2 * XR, PY), :])
    share = shares(pf, plast, coi, nb, ib, PY, XR)
    for k in range(na * nb):
        for i, (own, joined) in enumerate(zip((pf, plast), share)):
            put(msg2, 2 * k + i, jnp.where(ia == k // nb, own, joined))


def k_y3(f, xr, q1, mx, ey1, ez1, hx1, ex1, elo, ex2, hy1, q2, r):
    n = y_size()
    gy = y_index()
    yon = jnp.where(gy < n - 1, 1.0, 0.0)
    yin = jnp.where(gy > 0, 1.0, 0.0)
    zeros = jnp.zeros((PY, PZ), F32)
    for x in range(PX + 2, YR):
        put(r, x, zeros)
    put(r, PX, zeros)
    for x in range(PX + 1):
        at = x * XR
        z = ez1[pl.ds(at, PY), :]
        zlo = ez1[pl.ds(at + PY, 1), :]
        zhi = yon * ez1[pl.ds(at + PY + 1, 1), :]
        fe = fz(plane(ey1, x))
        d = 32.0 * (y_next(z, zhi) - z) - fe
        k = x if x < PX else PX + 1
        dlo = yin * (32.0 * (z[:1] - zlo) - elo[pl.ds(k, 1), :])
        ez = fplane(f, EZ, x) if x < PX else plane(xr, 1)
        e = mx[pl.ds(at, PY), :] * 1024.0 if x < PX else plane(xr, 4)
        ie = 1.0 / e
        put(r, k, 2.0 * z - ez + (32.0 * ie) * (d - y_prev(d, dlo)))
        if x < PX:
            t = plane(q1, x) + 32.0 * (ez1[pl.ds(at + XR, PY), :] - z)
            put(hy1, x, t)
            put(ex2, x, 2.0 * plane(ex1, x) - fplane(f, EX, x) + (0.5 * ie) * bz(fplane(f, HY, x) - t))
            put(q2, x, plane(hx1, x) + 0.5 * fe)


def k_y3_sweep(r, m, hb, msg2, v2, vn2):
    m_at = lambda j: plane(m, j, YR)
    last, vn = sweep(m_at, lambda j: r[pl.ds(j, YR, stride=PY), :], PY, v2, YR)
    vn2[...] = vn
    pf, plast = ends(last, vn, plane(hb, 0, YR), plane(hb, 2, YR))
    spread(msg2, 1, (pf, plast))


def y_ends(msg):
    return lambda j, k: msg[pl.ds((2 * j + k) * YR, YR), :]


def k_join_ends(gi, tp, bp, ts, bs, msg, al, ga):
    nc = lax.axis_size("gc")
    zero = jnp.zeros((YR, PZ), F32)
    spread(msg, 1, chain(y_ends(gi), nc, YR, YR, tp, bp, ts, bs, al, ga, zero, zero))


def k_y4(gi, go, h, b, v2, vn2, hb, *more):
    coi, coo, (ex2, hy1, q2, out, al, ga, w2, dw) = more[:6], more[6:12], more[12:]
    nz, nc = lax.axis_size("gz"), lax.axis_size("gc")
    iz, ic = lax.axis_index("gz"), lax.axis_index("gc")
    left, right = interface(y_ends(go), nz, iz, YR, coo, al, ga)
    left, right = interface(y_ends(gi), nc, ic, YR, coi, al, ga, left, right)
    lw = left * plane(hb, 1, YR)
    rw = (right - vn2[...]) * plane(hb, 0, YR)
    later = right
    for j in range(PY - 1, -1, -1):
        w = plane(v2, j, YR) + plane(b, j, YR) * lw + plane(h, j, YR) * rw
        w2[pl.ds(j, YR, stride=PY), :] = w
        dw[pl.ds(j, YR, stride=PY), :] = later - w
        later = w
    xon = jnp.where(x_index() < x_size() - 1, 1.0, 0.0)
    for x in range(PX):
        w = plane(w2, x)
        nxt = plane(w2, x + 1) if x < PX - 1 else xon * plane(w2, PX + 1)
        e2 = plane(ex2, x)
        put(out, EX * PX + x, e2)
        put(out, EZ * PX + x, w)
        put(out, HX * PX + x, plane(q2, x) - 32.0 * plane(dw, x))
        put(out, HY * PX + x, plane(hy1, x) - 0.5 * fz(e2) + 32.0 * (nxt - w))


def k_x4(msg, h, b, v2, vn2, hb, *more):
    coi, coo, (p2, out, al, ga) = more[:6], more[6:12], more[12:]
    na, nb = lax.axis_size("ga"), lax.axis_size("gb")
    ia, ib = lax.axis_index("ga"), lax.axis_index("gb")
    left, right = gathered(msg, na, nb, ia, ib, PY, XR, coi, coo, al, ga)
    lw = left * hb[pl.ds(XR, PY), :]
    rw = (right - vn2[...]) * hb[pl.ds(0, PY), :]
    later = right
    for x in range(PX - 1, -1, -1):
        w = plane(v2, x) + b[pl.ds(x * XR, PY), :] * lw + h[pl.ds(x * XR, PY), :] * rw
        put(out, EY * PX + x, w)
        put(out, HZ * PX + x, plane(p2, x) - 32.0 * (later - w))
        later = w


def call(name, parts, args, outs, scratch=(), smem=(), into=(), flush=(), near=(), only=(), views=()):
    into, flush, scratch, only = dict(into), dict(flush), dict(scratch), dict(only)
    views = dict(views)
    touched = [list(used) + [views[k][0] for k in used if k in views] for _, used in parts]
    moved = [k for k in args if k not in smem and (k not in near or k in into)]
    pieces = {k for group in flush.values() for k, _, _ in group}
    last = {k: max(i for i, used in enumerate(touched) if k in used) for k in outs}
    leave = [
        [(k, 0, outs[k]) for k in outs if last[k] == i and k not in pieces and k not in near]
        + list(flush.get(i, ()))
        for i in range(len(parts))
    ]
    own = [k for k in moved if k not in into]

    def body(*refs):
        take = iter(refs)
        hbm = {k: next(take) for k in args}
        results = {k: next(take) for k in outs}
        env = {k: next(take) for k in own}
        env.update({k: results[k] if k in near else next(take) for k in outs})
        env.update({k: next(take) for k in scratch})
        env.update({k: hbm[k] for k in args if k not in moved})
        env.update({k: env[b].at[pl.ds(at, rows), :] for k, (b, at, rows) in views.items()})
        sem_in, sem_out = next(take), next(take)
        pending = {}
        count = 0
        for k in moved:
            pairs = [(hbm[k], env.get(k))]
            if k in into:
                buffer, row = into[k]
                pairs = [(hbm[k], env[buffer].at[pl.ds(row(), args[k].shape[0]), :])]
            elif k in only:
                windows = [pl.ds(at, rows) for at, rows in only[k]]
                pairs = [(hbm[k].at[w, :], env[k].at[w, :]) for w in windows]
            for source, where in pairs:
                copy = pltpu.make_async_copy(source, where, sem_in.at[count])
                copy.start()
                count += 1
                pending.setdefault(into[k][0] if k in into else k, []).append(copy)
        sent = []
        for i, (function, used) in enumerate(parts):
            for k in touched[i]:
                for copy in pending.pop(k, ()):
                    copy.wait()
            function(*[env[k] for k in used])
            for k, row, rows in leave[i]:
                window = pl.ds(row, rows)
                copy = pltpu.make_async_copy(
                    env[k].at[window, :], results[k].at[window, :], sem_out.at[len(sent)]
                )
                copy.start()
                sent.append(copy)
        for copy in sent:
            copy.wait()

    far, close, scalars = [
        pl.BlockSpec(memory_space=m) for m in (pltpu.HBM, pltpu.VMEM, pltpu.SMEM)
    ]
    got = pl.pallas_call(
        body,
        out_shape=[(pltpu.VMEM if k in near else pltpu.HBM)((c, PZ), F32) for k, c in outs.items()],
        in_specs=[scalars if k in smem else close if k in near else far for k in args],
        out_specs=[close if k in near else far for k in outs],
        scratch_shapes=[pltpu.VMEM(args[k].shape, args[k].dtype) for k in own]
        + [pltpu.VMEM((c, PZ), F32) for k, c in outs.items() if k not in near]
        + [pltpu.VMEM((c, PZ), F32) for c in scratch.values()]
        + [
            pltpu.SemaphoreType.DMA((sum(len(only.get(k, (0,))) for k in moved),)),
            pltpu.SemaphoreType.DMA((max(1, sum(len(group) for group in leave)),)),
        ],
        compiler_params=pltpu.CompilerParams(vmem_limit_bytes=LIMIT * 1024 * 1024),
        cost_estimate=pl.CostEstimate(flops=1000, bytes_accessed=1000, transcendentals=0),
        name=name,
    )(*[a if k in smem else pltpu.with_memory_space_constraint(a, pltpu.VMEM if k in near else pltpu.HBM) for k, a in args.items()])
    return dict(zip(outs, got))


def stacked(buffer, names, rows):
    return {k: (buffer, sum(rows[:i]), rows[i]) for i, k in enumerate(names)}


def ring(block, axis, step):
    n = lax.axis_size(axis)
    return lax.ppermute(block, axis, [(i, (i + step) % n) for i in range(n)])


def swap(msg, axis):
    n = lax.axis_size(axis)
    got = lax.all_to_all(msg.reshape(n, -1, PZ), axis, 0, 0, tiled=True)
    return got.reshape(-1, PZ)


def from_all(msg, axis, buffer):
    n = lax.axis_size(axis)
    rows = msg.shape[0]
    args, into = {}, {}
    for step in range(n):
        k = buffer + str(step)
        args[k] = ring(msg, axis, step) if step else msg

        def row(step=step):
            return pl.multiple_of(lax.rem(lax.axis_index(axis) - step + n, n) * rows, 8)

        into[k] = (buffer, row)
    return args, into


def local(fields, region, eps_table):
    na, nb = lax.axis_size("ga"), lax.axis_size("gb")
    along_x, along_y = ("ga", "gb"), ("gz", "gc")
    nz, nc = lax.axis_size("gz"), lax.axis_size("gc")
    ny = nz * nc
    ey = (max(nz, nc) + 1) * YR
    cells = PX * PY
    nxl, nyl = PX * XR, PY * YR
    f = fields.reshape(6 * cells, PZ)
    reg = region.reshape(cells, PZ)
    xup, xdn, yup, ydn = edges(fields, region, eps_table)
    xl = ring(xup, along_x, 1)
    xr = ring(xdn, along_x, -1)
    yl = ring(yup, along_y, 1)
    yr = ring(ydn, along_y, -1)
    linex = ("mx", "hx", "bx", "vx", "hbx")
    liney = ("my", "hy", "by", "vy", "hby")
    lines_x, lines_y = 4 * nxl + 4 * XR, 4 * nyl + 4 * YR
    lines = {
        **stacked("lx", ("mx", "vx", "hx", "bx", "hbx"), (nxl,) * 4 + (4 * XR,)),
        **stacked("ly", ("my", "vy", "hy", "by", "hby"), (nyl,) * 4 + (4 * YR,)),
    }
    of = lambda names: {k: lines[k] for k in names}
    pre = call(
        "eps",
        [(k_eps, ("reg", "table", "eps")), (k_q1, ("f", "q1"))],
        dict(reg=reg, table=eps_table, f=f),
        dict(eps=cells, q1=cells),
        smem=("table",),
        only=dict(f=[(EX * cells, cells), (HY * cells, cells)]),
    )
    one = call(
        "onex",
        [
            (k_x1, ("f", "eps", "q1", "xl", "xr", "yl", "yr", "msgx") + linex + ("r",)),
        ],
        dict(xl=xl, xr=xr, yl=yl, yr=yr, eps=pre["eps"], q1=pre["q1"], f=f),
        dict( lx=lines_x, msgx=nb * XB),
        dict(r=nxl),
        near=("xl", "xr", "yl", "yr") + NEAR,
        views=of(linex),
        only=dict(f=[(EZ * cells, 2 * cells)]),
    )
    oney = call(
        "oney",
        [(k_y1, ("f", "eps", "xl", "xr", "msgy", "p1", "ey1") + liney + ("rt", "ep"))],
        dict(f=f, eps=pre["eps"], xl=xl, xr=xr),
        dict(msgy=YB, p1=cells + PY, ey1=cells + PY, ly=lines_y),
        dict(rt=YR * PY, ep=YR * PY),
        near=("msgy",),
        views=of(liney),
        only=dict(f=[(EX * cells, 2 * cells), (HX * cells, 3 * cells)]),
    )
    one.update(oney)
    pair, into = from_all(one["msgy"], "gc", "gyi")
    group = call(
        "group",
        [
            (k_join_y, ("gyi", "msgyo")),
            (k_join_x, ("gi", "msgo", "inner")),
        ],
        dict(pair, gi=swap(one["msgx"], "gb")),
        dict(msgyo=YB, msgo=na * XB, inner=nb * XB),
        dict(gyi=nc * YB),
        into=into,
        near=("gi", "msgyo") + NEAR + tuple(pair),
    )
    goto = swap(group["msgo"], "ga")
    argy, into_o = from_all(group["msgyo"], "gz", "gyo")
    argy.update(pair)
    into.update(into_o)
    chains = ("tp", "bp", "ts", "bs", "bet", "del")
    ci, co, cyi, cyo = [tuple(k + a for k in chains) for a in ("i", "o", "yi", "yo")]
    cx, cy = ci + co, cyi + cyo
    size = lambda n, rows: (n * rows,) * 4 + ((n + 1) * rows,) * 2
    keep = {k: one[k] for k in ("p1", "ey1", "lx", "ly")}
    keep["q1"] = pre["q1"]
    rows_y, rows_x = size(nc, YR) + size(nz, YR), size(nb, XR) + size(na, XR)
    views = {**stacked("cy", cy, rows_y), **stacked("cx", cx, rows_x)}
    two = call(
        "two",
        [
            (k_y2, ("gyi", "gyo", "p1", "hy", "by", "vy", "hby", "ex1", "p2", "elo") + cy + ("aly", "gay", "dex")),
            (
                k_x2,
                ("gi", "go", "f", "q1", "ey1", "p2", "hx", "bx", "vx", "mx", "hbx")
                + ("ez1", "hx1", "msgx2", "vx2", "vnx2")
                + cx
                + ("alx", "gax", "r"),
            ),
            (
                k_y3,
                ("f", "xr", "q1", "mx", "ey1", "ez1", "hx1", "ex1", "elo", "ex2", "hy1", "q2", "rt"),
            ),
            (k_y3_sweep, ("rt", "my", "hby", "msgy2", "vy2", "vny2")),
        ],
        dict(argy, **{k: keep[k] for k in ("ly", "p1")}, gi=group["inner"], go=goto, f=f, xr=xr, **{k: keep[k] for k in ("lx", "ey1", "q1")}),
        dict(
            zip(
                ("p2", "cy", "msgx2", "vx2", "vnx2", "cx", "msgy2", "vy2", "vny2", "ex2", "hy1", "q2"),
                (cells + PY, sum(rows_y), na * nb * 2 * PY, cells, PY, sum(rows_x))
                + (2 * YR, nyl, YR, cells, cells, cells),
            )
        ),
        dict(
            gyi=nc * YB, gyo=nz * YB, ex1=YR * PY, elo=YR, aly=ey, gay=ey, dex=YR * PY,
            ez1=nxl + XR, hx1=cells, alx=(max(na, nb) + 1) * XR, gax=(max(na, nb) + 1) * XR, r=cells, rt=YR * PY,
        ),
        into=into,
        near=("go", "msgy2", "party2") + NEAR + tuple(k for k in argy if k not in pair),
        flush={0: [("p2", 0, cells + PY), ("cy", 0, sum(rows_y))]},
        views={**views, **lines},
        only=dict(f=[(EX * cells, cells), (EZ * cells, 3 * cells)]),
    )
    gotx = swap(two["msgx2"], along_x)
    pair, into = from_all(two["msgy2"], "gc", "gyi")
    group = call(
        "ends",
        [(k_join_ends, ("gyi",) + cyi[:4] + ("msg", "aly", "gay"))],
        dict(pair, cy=two["cy"]),
        dict(msg=2 * YR),
        dict(gyi=nc * 2 * YR, aly=ey, gay=ey),
        into=into,
        near=tuple(pair) + ("msg",),
        views={k: views[k] for k in cyi[:4]},
        only=dict(cy=[(0, sum(rows_y[:4]))]),
    )
    argy, into_o = from_all(group["msg"], "gz", "gyo")
    argy.update(pair)
    into.update(into_o)
    order = ("cy", "ly", "vny2", "vy2", "ex2", "q2", "hy1", "cx", "lx", "vnx2", "vx2", "p2")
    need = {k: two.get(k, one.get(k)) for k in order}
    three = call(
        "three",
        [
            (
                k_y4,
                ("gyi", "gyo", "hy", "by", "vy2", "vny2", "hby") + cy + ("ex2", "hy1", "q2", "out")
                + ("aly", "gay", "w2", "dw"),
            ),
            (k_x4, ("gx", "hx", "bx", "vx2", "vnx2", "hbx") + cx + ("p2", "out", "alx", "gax")),
        ],
        dict(argy, gx=gotx, **need),
        dict(out=6 * cells),
        dict(
            gyi=nc * 2 * YR, gyo=nz * 2 * YR, aly=ey, gay=ey, w2=YR * PY, dw=YR * PY,
            alx=(max(na, nb) + 1) * PY, gax=(max(na, nb) + 1) * PY,
        ),
        into=into,
        near=("gx",) + tuple(argy),
        views={**views, **of(("hx", "bx", "hbx", "hy", "by", "hby"))},
        only=dict(lx=[(2 * nxl, lines_x - 2 * nxl)], ly=[(2 * nyl, lines_y - 2 * nyl)]),
        flush={
            0: [("out", EX * cells, cells), ("out", EZ * cells, 3 * cells)],
            1: [("out", EY * cells, cells), ("out", HZ * cells, cells)],
        },
    )
    return three["out"].reshape(6, PX, PY, PZ)


def solution(mesh):
    nx, ny = mesh.devices.shape
    nb = max(d for d in range(1, nx + 1) if nx % d == 0 and d * d <= nx)
    shape = (nx // nb, nb, ny // 2, 2)
    grid = Mesh(mesh.devices.reshape(shape), ("ga", "gb", "gz", "gc"))
    columns = P(("ga", "gb"), ("gz", "gc"), None)
    return jax.shard_map(
        local,
        mesh=grid,
        in_specs=(P(None, *columns), columns, P()),
        out_specs=P(None, *columns),
        check_vma=False,
    )
```
